32 devices in a mesh: dp: 8 (over z, y), fsdp: 4 (over x, core).
Axes of the slice: x: 2, y: 2, z: 4, core: 2. Of those that a mesh axis runs over, the one named last changes fastest.
Arguments:
- tokens: bfloat16 [16384, 768], P(('dp', 'fsdp')), may hold values from -6 to 6
- cotangent: bfloat16 [16384, 768], P(('dp', 'fsdp'))
- starts: int32 [32, 3], P(('dp', 'fsdp')), may hold values from -257 to 513, as said below
- attn_in: float32 [768, 2304], P(('dp', 'fsdp')), may hold values from -0.21875 to 0.21875
- attn_out: float32 [768, 768], P(('dp', 'fsdp')), may hold values from -1.5 to 1.5
- ff_in: float32 [768, 4096], P(('dp', 'fsdp')), may hold values from -0.21875 to 0.21875
- ff_out: float32 [768, 2048], P(('dp', 'fsdp')), may hold values from -0.125 to 0.125
- gains: float32 [2, 768], P(None, ('dp', 'fsdp'))
- attn_in_m: float32 [768, 2304], P(('dp', 'fsdp')), may hold values from -0.0024414062 to 0.0024414062
- attn_out_m: float32 [768, 768], P(('dp', 'fsdp')), may hold values from -0.0007324219 to 0.0007324219
- ff_in_m: float32 [768, 4096], P(('dp', 'fsdp')), may hold values from -0.0024414062 to 0.0024414062
- ff_out_m: float32 [768, 2048], P(('dp', 'fsdp')), may hold values from -0.0024414062 to 0.0024414062
- gains_m: float32 [2, 768], P(None, ('dp', 'fsdp')), may hold values from -0.0024414062 to 0.0024414062
- attn_in_v: float32 [768, 2304], P(('dp', 'fsdp')), may hold values from 7.0627216e-08 to 1.1300355e-06
- attn_out_v: float32 [768, 768], P(('dp', 'fsdp')), may hold values from 7.8474685e-09 to 1.255595e-07
- ff_in_v: float32 [768, 4096], P(('dp', 'fsdp')), may hold values from 7.0627216e-08 to 1.1300355e-06
- ff_out_v: float32 [768, 2048], P(('dp', 'fsdp')), may hold values from 7.0627216e-08 to 1.1300355e-06
- gains_v: float32 [2, 768], P(None, ('dp', 'fsdp')), may hold values from 7.0627216e-08 to 1.1300355e-06
Outputs:
- block_out: float32 [16384, 768], P(('dp', 'fsdp'))
- token_input_gradient: float32 [16384, 768], P(('dp', 'fsdp'))
- grad_norm: float32 [], replicated
- attn_in_new: float32 [768, 2304], P(('dp', 'fsdp'))
- attn_out_new: float32 [768, 768], P(('dp', 'fsdp'))
- ff_in_new: float32 [768, 4096], P(('dp', 'fsdp'))
- ff_out_new: float32 [768, 2048], P(('dp', 'fsdp'))
- gains_new: float32 [2, 768], P(None, ('dp', 'fsdp'))
- attn_in_m_new: float32 [768, 2304], P(('dp', 'fsdp'))
- attn_out_m_new: float32 [768, 768], P(('dp', 'fsdp'))
- ff_in_m_new: float32 [768, 4096], P(('dp', 'fsdp'))
- ff_out_m_new: float32 [768, 2048], P(('dp', 'fsdp'))
- gains_m_new: float32 [2, 768], P(None, ('dp', 'fsdp'))
- attn_in_v_new: float32 [768, 2304], P(('dp', 'fsdp'))
- attn_out_v_new: float32 [768, 768], P(('dp', 'fsdp'))
- ff_in_v_new: float32 [768, 4096], P(('dp', 'fsdp'))
- ff_out_v_new: float32 [768, 2048], P(('dp', 'fsdp'))
- gains_v_new: float32 [2, 768], P(None, ('dp', 'fsdp'))
The draws below stay inside these ranges and needn't reach their ends.
Inputs may be any that keep to these rules, and one draw needn't show every extreme that they name: In each row consecutive starts differ by exactly 257; the first is negative and the second lies in 0 to 256, so every token has a start at or before it.
All inputs are finite; a program needn't handle non-finite values.
Results may differ from the reference program's by a relative error of at most 0.013.
The reference program's roundings to bfloat16 on the way count: a program that leaves them out, or rounds other values in their place, can miss the bound.
Values may be sent and summed in bfloat16 or wider, within the bound.
A program may use at most 192 MiB of HBM per device.

```python
import math
import jax
import jax.numpy as jnp
from jax import lax

D = 768
HEADS = 12
HD = 64
FF = 2048
ROW_LEN = 512
IMG = 257
STEP = 10
SEGS = 3
ROWS = 32
TOKENS = 16384


def draw_starts(key, part):
    key = jax.random.fold_in(key, 11)
    key_phase, key_order = jax.random.split(key)
    phase = jax.random.randint(key_phase, (ROWS,), 0, IMG)
    order = jax.random.permutation(key_order, ROWS)
    phase = phase.at[order[0]].set(0).at[order[1]].set(IMG - 1)
    offsets = jnp.arange(SEGS, dtype=jnp.int32) - 1
    return (phase[:, None] + offsets[None, :] * IMG).astype(jnp.int32)


def draw_gains(key, part):
    key = jax.random.fold_in(key, 21)
    ramp = jnp.arange(D, dtype=jnp.float32) / (D - 1)
    bottom, summit = (0.6, 1.8)
    base = bottom * (summit / bottom) ** ramp
    rough = jax.random.uniform(key, (2, D), jnp.float32, 0.8, 1.25)
    return (base[None, :] * rough).astype(jnp.float32)


def draw_cotangent(key, part):
    key = jax.random.fold_in(key, 31)
    key_noise, key_rough = jax.random.split(key)
    ramp = jnp.arange(D, dtype=jnp.float32) / (D - 1)
    base = 0.6 * 3.0 ** ramp
    noise = jnp.clip(jax.random.normal(key_noise, (TOKENS, D), jnp.float32), -5.0, 5.0)
    rough = jax.random.uniform(key_rough, (D,), jnp.float32, 0.8, 1.25)
    return (noise * (base * rough)[None, :]).astype(jnp.bfloat16)


def block_scale(rng, shape, cuts, smallest, high):
    def one(axis_at, parts):
        steps = jax.random.uniform(jax.random.fold_in(jax.random.fold_in(rng, 6), axis_at), (parts,), jnp.float32, smallest / len(cuts), high / len(cuts))
        return jnp.repeat(jnp.exp(steps), shape[axis_at] // parts).reshape((-1,) + (1,) * (len(shape) - axis_at - 1))

    factor_of = one(*cuts[0])
    for cut in cuts[1:]:
        factor_of = factor_of * one(*cut)
    return factor_of


def gaussian(key, extent, deviation, limit, cuts=(), kind=jnp.bfloat16):
    loudness = block_scale(key, extent, cuts, -0.22, 0.18) if cuts else 1.0
    array = jax.random.normal(key, extent, jnp.float32) * deviation * loudness
    return jnp.minimum(jnp.maximum(array, -limit), limit).astype(kind)


def setup_inputs(seed: int = 0) -> dict:
    seeds = jax.random.split(jax.random.key(seed), 19)
    tokens = gaussian(seeds[0], (TOKENS, D), 1.0, 6.0, ((0, 32),))
    cotangent = draw_cotangent(jax.random.fold_in(seeds[18], 71), 0)
    starts = draw_starts(jax.random.fold_in(seeds[18], 71), 0)
    attn_in = gaussian(seeds[3], (D, 3 * D), D ** -0.5, 0.21875, ((0, 32),), jnp.float32)
    attn_out = gaussian(seeds[4], (D, D), (D // 48) ** -0.5, 1.5, ((0, 32),), jnp.float32)
    ff_in = gaussian(seeds[5], (D, 2 * FF), D ** -0.5, 0.21875, ((0, 32),), jnp.float32)
    ff_out = gaussian(seeds[6], (D, FF), FF ** -0.5, 0.125, ((0, 32),), jnp.float32)
    gains = draw_gains(jax.random.fold_in(seeds[18], 71), 0)
    attn_in_m = gaussian(seeds[8], (D, 3 * D), ((D * (4 * D + 3 * FF + 2)) ** -0.5), 0.0024414062, ((0, 32),), jnp.float32)
    attn_out_m = gaussian(seeds[9], (D, D), (((IMG // 32 + 1) * D * (4 * D + 3 * FF + 2)) ** -0.5), 0.0007324219, ((0, 32),), jnp.float32)
    ff_in_m = gaussian(seeds[10], (D, 2 * FF), ((D * (4 * D + 3 * FF + 2)) ** -0.5), 0.0024414062, ((0, 32),), jnp.float32)
    ff_out_m = gaussian(seeds[11], (D, FF), ((D * (4 * D + 3 * FF + 2)) ** -0.5), 0.0024414062, ((0, 32),), jnp.float32)
    gains_m = gaussian(seeds[12], (2, D), ((D * (4 * D + 3 * FF + 2)) ** -0.5), 0.0024414062, ((1, 32),), jnp.float32)
    attn_in_v = jnp.clip(jnp.exp(math.log(1.130035457208578e-06) - 2.7725887 * jax.random.uniform(seeds[13], (D, 3 * D), jnp.float32) ** block_scale(seeds[13], (D, 3 * D), ((0, 32),), -0.2, 0.2)), 7.062721607553613e-08, 1.130035457208578e-06)
    attn_out_v = jnp.clip(jnp.exp(math.log(1.2555949524539756e-07) - 2.7725887 * jax.random.uniform(seeds[14], (D, D), jnp.float32) ** block_scale(seeds[14], (D, D), ((0, 32),), -0.2, 0.2)), 7.847468452837347e-09, 1.2555949524539756e-07)
    ff_in_v = jnp.clip(jnp.exp(math.log(1.130035457208578e-06) - 2.7725887 * jax.random.uniform(seeds[15], (D, 2 * FF), jnp.float32) ** block_scale(seeds[15], (D, 2 * FF), ((0, 32),), -0.2, 0.2)), 7.062721607553613e-08, 1.130035457208578e-06)
    ff_out_v = jnp.clip(jnp.exp(math.log(1.130035457208578e-06) - 2.7725887 * jax.random.uniform(seeds[16], (D, FF), jnp.float32) ** block_scale(seeds[16], (D, FF), ((0, 32),), -0.2, 0.2)), 7.062721607553613e-08, 1.130035457208578e-06)
    gains_v = jnp.clip(jnp.exp(math.log(1.130035457208578e-06) - 2.7725887 * jax.random.uniform(seeds[17], (2, D), jnp.float32) ** block_scale(seeds[17], (2, D), ((1, 32),), -0.2, 0.2)), 7.062721607553613e-08, 1.130035457208578e-06)
    return {"tokens": tokens, "cotangent": cotangent, "starts": starts, "attn_in": attn_in, "attn_out": attn_out, "ff_in": ff_in, "ff_out": ff_out, "gains": gains, "attn_in_m": attn_in_m, "attn_out_m": attn_out_m, "ff_in_m": ff_in_m, "ff_out_m": ff_out_m, "gains_m": gains_m, "attn_in_v": attn_in_v, "attn_out_v": attn_out_v, "ff_in_v": ff_in_v, "ff_out_v": ff_out_v, "gains_v": gains_v}


NORM_EPS = 1e-05
CLIP_NORM = 1.0
LEARN_RATES = (0.02, 0.1, 0.02, 0.02, 0.5)
FIRST_DECAY = 0.5
SECOND_DECAY = 0.5
ADAM_EPS = 1e-08
WEIGHT_DECAY = 0.05
ROPE_BASE = 10000.0
MASKED = -1e+30
HIGH = lax.Precision.HIGHEST

@jax.custom_vjp
def low(v):
    return lax.optimization_barrier(v.astype(jnp.bfloat16)).astype(jnp.float32)

@jax.custom_vjp
def low_back(v):
    return v

def low_keep(v):
    return (low(v), None)

def low_pass(kept, grad):
    return (grad,)

def back_keep(v):
    return (v, None)

def back_low(kept, grad):
    return (low(grad),)
low.defvjp(low_keep, low_pass)
low_back.defvjp(back_keep, back_low)

def positions(begins, length):
    tok_index = jnp.arange(length, dtype=jnp.int32)
    began = begins[None, :] <= tok_index[:, None]
    segment = lax.optimization_barrier(jnp.sum(began.astype(jnp.int32), axis=1))
    latest = lax.optimization_barrier(jnp.max(jnp.where(began, begins[None, :], -4 * IMG), axis=1))
    return ((tok_index - latest).astype(jnp.float32), segment)

def rotation(rotary_place):
    half = HD // 2
    freq = ROPE_BASE ** (-jnp.arange(half, dtype=jnp.float32) * (2.0 / HD))
    angle = rotary_place[:, None] * freq[None, :]
    return (jnp.cos(angle), jnp.sin(angle))

def rotate(values, cosine, sine_table):
    half = values.shape[-1] // 2
    front, behind = (values[..., :half], values[..., half:])
    cos_part = cosine[:, None, :]
    sin_part = sine_table[:, None, :]
    return jnp.concatenate([front * cos_part - behind * sin_part, behind * cos_part + front * sin_part], axis=-1)

def normed(values, norm_gain):
    return values * lax.rsqrt(lax.optimization_barrier(jnp.mean(values * values, axis=-1, keepdims=True)) + NORM_EPS) * norm_gain

def forward_row(layer_input, weights, begins):
    attn_in, attn_out, ff_in, ff_out, gains = weights
    length = layer_input.shape[0]
    rotary_place, segment = positions(begins, length)
    cosine, sine_table = rotation(rotary_place)
    tok_index = jnp.arange(length, dtype=jnp.int32)
    allowed = (segment[:, None] == segment[None, :]) & (tok_index[None, :] <= tok_index[:, None])
    first_normalized = low(normed(layer_input, gains[0]))
    projected = low_back(jnp.dot(first_normalized, attn_in, precision=HIGH))
    query = low(rotate(projected[:, :D].reshape(length, HEADS, HD), cosine, sine_table))
    keys = low(rotate(projected[:, D:2 * D].reshape(length, HEADS, HD), cosine, sine_table))
    values = low(projected[:, 2 * D:].reshape(length, HEADS, HD))
    scores = low_back(jnp.einsum('qhd,khd->hqk', query, keys, precision=HIGH) * HD ** (-0.5))
    scores = jnp.where(allowed[None], scores, MASKED)
    highest = lax.optimization_barrier(jnp.max(scores, axis=-1, keepdims=True))
    shifted = jnp.exp(scores - highest)
    soft_weights = low(shifted / lax.optimization_barrier(jnp.sum(shifted, axis=-1, keepdims=True)))
    mixed = jnp.einsum('hqk,khd->qhd', soft_weights, values, precision=HIGH).reshape(length, D)
    mixed = low(low_back(mixed))
    residual_state = layer_input + low_back(jnp.dot(mixed, attn_out.T, precision=HIGH))
    second_normalized = low(normed(residual_state, gains[1]))
    gate_up = low_back(jnp.dot(second_normalized, ff_in, precision=HIGH))
    activated = low(jax.nn.silu(gate_up[:, :FF]) * gate_up[:, FF:])
    return residual_state + low_back(jnp.dot(activated, ff_out.T, precision=HIGH))

def adam_update(weight, grad, first, second, clip_factor, decay, rate):
    grad = grad * clip_factor
    first = FIRST_DECAY * first + (1.0 - FIRST_DECAY) * grad
    second = SECOND_DECAY * second + (1.0 - SECOND_DECAY) * grad * grad
    fix_one = 1.0 - FIRST_DECAY ** STEP
    fix_two = 1.0 - SECOND_DECAY ** STEP
    change = first / fix_one / (jnp.sqrt(second / fix_two) + ADAM_EPS) + decay * weight
    return (weight - rate * change, first, second)

def reference(tokens, cotangent, starts, attn_in, attn_out, ff_in, ff_out, gains, attn_in_m, attn_out_m, ff_in_m, ff_out_m, gains_m, attn_in_v, attn_out_v, ff_in_v, ff_out_v, gains_v):
    masters = (attn_in, attn_out, ff_in, ff_out, gains)
    group = math.gcd(ROWS, max(1, 4096 // ROW_LEN))
    count = ROWS // group
    rows_all = tokens.astype(jnp.float32).reshape(count, group, ROW_LEN, D)
    backs_all = cotangent.astype(jnp.float32).reshape(count, group, ROW_LEN, D)
    begins_all = starts.reshape(count, group, SEGS)

    def one_group(totals, pieces):
        rows, backs, begins = pieces

        def forward(row_inputs, weights):
            lowered = tuple((low(w) for w in weights))

            def single(one_row, one_begin):
                return forward_row(one_row, lowered, one_begin)
            return jax.vmap(single)(row_inputs, begins)
        outputs, pullback = jax.vjp(forward, rows, masters)
        row_grads, weight_grads = pullback(backs)
        totals = jax.tree.map(jnp.add, totals, weight_grads)
        return (totals, (outputs, row_grads))
    zeros = tuple((jnp.zeros_like(w) for w in masters))
    totals, (outputs, row_grads) = lax.scan(one_group, zeros, (rows_all, backs_all, begins_all))
    squares = sum((jnp.sum(g * g) for g in totals))
    grad_norm = jnp.sqrt(squares)
    clip_factor = CLIP_NORM / jnp.maximum(grad_norm, CLIP_NORM)
    firsts = (attn_in_m, attn_out_m, ff_in_m, ff_out_m, gains_m)
    seconds = (attn_in_v, attn_out_v, ff_in_v, ff_out_v, gains_v)
    decays = (WEIGHT_DECAY, WEIGHT_DECAY, WEIGHT_DECAY, WEIGHT_DECAY, 0.0)
    results = [adam_update(w, g, m, v, clip_factor, dec, rate) for w, g, m, v, dec, rate in zip(masters, totals, firsts, seconds, decays, LEARN_RATES)]
    block_out = outputs.reshape(TOKENS, D)
    token_input_gradient = row_grads.reshape(TOKENS, D)
    return (block_out, token_input_gradient, grad_norm, results[0][0], results[1][0], results[2][0], results[3][0], results[4][0], results[0][1], results[1][1], results[2][1], results[3][1], results[4][1], results[0][2], results[1][2], results[2][2], results[3][2], results[4][2])
```

```python
import functools

import jax
import jax.numpy as jnp
from jax import lax
from jax.experimental import pallas as pl
from jax.experimental.pallas import tpu as pltpu
from jax.sharding import PartitionSpec as P

BF = jnp.bfloat16
F32 = jnp.float32
MESH_ID = pl.DeviceIdType.MESH

WIDTHS = (2304, 768, 4096, 2048)
PIECES = (
    (0, 0, 384, 384, 128),
    (0, 768, 1152, 384, 256),
    (0, 1536, 1920, 384, 128),
    (1, 0, 384, 384, 256),
    (2, 0, 2048, 512, 256),
    (3, 0, 256, 256, 128),
    (2, 512, 2560, 512, 256),
    (3, 512, 768, 256, 128),
    (2, 1024, 3072, 512, 256),
    (3, 1024, 1280, 256, 128),
    (2, 1536, 3584, 512, 256),
    (3, 1536, 1792, 256, 128),
)
OFFSETS = tuple(sum(p[3] for p in PIECES[:k]) for k in range(len(PIECES)))
HALF = sum(p[3] for p in PIECES)
COUNT = len(PIECES)


class Place:
    def __init__(self):
        dp, fs = lax.axis_index("dp"), lax.axis_index("fsdp")
        self.dp, self.fs = dp, fs
        self.x, self.c = fs // 2, fs % 2
        self.z, self.y = dp // 2, dp % 2
        self.yx = self.y * 2 + self.x
        self.me = dp * 4 + fs
        self.sibling = (dp, self.x * 2 + 1 - self.c)
        self.xn = (dp, (1 - self.x) * 2 + self.c)
        self.yn = (self.z * 2 + 1 - self.y, fs)
        self.x_column = self.y * 2 + 1 - self.x
        self.y_column = (1 - self.y) * 2 + self.x
        self.diagonal = (1 - self.y) * 2 + 1 - self.x

    def z_peer(self, step):
        z = lax.rem(self.z + step, 4)
        return z, (z * 2 + self.y, self.fs)

    def group_peer(self, step):
        fs = lax.rem(self.fs + step, 4)
        return fs, (self.dp, fs)

    def plane_peer(self, step):
        dp = lax.rem(self.dp + step, 8)
        return dp, (dp, self.fs)

    def greet(self):
        barrier = pltpu.get_barrier_semaphore()
        for step in range(1, 4):
            pl.semaphore_signal(
                barrier, inc=1, device_id=self.group_peer(step)[1], device_id_type=MESH_ID
            )
        for step in range(1, 8):
            pl.semaphore_signal(
                barrier, inc=1, device_id=self.plane_peer(step)[1], device_id_type=MESH_ID
            )
        pl.semaphore_wait(barrier, 10)

    def columns(self, piece, sibling=False):
        first, second, width = piece[1], piece[2], piece[3]
        core = 1 - self.c if sibling else self.c
        start = jnp.where(core == 0, first, second)
        return pl.ds(pl.multiple_of(start, 128), width)

    def parts(self, piece):
        return (0, piece[4]), (piece[4], piece[3] - piece[4])


def remote(src, dst, send, recv, device):
    return pltpu.make_async_remote_copy(
        src_ref=src,
        dst_ref=dst,
        send_sem=send,
        recv_sem=recv,
        device_id=device,
        device_id_type=MESH_ID,
    )


GATHER_SEMS = 12
REDUCE_SEMS = 9


class Gather:
    def __init__(self, place, shards, whole, sibling_rows, send, recv):
        self.p, self.shards, self.whole = place, shards, whole
        self.rows, self.send, self.recv = sibling_rows, send, recv

    def copy(self, k, which):
        p, piece = self.p, PIECES[k]
        w = self.whole[piece[0]]
        sem = (self.send.at[k * GATHER_SEMS + which], self.recv.at[k * GATHER_SEMS + which])
        cols = p.columns(piece)

        def part(i):
            start, width = p.parts(piece)[i]
            return pl.ds(pl.multiple_of(cols.start + start, 128), width)

        if which == 0:
            shard = self.shards[piece[0]]
            return remote(
                shard.at[:, p.columns(piece, sibling=True)],
                self.rows.at[:, pl.ds(OFFSETS[k], piece[3])],
                *sem,
                p.sibling,
            )
        if which in (1, 2, 3):
            block = w.at[p.z, p.yx, :, cols]
            return remote(block, block, *sem, p.z_peer(which)[1])
        if which in (4, 5):
            block = w.at[:, p.yx, :, cols]
            return remote(block, block, *sem, (p.xn, p.yn)[which - 4])
        if which in (6, 7):
            along_x = p.c == which - 6
            column = jnp.where(along_x, p.y_column, p.x_column)
            block = w.at[:, column, :, part(which - 6)]
            device = (
                jnp.where(along_x, p.xn[0], p.yn[0]),
                jnp.where(along_x, p.xn[1], p.yn[1]),
            )
            return remote(block, block, *sem, device)
        column = (p.yx, p.x_column, p.y_column, p.diagonal)[which - 8]
        block = w.at[:, column, :, cols]
        return remote(block, block, *sem, p.sibling)

    def exchange(self, k):
        self.copy(k, 0).start()

    def begin(self, k):
        p, piece = self.p, PIECES[k]
        self.copy(k, 0).wait_recv()
        mine = self.shards[piece[0]][:, p.columns(piece)]
        other = self.rows[:, OFFSETS[k] : OFFSETS[k] + piece[3]]
        first = p.c == 0
        both = jnp.concatenate(
            [jnp.where(first, mine, other), jnp.where(first, other, mine)], axis=0
        )
        self.whole[piece[0]][p.z, p.yx, :, p.columns(piece)] = both.astype(BF)
        for i in (1, 2, 3):
            self.copy(k, i).start()

    def step1(self, k):
        for i in (1, 2, 3):
            self.copy(k, i).wait_recv()
        for i in (4, 5, 8):
            self.copy(k, i).start()

    def step2(self, k):
        for i in (4, 5):
            self.copy(k, i).wait_recv()
        for i in (6, 7, 9, 10):
            self.copy(k, i).start()

    def step3(self, k):
        for i in (6, 7):
            self.copy(k, i).wait_recv()
        self.copy(k, 11).start()

    def finish(self, k):
        for i in (8, 9, 10, 11):
            self.copy(k, i).wait_recv()

    def drain(self, k):
        for i in range(GATHER_SEMS):
            self.copy(k, i).wait_send()


class Reduce:
    def __init__(self, place, mine, other, landed, diag, cols, zed, done, got, send, recv):
        self.p = place
        self.mine, self.other, self.landed = mine, other, landed
        self.diag, self.cols, self.zed, self.done, self.got = diag, cols, zed, done, got
        self.send, self.recv = send, recv

    def copy(self, k, which):
        p, piece = self.p, PIECES[k]
        off, width = OFFSETS[k], piece[3]
        sem = (self.send.at[k * REDUCE_SEMS + which], self.recv.at[k * REDUCE_SEMS + which])
        span = pl.ds(off, width)
        if which == 0:
            return remote(
                self.other(k), self.landed.at[:, :, :, span], *sem, p.sibling
            )
        if which in (1, 2):
            start, wide = p.parts(piece)[which - 1]
            part = pl.ds(off + start, wide)
            along_x = p.c == which - 1
            device = (
                jnp.where(along_x, p.xn[0], p.yn[0]),
                jnp.where(along_x, p.xn[1], p.yn[1]),
            )
            return remote(
                self.mine.at[:, p.diagonal, :, part], self.diag.at[:, :, part], *sem, device
            )
        if which in (3, 4):
            column, device = ((p.x_column, p.xn), (p.y_column, p.yn))[which - 3]
            return remote(
                self.mine.at[:, column, :, span], self.cols.at[which - 3, :, :, span], *sem, device
            )
        if which in (5, 6, 7):
            z, device = p.z_peer(which - 4)
            return remote(
                self.mine.at[z, p.yx, :, span], self.zed.at[which - 5, :, span], *sem, device
            )
        return remote(
            self.done.at[1 - p.c, :, span], self.got.at[:, span], *sem, p.sibling
        )

    def begin(self, k):
        self.copy(k, 0).start()

    def step1(self, k):
        off, width = OFFSETS[k], PIECES[k][3]
        self.copy(k, 0).wait_recv()

        @pl.loop(0, 4)
        def _(z):
            for yx in range(4):
                total = self.mine[z, yx, :, off : off + width].astype(F32) + self.landed[
                    z, yx, :, off : off + width
                ].astype(F32)
                self.mine[z, yx, :, off : off + width] = total.astype(BF)

        for i in (1, 2):
            self.copy(k, i).start()

    def step2(self, k):
        p, piece = self.p, PIECES[k]
        off = OFFSETS[k]
        for i in (1, 2):
            self.copy(k, i).wait_recv()
        for i in (0, 1):
            start, wide = p.parts(piece)[i]
            column = jnp.where(p.c == i, p.y_column, p.x_column)
            part = slice(off + start, off + start + wide)

            @pl.loop(0, 4)
            def _(z):
                total = self.mine[z, column, :, part].astype(F32) + self.diag[z, :, part].astype(
                    F32
                )
                self.mine[z, column, :, part] = total.astype(BF)

        for i in (3, 4):
            self.copy(k, i).start()

    def step3(self, k):
        p = self.p
        off, width = OFFSETS[k], PIECES[k][3]
        span = slice(off, off + width)
        for i in (3, 4):
            self.copy(k, i).wait_recv()

        @pl.loop(0, 4)
        def _(z):
            total = (
                self.mine[z, p.yx, :, span].astype(F32)
                + self.cols[0, z, :, span].astype(F32)
                + self.cols[1, z, :, span].astype(F32)
            )
            self.mine[z, p.yx, :, span] = total.astype(BF)

        for i in (5, 6, 7):
            self.copy(k, i).start()

    def step4(self, k):
        p = self.p
        off, width = OFFSETS[k], PIECES[k][3]
        span = slice(off, off + width)
        for i in (5, 6, 7):
            self.copy(k, i).wait_recv()
        total = self.mine[p.z, p.yx, :, span].astype(F32)
        for i in range(3):
            total = total + self.zed[i, :, span].astype(F32)
        self.done[0, :, span] = total[:24]
        self.done[1, :, span] = total[24:]
        self.copy(k, 8).start()

    def finish(self, k):
        self.copy(k, 8).wait_recv()

    def drain(self, k):
        for i in range(REDUCE_SEMS):
            self.copy(k, i).wait_send()


SMALL_SEMS = 10


class Small:
    def __init__(self, place, group, plane, send, recv, base):
        self.p, self.group, self.plane = place, group, plane
        self.send, self.recv, self.base = send, recv, base

    def first(self, step):
        i = self.base + step - 1
        slot = self.group.at[self.p.fs]
        return remote(slot, slot, self.send.at[i], self.recv.at[i], self.p.group_peer(step)[1])

    def second(self, step):
        i = self.base + 2 + step
        slot = self.plane.at[self.p.dp]
        return remote(slot, slot, self.send.at[i], self.recv.at[i], self.p.plane_peer(step)[1])

    def start_first(self):
        for step in range(1, 4):
            self.first(step).start()

    def wait_first(self):
        for step in range(1, 4):
            self.first(step).wait_recv()

    def start_second(self):
        for step in range(1, 8):
            self.second(step).start()

    def wait_second(self):
        for step in range(1, 8):
            self.second(step).wait_recv()

    def drain(self):
        for step in range(1, 4):
            self.first(step).wait_send()
        for step in range(1, 8):
            self.second(step).wait_send()


def spread_gains(plane, count, wide, total):
    slots = plane.reshape(count, 8, 128)
    owner = lax.broadcasted_iota(jnp.int32, (count, total), 1) // wide
    pick = (owner == lax.broadcasted_iota(jnp.int32, (count, total), 0)).astype(F32)
    lane = lax.broadcasted_iota(jnp.int32, (128, total), 1) % wide
    keep = lane == lax.broadcasted_iota(jnp.int32, (128, total), 0)
    rows = []
    for g in range(2):
        spread = lax.dot_general(
            slots[:, g, :], pick, (((0,), (0,)), ((), ())), preferred_element_type=F32
        )
        rows.append(jnp.sum(jnp.where(keep, spread, 0.0), axis=0, keepdims=True))
    return rows


def gather_kernel(
    w0, w1, w2, w3, gains, out0, out1, out2, out3, out_gains,
    big0, big1, big2, big3, rows, group, plane, send, recv, small_send, small_recv, local,
):
    place = Place()
    place.greet()
    whole = (big0, big1, big2, big3)
    gather = Gather(place, (w0, w1, w2, w3), whole, rows, send, recv)
    small = Small(place, group, plane, small_send, small_recv, 0)
    for k in range(COUNT):
        gather.exchange(k)
    width = gains.shape[1]
    group[place.fs] = jnp.zeros((8, 128), F32)
    group[place.fs, 0:2, 0:width] = gains[...].astype(BF).astype(F32)
    small.start_first()
    gather.begin(0)
    gather.begin(1)
    small.wait_first()
    for i in range(4):
        plane[place.dp, i] = group[i]
    small.start_second()
    for slot in range(COUNT + 4):
        for stage, lag in ((gather.begin, -2), (gather.step1, 0), (gather.step2, 1), (gather.step3, 2), (gather.finish, 3)):
            k = slot - lag
            if 0 <= k < COUNT and not (lag == -2 and k < 2):
                stage(k)
    small.wait_second()
    first, second = spread_gains(plane, 32, width, 32 * width)
    out_gains[...] = jnp.zeros_like(out_gains)
    out_gains[0:1, :] = first
    out_gains[1:2, :] = second
    copies = [
        pltpu.make_async_copy(big, out, local.at[i])
        for i, (big, out) in enumerate(zip(whole, (out0, out1, out2, out3)))
    ]
    for copy in copies:
        copy.start()
    for k in range(COUNT):
        gather.drain(k)
    small.drain()
    for copy in copies:
        copy.wait()


def reduce_kernel(
    g0, g1, g2, g3, dgains, out0, out1, out2, out3, out_gains, out_square,
    mine, landed, diag, cols, zed, done, got, group, plane, group2, plane2, group_sum,
    send, recv, small_send, small_recv, local,
):
    place = Place()
    place.greet()
    grads = (g0, g1, g2, g3)

    def other(k):
        return grads[PIECES[k][0]].at[:, :, :, place.columns(PIECES[k], sibling=True)]

    reduce = Reduce(place, mine, other, landed, diag, cols, zed, done, got, send, recv)
    small = Small(place, group, plane, small_send, small_recv, 0)
    small2 = Small(place, group2, plane2, small_send, small_recv, 10)

    def own(k):
        return pltpu.make_async_copy(
            grads[PIECES[k][0]].at[:, :, :, place.columns(PIECES[k])],
            mine.at[:, :, :, pl.ds(OFFSETS[k], PIECES[k][3])],
            local.at[k],
        )

    def begin(k):
        reduce.begin(k)
        own(k).start()

    def step1(k):
        own(k).wait()
        reduce.step1(k)

    group[place.fs] = dgains[...]
    small.start_first()
    begin(0)
    begin(1)
    small.wait_first()
    plane[place.dp] = group[0] + group[1] + group[2] + group[3]
    small.start_second()
    for slot in range(COUNT + 5):
        for stage, lag in ((begin, -2), (step1, 0), (reduce.step2, 1), (reduce.step3, 2), (reduce.step4, 3), (reduce.finish, 4)):
            k = slot - lag
            if 0 <= k < COUNT and not (lag == -2 and k < 2):
                stage(k)
    small.wait_second()
    total = plane[0]
    for i in range(1, 8):
        total = total + plane[i]
    width = out_gains.shape[1]
    model = total.shape[1]
    wanted = lax.broadcasted_iota(jnp.int32, (model, 128), 0) == place.me * width + lax.broadcasted_iota(jnp.int32, (model, 128), 1)
    wanted = wanted & (lax.broadcasted_iota(jnp.int32, (model, 128), 1) < width)
    slot_gains = jnp.dot(total, wanted.astype(F32), preferred_element_type=F32, precision=lax.Precision.HIGHEST)
    out_gains[...] = slot_gains[0:2, 0:width]
    square = jnp.sum(slot_gains[0:2] * slot_gains[0:2], axis=(0, 1), keepdims=True)
    outs = (out0, out1, out2, out3)
    for k, piece in enumerate(PIECES):
        span = slice(OFFSETS[k], OFFSETS[k] + piece[3])
        a = done[place.c, :, span]
        b = got[:, span]
        outs[piece[0]][:, place.columns(piece)] = a
        outs[piece[0]][:, place.columns(piece, sibling=True)] = b
        square = square + jnp.sum(a * a + b * b, axis=(0, 1), keepdims=True)
    group2[place.fs] = jnp.broadcast_to(square, (8, 128))
    small2.start_first()
    small2.wait_first()
    plane2[place.dp] = group2[0] + group2[1] + group2[2] + group2[3]
    small2.start_second()
    for k in range(COUNT):
        reduce.drain(k)
    small.drain()
    small2.wait_second()
    square = plane2[0]
    for i in range(1, 8):
        square = square + plane2[i]
    out_square[...] = square
    small2.drain()


def any_spec():
    return pl.BlockSpec(memory_space=pl.ANY)


def vmem_spec():
    return pl.BlockSpec(memory_space=pltpu.VMEM)


def gather_all(attn_in, attn_out, ff_in, ff_out, gains):
    dma = pltpu.SemaphoreType.DMA
    total = gains.shape[1] * 32
    *weights, wide = pl.pallas_call(
        gather_kernel,
        out_shape=[jax.ShapeDtypeStruct((4, 4, 48, w), BF) for w in WIDTHS]
        + [jax.ShapeDtypeStruct((8, total), F32)],
        in_specs=[vmem_spec()] * 5,
        out_specs=[any_spec()] * 4 + [vmem_spec()],
        scratch_shapes=[pltpu.VMEM((4, 4, 48, w), BF) for w in WIDTHS]
        + [
            pltpu.VMEM((24, HALF), F32),
            pltpu.VMEM((4, 8, 128), F32),
            pltpu.VMEM((8, 4, 8, 128), F32),
            dma((COUNT * GATHER_SEMS,)),
            dma((COUNT * GATHER_SEMS,)),
            dma((SMALL_SEMS,)),
            dma((SMALL_SEMS,)),
            dma((4,)),
        ],
        compiler_params=pltpu.CompilerParams(
            collective_id=1, has_side_effects=True, vmem_limit_bytes=56 * 2**20
        ),
        name="gather_weights",
    )(attn_in, attn_out, ff_in, ff_out, gains)
    return [w.reshape(768, -1) for w in weights] + [wide[:2]]


def reduce_all(grads, dgains, width):
    dma = pltpu.SemaphoreType.DMA
    grads = [g.reshape(4, 4, 48, -1) for g in grads]
    model = dgains.shape[1]
    return pl.pallas_call(
        reduce_kernel,
        out_shape=[jax.ShapeDtypeStruct((24, w), F32) for w in WIDTHS]
        + [jax.ShapeDtypeStruct((2, width), F32), jax.ShapeDtypeStruct((8, 128), F32)],
        in_specs=[any_spec()] * 4 + [vmem_spec()],
        out_specs=[vmem_spec()] * 6,
        scratch_shapes=[
            pltpu.VMEM((4, 4, 48, HALF), BF),
            pltpu.VMEM((4, 4, 48, HALF), BF),
            pltpu.VMEM((4, 48, HALF), BF),
            pltpu.VMEM((2, 4, 48, HALF), BF),
            pltpu.VMEM((3, 48, HALF), BF),
            pltpu.VMEM((2, 24, HALF), F32),
            pltpu.VMEM((24, HALF), F32),
            pltpu.VMEM((4, 8, model), F32),
            pltpu.VMEM((8, 8, model), F32),
            pltpu.VMEM((4, 8, 128), F32),
            pltpu.VMEM((8, 8, 128), F32),
            pltpu.VMEM((8, 128), F32),
            dma((COUNT * REDUCE_SEMS,)),
            dma((COUNT * REDUCE_SEMS,)),
            dma((2 * SMALL_SEMS,)),
            dma((2 * SMALL_SEMS,)),
            dma((COUNT,)),
        ],
        compiler_params=pltpu.CompilerParams(
            collective_id=2, has_side_effects=True, vmem_limit_bytes=56 * 2**20
        ),
        name="reduce_gradients",
    )(*grads, jnp.pad(dgains, ((0, 6), (0, 0))))


HD = 64
IMG = 257
STEP = 10


NORM_EPS = 1e-05
CLIP_NORM = 1.0
LEARN_RATES = (0.02, 0.1, 0.02, 0.02, 0.5)
FIRST_DECAY = 0.5
SECOND_DECAY = 0.5
ADAM_EPS = 1e-08
WEIGHT_DECAY = 0.05
ROPE_BASE = 10000.0
MASKED = -1e30
ROWS_CONTRACT = (((1,), (1,)), ((), ()))
TOKENS_CONTRACT = (((0,), (0,)), ((), ()))


def positions(begins, length):
    tok_index = jnp.arange(length, dtype=jnp.int32)
    began = begins[None, :] <= tok_index[:, None]
    segment = jnp.sum(began.astype(jnp.int32), axis=1)
    latest = jnp.max(jnp.where(began, begins[None, :], -4 * IMG), axis=1)
    return ((tok_index - latest).astype(jnp.float32), segment)


def rotation(rotary_place):
    half = HD // 2
    freq = ROPE_BASE ** (-jnp.arange(half, dtype=jnp.float32) * (2.0 / HD))
    angle = rotary_place[:, None] * freq[None, :]
    return (jnp.cos(angle), jnp.sin(angle))


def rotate(values, cosine, sine_table):
    half = values.shape[-1] // 2
    front, behind = (values[..., :half], values[..., half:])
    cos_part = cosine[:, None, :]
    sin_part = sine_table[:, None, :]
    return jnp.concatenate(
        [front * cos_part - behind * sin_part, behind * cos_part + front * sin_part], axis=-1
    )


def unrotate(grads, cosine, sine_table):
    half = grads.shape[-1] // 2
    front, behind = (grads[..., :half], grads[..., half:])
    cos_part = cosine[:, None, :]
    sin_part = sine_table[:, None, :]
    return jnp.concatenate(
        [front * cos_part + behind * sin_part, behind * cos_part - front * sin_part], axis=-1
    )


def norm_backward(normalized_gradient, standardized_input, inverse_norm, norm_gain):
    gain_scaled = normalized_gradient * norm_gain
    return inverse_norm * (
        gain_scaled
        - standardized_input * jnp.mean(gain_scaled * standardized_input, axis=-1, keepdims=True)
    )


def adam_update(weight, grad, first, second, clip_factor, decay, rate):
    grad = grad * clip_factor
    first = FIRST_DECAY * first + (1.0 - FIRST_DECAY) * grad
    second = SECOND_DECAY * second + (1.0 - SECOND_DECAY) * grad * grad
    fix_one = 1.0 - FIRST_DECAY**STEP
    fix_two = 1.0 - SECOND_DECAY**STEP
    change = first / fix_one / (jnp.sqrt(second / fix_two) + ADAM_EPS) + decay * weight
    return (weight - rate * change, first, second)


def body(
    fast,
    tokens,
    cotangent,
    starts,
    attn_in,
    attn_out,
    ff_in,
    ff_out,
    gains,
    attn_in_m,
    attn_out_m,
    ff_in_m,
    ff_out_m,
    gains_m,
    attn_in_v,
    attn_out_v,
    ff_in_v,
    ff_out_v,
    gains_v,
):
    length, model_width = tokens.shape
    head_count = model_width // HD
    hidden_width = ff_in.shape[1] // 2
    scale = HD ** (-0.5)
    lowered = (
        attn_in.astype(jnp.bfloat16),
        attn_out.astype(jnp.bfloat16),
        ff_in.astype(jnp.bfloat16),
        ff_out.astype(jnp.bfloat16),
        gains.astype(jnp.bfloat16),
    )
    if fast:
        w_qkv, w_out, w_in, w_down, paired_gains = gather_all(
            attn_in, attn_out, ff_in, ff_out, gains
        )
    else:
        w_qkv, w_out, w_in, w_down, paired_gains = (
            lax.all_gather(lowered[0], ("dp", "fsdp"), axis=0, tiled=True),
            lax.all_gather(lowered[1], ("dp", "fsdp"), axis=0, tiled=True),
            lax.all_gather(lowered[2], ("dp", "fsdp"), axis=0, tiled=True),
            lax.all_gather(lowered[3], ("dp", "fsdp"), axis=0, tiled=True),
            lax.all_gather(lowered[4], ("dp", "fsdp"), axis=1, tiled=True),
        )
        paired_gains = paired_gains.astype(jnp.float32)
    rotary_place, segment = positions(starts[0], length)
    cosine, sine_table = rotation(rotary_place)
    tok_index = jnp.arange(length, dtype=jnp.int32)
    allowed = (segment[:, None] == segment[None, :]) & (tok_index[None, :] <= tok_index[:, None])
    layer_input = tokens.astype(jnp.float32)
    first_inverse_norm = lax.rsqrt(
        jnp.mean(layer_input * layer_input, axis=-1, keepdims=True) + NORM_EPS
    )
    first_standardized = layer_input * first_inverse_norm
    first_normalized = (first_standardized * paired_gains[0]).astype(jnp.bfloat16)
    projected = jnp.dot(first_normalized, w_qkv, preferred_element_type=jnp.float32)
    query = rotate(
        projected[:, :model_width].reshape(length, head_count, HD), cosine, sine_table
    ).astype(jnp.bfloat16)
    keys = rotate(
        projected[:, model_width : 2 * model_width].reshape(length, head_count, HD),
        cosine,
        sine_table,
    ).astype(jnp.bfloat16)
    values = projected[:, 2 * model_width :].reshape(length, head_count, HD).astype(jnp.bfloat16)
    span_rows = min(512, length)
    starting = 0
    scores = jnp.einsum("qhd,khd->hqk", query, keys, preferred_element_type=jnp.float32) * scale
    scores = jnp.where(allowed[None, starting : starting + span_rows], scores, MASKED)
    highest = jnp.max(scores, axis=-1, keepdims=True)
    shifted = jnp.exp(scores - highest)
    totals = jnp.sum(shifted, axis=-1, keepdims=True)
    soft_weights = (shifted / totals).astype(jnp.bfloat16)
    mixed_parts = jnp.einsum(
        "hqk,khd->qhd", soft_weights, values, preferred_element_type=jnp.float32
    )
    total_parts = highest[..., 0] + jnp.log(totals[..., 0])
    mixed = mixed_parts.reshape(length, model_width).astype(jnp.bfloat16)
    residual_state = layer_input + lax.dot_general(
        mixed, w_out, ROWS_CONTRACT, preferred_element_type=jnp.float32
    )
    second_inverse_norm = lax.rsqrt(
        jnp.mean(residual_state * residual_state, axis=-1, keepdims=True) + NORM_EPS
    )
    second_standardized = residual_state * second_inverse_norm
    second_normalized = (second_standardized * paired_gains[1]).astype(jnp.bfloat16)
    gate_up = jnp.dot(second_normalized, w_in, preferred_element_type=jnp.float32)
    gate_part = gate_up[:, :hidden_width]
    up_part = gate_up[:, hidden_width:]
    sigmoid_gate = jax.nn.sigmoid(gate_part)
    swish = gate_part * sigmoid_gate
    activated = (swish * up_part).astype(jnp.bfloat16)
    block_out = residual_state + lax.dot_general(
        activated, w_down, ROWS_CONTRACT, preferred_element_type=jnp.float32
    )
    incoming_gradient = cotangent.astype(jnp.float32)
    grad_down = lax.dot_general(
        cotangent, activated, TOKENS_CONTRACT, preferred_element_type=jnp.float32
    )
    grad_act = jnp.dot(cotangent, w_down, preferred_element_type=jnp.float32)
    grad_gate = grad_act * up_part * sigmoid_gate * (1.0 + gate_part * (1.0 - sigmoid_gate))
    grad_up = grad_act * swish
    grad_gu = jnp.concatenate([grad_gate, grad_up], axis=1).astype(jnp.bfloat16)
    grad_in = lax.dot_general(
        second_normalized, grad_gu, TOKENS_CONTRACT, preferred_element_type=jnp.float32
    )
    second_normalized_gradient = lax.dot_general(
        grad_gu, w_in, ROWS_CONTRACT, preferred_element_type=jnp.float32
    )
    second_gain_gradient = jnp.sum(second_normalized_gradient * second_standardized, axis=0)
    residual_gradient = incoming_gradient + norm_backward(
        second_normalized_gradient, second_standardized, second_inverse_norm, paired_gains[1]
    )
    grad_branch = residual_gradient.astype(jnp.bfloat16)
    grad_out = lax.dot_general(
        grad_branch, mixed, TOKENS_CONTRACT, preferred_element_type=jnp.float32
    )
    grad_mixed = jnp.dot(grad_branch, w_out, preferred_element_type=jnp.float32).astype(
        jnp.bfloat16
    )
    grad_mixed = grad_mixed.reshape(length, head_count, HD)
    starting = 0
    scores = jnp.einsum("qhd,khd->hqk", query, keys, preferred_element_type=jnp.float32) * scale
    scores = jnp.where(allowed[None, starting : starting + span_rows], scores, MASKED)
    soft_weights = jnp.exp(scores - total_parts[:, starting : starting + span_rows, None])
    grad_soft = jnp.einsum("qhd,khd->hqk", grad_mixed, values, preferred_element_type=jnp.float32)
    centre = jnp.sum(soft_weights * grad_soft, axis=-1, keepdims=True)
    grad_scores = (soft_weights * (grad_soft - centre)).astype(jnp.bfloat16)
    query_parts = (
        jnp.einsum("hqk,khd->qhd", grad_scores, keys, preferred_element_type=jnp.float32) * scale
    )
    grad_keys = (
        jnp.einsum("hqk,qhd->khd", grad_scores, query, preferred_element_type=jnp.float32) * scale
    )
    grad_values = jnp.einsum(
        "hqk,qhd->khd",
        soft_weights.astype(jnp.bfloat16),
        grad_mixed,
        preferred_element_type=jnp.float32,
    )
    grad_query = unrotate(query_parts, cosine, sine_table)
    grad_keys = unrotate(grad_keys, cosine, sine_table)
    grad_proj = jnp.concatenate(
        [
            grad_query.reshape(length, model_width),
            grad_keys.reshape(length, model_width),
            grad_values.reshape(length, model_width),
        ],
        axis=1,
    ).astype(jnp.bfloat16)
    grad_qkv = lax.dot_general(
        first_normalized, grad_proj, TOKENS_CONTRACT, preferred_element_type=jnp.float32
    )
    first_normalized_gradient = lax.dot_general(
        grad_proj, w_qkv, ROWS_CONTRACT, preferred_element_type=jnp.float32
    )
    first_gain_gradient = jnp.sum(first_normalized_gradient * first_standardized, axis=0)
    token_input_gradient = residual_gradient + norm_backward(
        first_normalized_gradient, first_standardized, first_inverse_norm, paired_gains[0]
    )
    gain_gradients = jnp.stack([first_gain_gradient, second_gain_gradient])
    if fast:
        *shards, squares = reduce_all(
            [g.astype(BF) for g in (grad_qkv, grad_out, grad_in, grad_down)],
            gain_gradients,
            gains.shape[1],
        )
        global_squares = squares[0, 0]
    else:
        shard_qkv, shard_out, shard_in, shard_down, shard_gains = (
            lax.psum_scatter(grad_qkv, ("dp", "fsdp"), scatter_dimension=0, tiled=True),
            lax.psum_scatter(grad_out, ("dp", "fsdp"), scatter_dimension=0, tiled=True),
            lax.psum_scatter(grad_in, ("dp", "fsdp"), scatter_dimension=0, tiled=True),
            lax.psum_scatter(grad_down, ("dp", "fsdp"), scatter_dimension=0, tiled=True),
            lax.psum_scatter(
                jnp.stack([first_gain_gradient, second_gain_gradient]),
                ("dp", "fsdp"),
                scatter_dimension=1,
                tiled=True,
            ),
        )
        shards = (shard_qkv, shard_out, shard_in, shard_down, shard_gains)
        local_sum = sum((jnp.sum(piece * piece) for piece in shards))
        global_squares = lax.psum(local_sum, ("dp", "fsdp"))
    grad_norm = jnp.sqrt(global_squares)
    clip_factor = CLIP_NORM / jnp.maximum(grad_norm, CLIP_NORM)
    masters = (attn_in, attn_out, ff_in, ff_out, gains)
    firsts = (attn_in_m, attn_out_m, ff_in_m, ff_out_m, gains_m)
    seconds = (attn_in_v, attn_out_v, ff_in_v, ff_out_v, gains_v)
    decays = (WEIGHT_DECAY, WEIGHT_DECAY, WEIGHT_DECAY, WEIGHT_DECAY, 0.0)
    results = [
        adam_update(w, g, m, v, clip_factor, dec, rate)
        for w, g, m, v, dec, rate in zip(masters, shards, firsts, seconds, decays, LEARN_RATES)
    ]
    return (
        block_out,
        token_input_gradient,
        grad_norm,
        results[0][0],
        results[1][0],
        results[2][0],
        results[3][0],
        results[4][0],
        results[0][1],
        results[1][1],
        results[2][1],
        results[3][1],
        results[4][1],
        results[0][2],
        results[1][2],
        results[2][2],
        results[3][2],
        results[4][2],
    )


def solution(mesh):
    in_specs = (
        P(("dp", "fsdp"), None),
        P(("dp", "fsdp"), None),
        P(("dp", "fsdp"), None),
        P(("dp", "fsdp"), None),
        P(("dp", "fsdp"), None),
        P(("dp", "fsdp"), None),
        P(("dp", "fsdp"), None),
        P(None, ("dp", "fsdp")),
        P(("dp", "fsdp"), None),
        P(("dp", "fsdp"), None),
        P(("dp", "fsdp"), None),
        P(("dp", "fsdp"), None),
        P(None, ("dp", "fsdp")),
        P(("dp", "fsdp"), None),
        P(("dp", "fsdp"), None),
        P(("dp", "fsdp"), None),
        P(("dp", "fsdp"), None),
        P(None, ("dp", "fsdp")),
    )
    out_specs = (
        P(("dp", "fsdp"), None),
        P(("dp", "fsdp"), None),
        P(),
        P(("dp", "fsdp"), None),
        P(("dp", "fsdp"), None),
        P(("dp", "fsdp"), None),
        P(("dp", "fsdp"), None),
        P(None, ("dp", "fsdp")),
        P(("dp", "fsdp"), None),
        P(("dp", "fsdp"), None),
        P(("dp", "fsdp"), None),
        P(("dp", "fsdp"), None),
        P(None, ("dp", "fsdp")),
        P(("dp", "fsdp"), None),
        P(("dp", "fsdp"), None),
        P(("dp", "fsdp"), None),
        P(("dp", "fsdp"), None),
        P(None, ("dp", "fsdp")),
    )
    fast = dict(mesh.shape) == {"dp": 8, "fsdp": 4}
    run = functools.partial(body, fast)
    return jax.shard_map(run, mesh=mesh, in_specs=in_specs, out_specs=out_specs, check_vma=False)
```

```python
import functools

import jax
import jax.numpy as jnp
from jax import lax
from jax.experimental import pallas as pl
from jax.experimental.pallas import tpu as pltpu
from jax.sharding import PartitionSpec as P

BF = jnp.bfloat16
F32 = jnp.float32
MESH_ID = pl.DeviceIdType.MESH

WIDTHS = (2304, 768, 4096, 2048)
PIECES = (
    (0, 0, 384, 384, 128),
    (0, 768, 1152, 384, 256),
    (0, 1536, 1920, 384, 128),
    (1, 0, 384, 384, 256),
    (2, 0, 2048, 512, 256),
    (3, 0, 256, 256, 128),
    (2, 512, 2560, 512, 256),
    (3, 512, 768, 256, 128),
    (2, 1024, 3072, 512, 256),
    (3, 1024, 1280, 256, 128),
    (2, 1536, 3584, 512, 256),
    (3, 1536, 1792, 256, 128),
)
OFFSETS = tuple(sum(p[3] for p in PIECES[:k]) for k in range(len(PIECES)))
HALF = sum(p[3] for p in PIECES)
COUNT = len(PIECES)


class Place:
    def __init__(self):
        dp, fs = lax.axis_index("dp"), lax.axis_index("fsdp")
        self.dp, self.fs = dp, fs
        self.x, self.c = fs // 2, fs % 2
        self.z, self.y = dp // 2, dp % 2
        self.yx = self.y * 2 + self.x
        self.me = dp * 4 + fs
        self.sibling = (dp, self.x * 2 + 1 - self.c)
        self.xn = (dp, (1 - self.x) * 2 + self.c)
        self.yn = (self.z * 2 + 1 - self.y, fs)
        self.x_column = self.y * 2 + 1 - self.x
        self.y_column = (1 - self.y) * 2 + self.x
        self.diagonal = (1 - self.y) * 2 + 1 - self.x

    def z_peer(self, step):
        z = lax.rem(self.z + step, 4)
        return z, (z * 2 + self.y, self.fs)

    def group_peer(self, step):
        fs = lax.rem(self.fs + step, 4)
        return fs, (self.dp, fs)

    def plane_peer(self, step):
        dp = lax.rem(self.dp + step, 8)
        return dp, (dp, self.fs)

    def greet(self):
        barrier = pltpu.get_barrier_semaphore()
        for step in range(1, 4):
            pl.semaphore_signal(
                barrier, inc=1, device_id=self.group_peer(step)[1], device_id_type=MESH_ID
            )
        for step in range(1, 8):
            pl.semaphore_signal(
                barrier, inc=1, device_id=self.plane_peer(step)[1], device_id_type=MESH_ID
            )
        pl.semaphore_wait(barrier, 10)

    def columns(self, piece, sibling=False):
        first, second, width = piece[1], piece[2], piece[3]
        core = 1 - self.c if sibling else self.c
        start = jnp.where(core == 0, first, second)
        return pl.ds(pl.multiple_of(start, 128), width)

    def parts(self, piece):
        return (0, piece[4]), (piece[4], piece[3] - piece[4])


def remote(src, dst, send, recv, device):
    return pltpu.make_async_remote_copy(
        src_ref=src,
        dst_ref=dst,
        send_sem=send,
        recv_sem=recv,
        device_id=device,
        device_id_type=MESH_ID,
    )


GATHER_SEMS = 12
REDUCE_SEMS = 9


class Gather:
    def __init__(self, place, shards, whole, sibling_rows, send, recv):
        self.p, self.shards, self.whole = place, shards, whole
        self.rows, self.send, self.recv = sibling_rows, send, recv

    def copy(self, k, which):
        p, piece = self.p, PIECES[k]
        w = self.whole[piece[0]]
        sem = (self.send.at[k * GATHER_SEMS + which], self.recv.at[k * GATHER_SEMS + which])
        cols = p.columns(piece)

        def part(i):
            start, width = p.parts(piece)[i]
            return pl.ds(pl.multiple_of(cols.start + start, 128), width)

        if which == 0:
            shard = self.shards[piece[0]]
            return remote(
                shard.at[:, p.columns(piece, sibling=True)],
                self.rows.at[:, pl.ds(OFFSETS[k], piece[3])],
                *sem,
                p.sibling,
            )
        if which in (1, 2, 3):
            block = w.at[p.z, p.yx, :, cols]
            return remote(block, block, *sem, p.z_peer(which)[1])
        if which in (4, 5):
            block = w.at[:, p.yx, :, cols]
            return remote(block, block, *sem, (p.xn, p.yn)[which - 4])
        if which in (6, 7):
            along_x = p.c == which - 6
            column = jnp.where(along_x, p.y_column, p.x_column)
            block = w.at[:, column, :, part(which - 6)]
            device = (
                jnp.where(along_x, p.xn[0], p.yn[0]),
                jnp.where(along_x, p.xn[1], p.yn[1]),
            )
            return remote(block, block, *sem, device)
        column = (p.yx, p.x_column, p.y_column, p.diagonal)[which - 8]
        block = w.at[:, column, :, cols]
        return remote(block, block, *sem, p.sibling)

    def exchange(self, k):
        self.copy(k, 0).start()

    def begin(self, k):
        p, piece = self.p, PIECES[k]
        self.copy(k, 0).wait_recv()
        mine = self.shards[piece[0]][:, p.columns(piece)]
        other = self.rows[:, OFFSETS[k] : OFFSETS[k] + piece[3]]
        first = p.c == 0
        both = jnp.concatenate(
            [jnp.where(first, mine, other), jnp.where(first, other, mine)], axis=0
        )
        self.whole[piece[0]][p.z, p.yx, :, p.columns(piece)] = both.astype(BF)
        for i in (1, 2, 3):
            self.copy(k, i).start()

    def step1(self, k):
        for i in (1, 2, 3):
            self.copy(k, i).wait_recv()
        for i in (4, 5, 8):
            self.copy(k, i).start()

    def step2(self, k):
        for i in (4, 5):
            self.copy(k, i).wait_recv()
        for i in (6, 7, 9, 10):
            self.copy(k, i).start()

    def step3(self, k):
        for i in (6, 7):
            self.copy(k, i).wait_recv()
        self.copy(k, 11).start()

    def finish(self, k):
        for i in (8, 9, 10, 11):
            self.copy(k, i).wait_recv()

    def drain(self, k):
        for i in range(GATHER_SEMS):
            self.copy(k, i).wait_send()


class Reduce:
    def __init__(self, place, mine, other, landed, diag, cols, zed, done, got, send, recv):
        self.p = place
        self.mine, self.other, self.landed = mine, other, landed
        self.diag, self.cols, self.zed, self.done, self.got = diag, cols, zed, done, got
        self.send, self.recv = send, recv

    def copy(self, k, which):
        p, piece = self.p, PIECES[k]
        off, width = OFFSETS[k], piece[3]
        sem = (self.send.at[k * REDUCE_SEMS + which], self.recv.at[k * REDUCE_SEMS + which])
        span = pl.ds(off, width)
        if which == 0:
            return remote(
                self.other(k), self.landed.at[:, :, :, span], *sem, p.sibling
            )
        if which in (1, 2):
            start, wide = p.parts(piece)[which - 1]
            part = pl.ds(off + start, wide)
            along_x = p.c == which - 1
            device = (
                jnp.where(along_x, p.xn[0], p.yn[0]),
                jnp.where(along_x, p.xn[1], p.yn[1]),
            )
            return remote(
                self.mine.at[:, p.diagonal, :, part], self.diag.at[:, :, part], *sem, device
            )
        if which in (3, 4):
            column, device = ((p.x_column, p.xn), (p.y_column, p.yn))[which - 3]
            return remote(
                self.mine.at[:, column, :, span], self.cols.at[which - 3, :, :, span], *sem, device
            )
        if which in (5, 6, 7):
            z, device = p.z_peer(which - 4)
            return remote(
                self.mine.at[z, p.yx, :, span], self.zed.at[which - 5, :, span], *sem, device
            )
        return remote(
            self.done.at[1 - p.c, :, span], self.got.at[:, span], *sem, p.sibling
        )

    def begin(self, k):
        self.copy(k, 0).start()

    def step1(self, k):
        off, width = OFFSETS[k], PIECES[k][3]
        self.copy(k, 0).wait_recv()

        @pl.loop(0, 4)
        def _(z):
            for yx in range(4):
                total = self.mine[z, yx, :, off : off + width].astype(F32) + self.landed[
                    z, yx, :, off : off + width
                ].astype(F32)
                self.mine[z, yx, :, off : off + width] = total.astype(BF)

        for i in (1, 2):
            self.copy(k, i).start()

    def step2(self, k):
        p, piece = self.p, PIECES[k]
        off = OFFSETS[k]
        for i in (1, 2):
            self.copy(k, i).wait_recv()
        for i in (0, 1):
            start, wide = p.parts(piece)[i]
            column = jnp.where(p.c == i, p.y_column, p.x_column)
            part = slice(off + start, off + start + wide)

            @pl.loop(0, 4)
            def _(z):
                total = self.mine[z, column, :, part].astype(F32) + self.diag[z, :, part].astype(
                    F32
                )
                self.mine[z, column, :, part] = total.astype(BF)

        for i in (3, 4):
            self.copy(k, i).start()

    def step3(self, k):
        p = self.p
        off, width = OFFSETS[k], PIECES[k][3]
        span = slice(off, off + width)
        for i in (3, 4):
            self.copy(k, i).wait_recv()

        @pl.loop(0, 4)
        def _(z):
            total = (
                self.mine[z, p.yx, :, span].astype(F32)
                + self.cols[0, z, :, span].astype(F32)
                + self.cols[1, z, :, span].astype(F32)
            )
            self.mine[z, p.yx, :, span] = total.astype(BF)

        for i in (5, 6, 7):
            self.copy(k, i).start()

    def step4(self, k):
        p = self.p
        off, width = OFFSETS[k], PIECES[k][3]
        span = slice(off, off + width)
        for i in (5, 6, 7):
            self.copy(k, i).wait_recv()
        total = self.mine[p.z, p.yx, :, span].astype(F32)
        for i in range(3):
            total = total + self.zed[i, :, span].astype(F32)
        self.done[0, :, span] = total[:24]
        self.done[1, :, span] = total[24:]
        self.copy(k, 8).start()

    def finish(self, k):
        self.copy(k, 8).wait_recv()

    def drain(self, k):
        for i in range(REDUCE_SEMS):
            self.copy(k, i).wait_send()


SMALL_SEMS = 10


class Small:
    def __init__(self, place, group, plane, send, recv, base):
        self.p, self.group, self.plane = place, group, plane
        self.send, self.recv, self.base = send, recv, base

    def first(self, step):
        i = self.base + step - 1
        slot = self.group.at[self.p.fs]
        return remote(slot, slot, self.send.at[i], self.recv.at[i], self.p.group_peer(step)[1])

    def second(self, step):
        i = self.base + 2 + step
        slot = self.plane.at[self.p.dp]
        return remote(slot, slot, self.send.at[i], self.recv.at[i], self.p.plane_peer(step)[1])

    def start_first(self):
        for step in range(1, 4):
            self.first(step).start()

    def wait_first(self):
        for step in range(1, 4):
            self.first(step).wait_recv()

    def start_second(self):
        for step in range(1, 8):
            self.second(step).start()

    def wait_second(self):
        for step in range(1, 8):
            self.second(step).wait_recv()

    def drain(self):
        for step in range(1, 4):
            self.first(step).wait_send()
        for step in range(1, 8):
            self.second(step).wait_send()


def spread_gains(plane, count, wide, total):
    slots = plane.reshape(count, 8, 128)
    owner = lax.broadcasted_iota(jnp.int32, (count, total), 1) // wide
    pick = (owner == lax.broadcasted_iota(jnp.int32, (count, total), 0)).astype(F32)
    lane = lax.broadcasted_iota(jnp.int32, (128, total), 1) % wide
    keep = lane == lax.broadcasted_iota(jnp.int32, (128, total), 0)
    rows = []
    for g in range(2):
        spread = lax.dot_general(
            slots[:, g, :], pick, (((0,), (0,)), ((), ())), preferred_element_type=F32
        )
        rows.append(jnp.sum(jnp.where(keep, spread, 0.0), axis=0, keepdims=True))
    return rows


TOKENS_PER = 512
MODEL = 768
PAIRS = MODEL // 128
BLOCK = 512
ROW_STEP = 64
LAST_PIECES = (4, 5, 6, 7, 8, 9, 10, 11, 3, 0, 1, 2)


def nn(a, b):
    return lax.dot_general(a, b, (((1,), (0,)), ((), ())), preferred_element_type=F32)


def nt(a, b):
    return lax.dot_general(a, b, (((1,), (1,)), ((), ())), preferred_element_type=F32)


def tn(a, b):
    return lax.dot_general(a, b, (((0,), (0,)), ((), ())), preferred_element_type=F32)


def aligned(start, size):
    return pl.ds(pl.multiple_of(start, 128), size)


def layer_kernel(
    tok, cot, starts, freq, gains, w0, w1, w2, w3,
    block_out, token_grad, shard0, shard1, shard2, shard3, gain_shard, square_out,
    big0, big1, big2, big3, rows, group, plane,
    mine, landed, diag, cols_in, zed, done, got, group_g, plane_g, group_s, plane_s,
    theirs_ff, theirs_at, gain_rows, dgain, cosine, signed_sine, bias, logs,
    h1, h1_t, query, keys, values, state, out_acc, dnorm, h2, h2_t, dy_t, dmixed,
    gate, up, dact, act, dgu,
    g_send, g_recv, r_send, r_recv, s_send, s_recv, local,
):
    place = Place()
    place.greet()
    whole = (big0, big1, big2, big3)
    mixed = h1
    gather = Gather(place, (w0, w1, w2, w3), whole, rows, g_send, g_recv)
    for k in range(COUNT):
        gather.exchange(k)

    wide = gains.shape[1]
    small = Small(place, group, plane, s_send, s_recv, 0)
    small_g = Small(place, group_g, plane_g, s_send, s_recv, SMALL_SEMS)
    small_s = Small(place, group_s, plane_s, s_send, s_recv, 2 * SMALL_SEMS)
    group[place.fs] = jnp.zeros((8, 128), F32)
    group[place.fs, 0:2, 0:wide] = gains[...].astype(BF).astype(F32)
    small.start_first()

    queue = []
    for slot in range(-2, COUNT + 4):
        for stage, lag in (
            (gather.finish, 3),
            (gather.step3, 2),
            (gather.step2, 1),
            (gather.step1, 0),
            (gather.begin, -2),
        ):
            k = slot - lag
            if 0 <= k < COUNT:
                queue.append((stage, k))

    def tick(n):
        for _ in range(min(n, len(queue))):
            stage, k = queue.pop(0)
            stage(k)

    def until(k, stage=gather.finish):
        while (stage, k) in queue:
            tick(1)

    until(1, gather.begin)
    small.wait_first()
    for i in range(4):
        plane[place.dp, i] = group[i]
    small.start_second()

    tokens_n = TOKENS_PER
    images = starts.shape[1]

    def began(t):
        latest = jnp.full(t.shape, -(10**6), jnp.int32)
        for j in range(images):
            s = starts[0, j]
            latest = jnp.maximum(latest, jnp.where(s <= t, s, -(10**6)))
        return latest

    @pl.loop(0, tokens_n // ROW_STEP)
    def _(i):
        r = pl.ds(pl.multiple_of(i * ROW_STEP, ROW_STEP), ROW_STEP)
        t = lax.broadcasted_iota(jnp.int32, (ROW_STEP, 128), 0) + i * ROW_STEP
        angle = (t - began(t)).astype(F32) * freq[0:1, :]
        cosine[r, :] = jnp.cos(angle)
        lane = lax.broadcasted_iota(jnp.int32, (ROW_STEP, 128), 1)
        signed_sine[r, :] = jnp.where(lane % 64 < 32, -1.0, 1.0) * jnp.sin(angle)
        u = lax.broadcasted_iota(jnp.int32, (ROW_STEP, tokens_n), 0) + i * ROW_STEP
        t = lax.broadcasted_iota(jnp.int32, (1, tokens_n), 1)
        bias[r, :] = jnp.where((u <= t) & (u >= began(t)), 0.0, -1e30)

    small.wait_second()
    first, second = spread_gains(plane, 32, wide, MODEL)
    gain_rows[0:1, :] = first
    gain_rows[1:2, :] = second
    dgain[...] = jnp.zeros_like(dgain)

    def inverse(x):
        return lax.rsqrt(jnp.mean(x * x, axis=-1, keepdims=True) + 1e-05)

    def row_loop(body):
        @pl.loop(0, tokens_n // ROW_STEP)
        def _(i):
            body(pl.ds(pl.multiple_of(i * ROW_STEP, ROW_STEP), ROW_STEP))

    def normed(source, gain, dest):
        def body(r):
            x = source[r, :].astype(F32)
            dest[r, :] = (x * inverse(x) * gain_rows[gain : gain + 1, :]).astype(BF)

        row_loop(body)

    def turn(source, dest):
        @pl.loop(0, PAIRS)
        def _(n):
            c = aligned(n * 128, 128)
            dest[c, :] = source[:, c].T

    normed(tok, 0, h1)
    turn(h1, h1_t)
    turn(cot, dy_t)

    def weight(k, c):
        block = whole[k][:, :, :, c]
        return block.reshape(MODEL, block.shape[-1])

    lane = lax.broadcasted_iota(jnp.int32, (1, 128), 1)
    front = lane % 64 < 32
    of_head = (lane < 64, lane >= 64)

    def swap(v):
        return jnp.where(front, pltpu.roll(v, 96, 1), pltpu.roll(v, 32, 1))

    def project(part, dest):
        @pl.loop(0, MODEL // 256)
        def _(n):
            p = nn(h1[...], weight(0, aligned(part * MODEL + n * 256, 256)))
            for half in range(2):
                v = p[:, half * 128 : half * 128 + 128]
                if part < 2:
                    v = v * cosine[...] + swap(v) * signed_sine[...]
                v = v.astype(BF)
                if part == 0:
                    v = v * jnp.asarray(0.125, BF)
                dest[:, aligned(n * 256 + half * 128, 128)] = v

    def only(v, head):
        return jnp.where(of_head[head], v, jnp.zeros((), v.dtype))

    def attend(n):
        c = aligned(n * 128, 128)
        k, v, q = keys[:, c], values[:, c], query[:, c]
        for i in range(2):
            t, u = slice(256 * i, 256 * i + 256), slice(0, 256 * i + 256)
            o = []
            for head in range(2):
                s = nt(k[u], only(q[t], head)) + bias[u, t]
                top = jnp.max(s, axis=0, keepdims=True)
                p = jnp.exp(s - top)
                total = jnp.sum(p, axis=0, keepdims=True)
                p = (p * (1.0 / total)).astype(BF)
                logs[n, head : head + 1, t] = top + jnp.log(total)
                o.append(tn(p, v[u]))
            mixed[t, c] = jnp.where(of_head[0], o[0], o[1]).astype(BF)

    def attend_back(n):
        c = aligned(n * 128, 128)
        k, v, q, do = keys[:, c], values[:, c], query[:, c], dmixed[:, c]
        dq, dk, dv = [None, None], [], []
        low_k = low_v = high_k = high_v = None

        def plus(a, b):
            return b if a is None else a + b

        for head in range(2):
            km = only(k, head)
            for i in range(2):
                t, u = slice(256 * i, 256 * i + 256), slice(0, 256 * i + 256)
                qm, dom = only(q[t], head), only(do[t], head)
                s = nt(k[u], qm) + bias[u, t]
                p = jnp.exp(s - logs[n, head : head + 1, t])
                dp = nt(v[u], dom)
                centre = jnp.sum(p * dp, axis=0, keepdims=True)
                ds = (p * (dp - centre)).astype(BF)
                pb = p.astype(BF)
                dq[i] = plus(dq[i], tn(ds, km[u]))
                dk, dv = nn(ds, qm), nn(pb, dom)
                low_k, low_v = plus(low_k, dk[:256]), plus(low_v, dv[:256])
                if i == 1:
                    high_k, high_v = plus(high_k, dk[256:]), plus(high_v, dv[256:])

        def back(v, t):
            return v * cosine[t, :] - swap(v) * signed_sine[t, :]

        for i in range(2):
            t = slice(256 * i, 256 * i + 256)
            query[t, c] = back(dq[i] * 0.125, t).astype(BF)
            keys[t, c] = back((low_k, high_k)[i], t).astype(BF)
            values[t, c] = (low_v, high_v)[i].astype(BF)

    until(0)
    project(0, query)
    until(1)
    project(1, keys)
    until(2)
    project(2, values)
    for n in range(3):
        pl.loop(2 * n, 2 * n + 2)(attend)
        tick(5)
    until(3)

    for n in range(3):
        c = slice(n * 256, n * 256 + 256)
        state[:, c] = tok[:, c].astype(F32) + nt(mixed[...], weight(1, slice(None))[c])
    normed(state, 1, h2)
    turn(h2, h2_t)

    def theirs(k):
        if k < 4:
            return theirs_at.at[:, :, :, pl.ds(OFFSETS[k], PIECES[k][3])]
        j, second = (k - 4) // 2, (k - 4) % 2
        return theirs_ff.at[j % 2, :, :, :, pl.ds(512 * second, 256 if second else 512)]

    reduce = Reduce(
        place, mine, theirs, landed, diag, cols_in, zed, done, got, r_send, r_recv
    )
    reduced = []
    square = [jnp.zeros((1, 1), F32)]
    shards = (shard0, shard1, shard2, shard3)

    def write_shard(k):
        piece = PIECES[k]
        span = pl.ds(OFFSETS[k], piece[3])
        return [
            pltpu.make_async_copy(
                source, shards[piece[0]].at[:, place.columns(piece, sibling)], local.at[i]
            )
            for source, sibling, i in (
                (done.at[place.c, :, span], False, 2 + 2 * k),
                (got.at[:, span], True, 3 + 2 * k),
            )
        ]

    def finish(k):
        reduce.finish(k)
        piece = PIECES[k]
        span = slice(OFFSETS[k], OFFSETS[k] + piece[3])
        a, b = done[place.c, :, span], got[:, span]
        for copy in write_shard(k):
            copy.start()
        square[0] = square[0] + jnp.sum(a * a + b * b, axis=(0, 1), keepdims=True)

    sums = []
    for slot in range(COUNT + 4):
        for stage, lag in (
            (finish, 4),
            (reduce.step4, 3),
            (reduce.step3, 2),
            (reduce.step2, 1),
            (reduce.step1, 0),
        ):
            i = slot - lag
            if 0 <= i < COUNT:
                sums.append((stage, LAST_PIECES[i]))

    def add(n):
        for _ in range(n):
            if not sums:
                return
            stage, k = sums[0]
            if stage == reduce.step1 and k not in reduced:
                return
            sums.pop(0)
            stage(k)

    drained = set()

    def send_gradient(k, left, right, base):
        piece = PIECES[k]
        width = piece[3]
        step = 256 if width % 256 == 0 else 128

        def run(core, store):
            @pl.loop(0, width // step)
            def _(n):
                g = nn(left[...], right[:, aligned(base + core * width + n * step, step)])
                store(n * step, g.astype(BF).reshape(4, 4, 48, step))

        other = theirs(k)

        def to_other(start, g):
            other[:, :, :, aligned(start, step)] = g

        def to_mine(start, g):
            mine[:, :, :, aligned(OFFSETS[k] + start, step)] = g

        run(1 - place.c, to_other)
        reduce.begin(k)
        run(place.c, to_mine)
        reduced.append(k)

    out_acc[...] = state[...]
    dnorm[...] = jnp.zeros_like(dnorm)
    for j in range(4):
        kf, kd = 4 + 2 * j, 5 + 2 * j
        until(kd)
        gcols, ucols = slice(j * BLOCK, j * BLOCK + BLOCK), slice(2048 + j * BLOCK, 2048 + j * BLOCK + BLOCK)
        for n in range(BLOCK // 256):
            c = slice(n * 256, n * 256 + 256)
            gc = slice(gcols.start + c.start, gcols.start + c.stop)
            uc = slice(ucols.start + c.start, ucols.start + c.stop)
            gate[...] = nn(h2[...], weight(2, gc))
            up[...] = nn(h2[...], weight(2, uc))
            dact[...] = nn(cot[...], weight(3, gc))

            def pointwise(r):
                z, w, da = gate[r, :], up[r, :], dact[r, :]
                s = jax.nn.sigmoid(z)
                swish = z * s
                act[r, c] = (swish * w).astype(BF)
                dgu[r, c] = (da * w * s * (1.0 + z * (1.0 - s))).astype(BF)
                dgu[r, BLOCK + c.start : BLOCK + c.stop] = (da * swish).astype(BF)

            row_loop(pointwise)
            tick(2)

        if j >= 2:
            for k in (kf - 4, kd - 4):
                reduce.copy(k, 0).wait_send()
                drained.add(k)
        send_gradient(kf, h2_t, dgu, 0)
        tick(3)
        send_gradient(kd, dy_t, act, 0)
        add(5)
        tick(3)
        for n in range(3):
            c = slice(n * 256, n * 256 + 256)
            out_acc[:, c] += nt(act[...], weight(3, gcols)[c])
            dnorm[:, c] += nt(dgu[:, 0:BLOCK], weight(2, gcols)[c]) + nt(
                dgu[:, BLOCK : 2 * BLOCK], weight(2, ucols)[c]
            )
        add(5)
    write_out = pltpu.make_async_copy(out_acc, block_out, local.at[0])
    write_out.start()

    def second_norm(r):
        x = state[r, :]
        inv = inverse(x)
        xh = x * inv
        dh = dnorm[r, :]
        dgain[1:2, :] += jnp.sum(dh * xh, axis=0, keepdims=True)
        e = dh * gain_rows[1:2, :]
        d = cot[r, :].astype(F32) + inv * (e - xh * jnp.mean(e * xh, axis=-1, keepdims=True))
        state[r, :] = d
        h2[r, :] = d.astype(BF)

    row_loop(second_norm)
    turn(h2, h2_t)
    add(3)
    send_gradient(3, h2_t, mixed, 0)
    for n in range(3):
        c = slice(n * 256, n * 256 + 256)
        dmixed[:, c] = nn(h2[...], weight(1, c)).astype(BF)
    add(3)
    for n in range(6):
        pl.loop(n, n + 1)(attend_back)
        add(4)
    send_gradient(0, h1_t, query, 0)
    add(4)
    send_gradient(1, h1_t, keys, 0)
    add(4)
    send_gradient(2, h1_t, values, 0)
    add(4)
    for n in range(3):
        c = slice(n * 256, n * 256 + 256)
        dnorm[:, c] = (
            nt(query[...], weight(0, slice(0, MODEL))[c])
            + nt(keys[...], weight(0, slice(MODEL, 2 * MODEL))[c])
            + nt(values[...], weight(0, slice(2 * MODEL, 3 * MODEL))[c])
        )
    add(4)

    def first_norm(r):
        x = tok[r, :].astype(F32)
        inv = inverse(x)
        xh = x * inv
        dh = dnorm[r, :]
        dgain[0:1, :] += jnp.sum(dh * xh, axis=0, keepdims=True)
        e = dh * gain_rows[0:1, :]
        state[r, :] += inv * (e - xh * jnp.mean(e * xh, axis=-1, keepdims=True))

    row_loop(first_norm)
    write_grad = pltpu.make_async_copy(state, token_grad, local.at[1])
    write_grad.start()
    group_g[place.fs] = dgain[...]
    small_g.start_first()
    add(4)
    small_g.wait_first()
    plane_g[place.dp] = group_g[0] + group_g[1] + group_g[2] + group_g[3]
    small_g.start_second()
    add(1000)
    small_g.wait_second()
    total = plane_g[0]
    for i in range(1, 8):
        total = total + plane_g[i]
    row = lax.broadcasted_iota(jnp.int32, (MODEL, 128), 0)
    lane = lax.broadcasted_iota(jnp.int32, (MODEL, 128), 1)
    wanted = (row == place.me * wide + lane) & (lane < wide)
    own = jnp.dot(
        total,
        wanted.astype(F32),
        preferred_element_type=F32,
        precision=lax.Precision.HIGHEST,
    )[0:2]
    gain_shard[...] = own[:, 0:wide]
    squares = square[0] + jnp.sum(own * own, axis=(0, 1), keepdims=True)
    group_s[place.fs] = jnp.broadcast_to(squares, (8, 128))
    small_s.start_first()
    small_s.wait_first()
    plane_s[place.dp] = group_s[0] + group_s[1] + group_s[2] + group_s[3]
    small_s.start_second()
    for k in range(COUNT):
        gather.drain(k)
        for i in range(1 if k in drained else 0, REDUCE_SEMS):
            reduce.copy(k, i).wait_send()
    small.drain()
    small_g.drain()
    write_out.wait()
    write_grad.wait()
    for k in range(COUNT):
        for copy in write_shard(k):
            copy.wait()
    small_s.wait_second()
    squares = plane_s[0]
    for i in range(1, 8):
        squares = squares + plane_s[i]
    square_out[...] = squares
    small_s.drain()


def update_kernel(*refs):
    squares, out_block, out_grad = refs[0:3]
    grads, weights, firsts, seconds = (refs[3 + 5 * i : 8 + 5 * i] for i in range(4))
    new_block, new_grad, norm = refs[23:26]
    new_w, new_m, new_v = (refs[26 + 5 * i : 31 + 5 * i] for i in range(3))
    local = refs[41]
    copies = [
        pltpu.make_async_copy(out_block, new_block, local.at[0]),
        pltpu.make_async_copy(out_grad, new_grad, local.at[1]),
    ]
    for copy in copies:
        copy.start()
    root = jnp.sqrt(squares[0:1, 0:1])
    norm[...] = root
    clip = CLIP_NORM / jnp.maximum(root, CLIP_NORM)
    decays = (WEIGHT_DECAY, WEIGHT_DECAY, WEIGHT_DECAY, WEIGHT_DECAY, 0.0)
    for i in range(5):
        step = 256 if weights[i].shape[1] % 256 == 0 else weights[i].shape[1]
        for n in range(weights[i].shape[1] // step):
            c = slice(n * step, n * step + step)
            results = adam_update(
                weights[i][:, c], grads[i][:, c], firsts[i][:, c], seconds[i][:, c],
                clip, decays[i], LEARN_RATES[i],
            )
            for dest, value in zip((new_w, new_m, new_v), results):
                dest[i][:, c] = value
    for copy in copies:
        copy.wait()


def any_spec():
    return pl.BlockSpec(memory_space=pl.ANY)


def vmem_spec():
    return pl.BlockSpec(memory_space=pltpu.VMEM)


def fast_body(tokens, cotangent, starts, *state):
    weights, firsts, seconds = state[0:5], state[5:10], state[10:15]
    wide = weights[4].shape[1]
    half = HD // 2
    place = jnp.arange(128, dtype=jnp.int32) % half
    freq = ROPE_BASE ** (-place.astype(F32) * (2.0 / HD))
    dma = pltpu.SemaphoreType.DMA
    shape = jax.ShapeDtypeStruct
    tall = (TOKENS_PER, MODEL)
    scratch = [pltpu.VMEM((4, 4, 48, w), BF) for w in WIDTHS] + [
        pltpu.VMEM((24, HALF), F32),
        pltpu.VMEM((4, 8, 128), F32),
        pltpu.VMEM((8, 4, 8, 128), F32),
        pltpu.VMEM((4, 4, 48, HALF), BF),
        pltpu.VMEM((4, 4, 48, HALF), BF),
        pltpu.VMEM((4, 48, HALF), BF),
        pltpu.VMEM((2, 4, 48, HALF), BF),
        pltpu.VMEM((3, 48, HALF), BF),
        pltpu.VMEM((2, 24, HALF), F32),
        pltpu.VMEM((24, HALF), F32),
        pltpu.VMEM((4, 8, MODEL), F32),
        pltpu.VMEM((8, 8, MODEL), F32),
        pltpu.VMEM((4, 8, 128), F32),
        pltpu.VMEM((8, 8, 128), F32),
        pltpu.VMEM((2, 4, 4, 48, 768), BF),
        pltpu.VMEM((4, 4, 48, 1536), BF),
        pltpu.VMEM((8, MODEL), F32),
        pltpu.VMEM((8, MODEL), F32),
        pltpu.VMEM((TOKENS_PER, 128), F32),
        pltpu.VMEM((TOKENS_PER, 128), F32),
        pltpu.VMEM((TOKENS_PER, TOKENS_PER), F32),
        pltpu.VMEM((PAIRS, 8, TOKENS_PER), F32),
        pltpu.VMEM(tall, BF),
        pltpu.VMEM((MODEL, TOKENS_PER), BF),
        pltpu.VMEM(tall, BF),
        pltpu.VMEM(tall, BF),
        pltpu.VMEM(tall, BF),
        pltpu.VMEM(tall, F32),
        pltpu.VMEM(tall, F32),
        pltpu.VMEM(tall, F32),
        pltpu.VMEM(tall, BF),
        pltpu.VMEM((MODEL, TOKENS_PER), BF),
        pltpu.VMEM((MODEL, TOKENS_PER), BF),
        pltpu.VMEM(tall, BF),
        pltpu.VMEM((TOKENS_PER, 256), F32),
        pltpu.VMEM((TOKENS_PER, 256), F32),
        pltpu.VMEM((TOKENS_PER, 256), F32),
        pltpu.VMEM((TOKENS_PER, BLOCK), BF),
        pltpu.VMEM((TOKENS_PER, 2 * BLOCK), BF),
        dma((COUNT * GATHER_SEMS,)),
        dma((COUNT * GATHER_SEMS,)),
        dma((COUNT * REDUCE_SEMS,)),
        dma((COUNT * REDUCE_SEMS,)),
        dma((3 * SMALL_SEMS,)),
        dma((3 * SMALL_SEMS,)),
        dma((2 + 2 * COUNT,)),
    ]
    block_out, token_grad, *shards, squares = pl.pallas_call(
        layer_kernel,
        out_shape=[shape(tall, F32)] * 2
        + [shape((24, w), F32) for w in WIDTHS]
        + [shape((2, wide), F32), shape((8, 128), F32)],
        in_specs=[vmem_spec()] * 2
        + [pl.BlockSpec(memory_space=pltpu.SMEM)]
        + [vmem_spec()] * 6,
        out_specs=[any_spec()] * 6 + [vmem_spec()] * 2,
        scratch_shapes=scratch,
        compiler_params=pltpu.CompilerParams(
            collective_id=1, has_side_effects=True, vmem_limit_bytes=64 * 2**20 - 2**18
        ),
        name="layer_and_gradients",
    )(tokens, cotangent, starts, freq.reshape(1, 128), weights[4], *weights[0:4])
    outs = pl.pallas_call(
        update_kernel,
        out_shape=[shape(tall, F32)] * 2
        + [shape((1, 1), F32)]
        + [shape(w.shape, F32) for _ in range(3) for w in weights],
        in_specs=[vmem_spec()] * 23,
        out_specs=[any_spec()] * 2 + [vmem_spec()] * 16,
        scratch_shapes=[dma((2,))],
        compiler_params=pltpu.CompilerParams(vmem_limit_bytes=64 * 2**20 - 2**18),
        name="update_weights",
    )(squares, block_out, token_grad, *shards, *weights, *firsts, *seconds)
    return (outs[0], outs[1], outs[2].reshape(()), *outs[3:])


HD = 64
IMG = 257
STEP = 10


NORM_EPS = 1e-05
CLIP_NORM = 1.0
LEARN_RATES = (0.02, 0.1, 0.02, 0.02, 0.5)
FIRST_DECAY = 0.5
SECOND_DECAY = 0.5
ADAM_EPS = 1e-08
WEIGHT_DECAY = 0.05
ROPE_BASE = 10000.0
MASKED = -1e30
ROWS_CONTRACT = (((1,), (1,)), ((), ()))
TOKENS_CONTRACT = (((0,), (0,)), ((), ()))


def positions(begins, length):
    tok_index = jnp.arange(length, dtype=jnp.int32)
    began = begins[None, :] <= tok_index[:, None]
    segment = jnp.sum(began.astype(jnp.int32), axis=1)
    latest = jnp.max(jnp.where(began, begins[None, :], -4 * IMG), axis=1)
    return ((tok_index - latest).astype(jnp.float32), segment)


def rotation(rotary_place):
    half = HD // 2
    freq = ROPE_BASE ** (-jnp.arange(half, dtype=jnp.float32) * (2.0 / HD))
    angle = rotary_place[:, None] * freq[None, :]
    return (jnp.cos(angle), jnp.sin(angle))


def rotate(values, cosine, sine_table):
    half = values.shape[-1] // 2
    front, behind = (values[..., :half], values[..., half:])
    cos_part = cosine[:, None, :]
    sin_part = sine_table[:, None, :]
    return jnp.concatenate(
        [front * cos_part - behind * sin_part, behind * cos_part + front * sin_part], axis=-1
    )


def unrotate(grads, cosine, sine_table):
    half = grads.shape[-1] // 2
    front, behind = (grads[..., :half], grads[..., half:])
    cos_part = cosine[:, None, :]
    sin_part = sine_table[:, None, :]
    return jnp.concatenate(
        [front * cos_part + behind * sin_part, behind * cos_part - front * sin_part], axis=-1
    )


def norm_backward(normalized_gradient, standardized_input, inverse_norm, norm_gain):
    gain_scaled = normalized_gradient * norm_gain
    return inverse_norm * (
        gain_scaled
        - standardized_input * jnp.mean(gain_scaled * standardized_input, axis=-1, keepdims=True)
    )


def adam_update(weight, grad, first, second, clip_factor, decay, rate):
    grad = grad * clip_factor
    first = FIRST_DECAY * first + (1.0 - FIRST_DECAY) * grad
    second = SECOND_DECAY * second + (1.0 - SECOND_DECAY) * grad * grad
    fix_one = 1.0 - FIRST_DECAY**STEP
    fix_two = 1.0 - SECOND_DECAY**STEP
    change = first / fix_one / (jnp.sqrt(second / fix_two) + ADAM_EPS) + decay * weight
    return (weight - rate * change, first, second)


def body(
    tokens,
    cotangent,
    starts,
    attn_in,
    attn_out,
    ff_in,
    ff_out,
    gains,
    attn_in_m,
    attn_out_m,
    ff_in_m,
    ff_out_m,
    gains_m,
    attn_in_v,
    attn_out_v,
    ff_in_v,
    ff_out_v,
    gains_v,
):
    length, model_width = tokens.shape
    head_count = model_width // HD
    hidden_width = ff_in.shape[1] // 2
    scale = HD ** (-0.5)
    lowered = (
        attn_in.astype(jnp.bfloat16),
        attn_out.astype(jnp.bfloat16),
        ff_in.astype(jnp.bfloat16),
        ff_out.astype(jnp.bfloat16),
        gains.astype(jnp.bfloat16),
    )
    w_qkv, w_out, w_in, w_down, paired_gains = (
        lax.all_gather(lowered[0], ("dp", "fsdp"), axis=0, tiled=True),
        lax.all_gather(lowered[1], ("dp", "fsdp"), axis=0, tiled=True),
        lax.all_gather(lowered[2], ("dp", "fsdp"), axis=0, tiled=True),
        lax.all_gather(lowered[3], ("dp", "fsdp"), axis=0, tiled=True),
        lax.all_gather(lowered[4], ("dp", "fsdp"), axis=1, tiled=True),
    )
    paired_gains = paired_gains.astype(jnp.float32)
    rotary_place, segment = positions(starts[0], length)
    cosine, sine_table = rotation(rotary_place)
    tok_index = jnp.arange(length, dtype=jnp.int32)
    allowed = (segment[:, None] == segment[None, :]) & (tok_index[None, :] <= tok_index[:, None])
    layer_input = tokens.astype(jnp.float32)
    first_inverse_norm = lax.rsqrt(
        jnp.mean(layer_input * layer_input, axis=-1, keepdims=True) + NORM_EPS
    )
    first_standardized = layer_input * first_inverse_norm
    first_normalized = (first_standardized * paired_gains[0]).astype(jnp.bfloat16)
    projected = jnp.dot(first_normalized, w_qkv, preferred_element_type=jnp.float32)
    query = rotate(
        projected[:, :model_width].reshape(length, head_count, HD), cosine, sine_table
    ).astype(jnp.bfloat16)
    keys = rotate(
        projected[:, model_width : 2 * model_width].reshape(length, head_count, HD),
        cosine,
        sine_table,
    ).astype(jnp.bfloat16)
    values = projected[:, 2 * model_width :].reshape(length, head_count, HD).astype(jnp.bfloat16)
    span_rows = min(512, length)
    starting = 0
    scores = jnp.einsum("qhd,khd->hqk", query, keys, preferred_element_type=jnp.float32) * scale
    scores = jnp.where(allowed[None, starting : starting + span_rows], scores, MASKED)
    highest = jnp.max(scores, axis=-1, keepdims=True)
    shifted = jnp.exp(scores - highest)
    totals = jnp.sum(shifted, axis=-1, keepdims=True)
    soft_weights = (shifted / totals).astype(jnp.bfloat16)
    mixed_parts = jnp.einsum(
        "hqk,khd->qhd", soft_weights, values, preferred_element_type=jnp.float32
    )
    total_parts = highest[..., 0] + jnp.log(totals[..., 0])
    mixed = mixed_parts.reshape(length, model_width).astype(jnp.bfloat16)
    residual_state = layer_input + lax.dot_general(
        mixed, w_out, ROWS_CONTRACT, preferred_element_type=jnp.float32
    )
    second_inverse_norm = lax.rsqrt(
        jnp.mean(residual_state * residual_state, axis=-1, keepdims=True) + NORM_EPS
    )
    second_standardized = residual_state * second_inverse_norm
    second_normalized = (second_standardized * paired_gains[1]).astype(jnp.bfloat16)
    gate_up = jnp.dot(second_normalized, w_in, preferred_element_type=jnp.float32)
    gate_part = gate_up[:, :hidden_width]
    up_part = gate_up[:, hidden_width:]
    sigmoid_gate = jax.nn.sigmoid(gate_part)
    swish = gate_part * sigmoid_gate
    activated = (swish * up_part).astype(jnp.bfloat16)
    block_out = residual_state + lax.dot_general(
        activated, w_down, ROWS_CONTRACT, preferred_element_type=jnp.float32
    )
    incoming_gradient = cotangent.astype(jnp.float32)
    grad_down = lax.dot_general(
        cotangent, activated, TOKENS_CONTRACT, preferred_element_type=jnp.float32
    )
    grad_act = jnp.dot(cotangent, w_down, preferred_element_type=jnp.float32)
    grad_gate = grad_act * up_part * sigmoid_gate * (1.0 + gate_part * (1.0 - sigmoid_gate))
    grad_up = grad_act * swish
    grad_gu = jnp.concatenate([grad_gate, grad_up], axis=1).astype(jnp.bfloat16)
    grad_in = lax.dot_general(
        second_normalized, grad_gu, TOKENS_CONTRACT, preferred_element_type=jnp.float32
    )
    second_normalized_gradient = lax.dot_general(
        grad_gu, w_in, ROWS_CONTRACT, preferred_element_type=jnp.float32
    )
    second_gain_gradient = jnp.sum(second_normalized_gradient * second_standardized, axis=0)
    residual_gradient = incoming_gradient + norm_backward(
        second_normalized_gradient, second_standardized, second_inverse_norm, paired_gains[1]
    )
    grad_branch = residual_gradient.astype(jnp.bfloat16)
    grad_out = lax.dot_general(
        grad_branch, mixed, TOKENS_CONTRACT, preferred_element_type=jnp.float32
    )
    grad_mixed = jnp.dot(grad_branch, w_out, preferred_element_type=jnp.float32).astype(
        jnp.bfloat16
    )
    grad_mixed = grad_mixed.reshape(length, head_count, HD)
    starting = 0
    scores = jnp.einsum("qhd,khd->hqk", query, keys, preferred_element_type=jnp.float32) * scale
    scores = jnp.where(allowed[None, starting : starting + span_rows], scores, MASKED)
    soft_weights = jnp.exp(scores - total_parts[:, starting : starting + span_rows, None])
    grad_soft = jnp.einsum("qhd,khd->hqk", grad_mixed, values, preferred_element_type=jnp.float32)
    centre = jnp.sum(soft_weights * grad_soft, axis=-1, keepdims=True)
    grad_scores = (soft_weights * (grad_soft - centre)).astype(jnp.bfloat16)
    query_parts = (
        jnp.einsum("hqk,khd->qhd", grad_scores, keys, preferred_element_type=jnp.float32) * scale
    )
    grad_keys = (
        jnp.einsum("hqk,qhd->khd", grad_scores, query, preferred_element_type=jnp.float32) * scale
    )
    grad_values = jnp.einsum(
        "hqk,qhd->khd",
        soft_weights.astype(jnp.bfloat16),
        grad_mixed,
        preferred_element_type=jnp.float32,
    )
    grad_query = unrotate(query_parts, cosine, sine_table)
    grad_keys = unrotate(grad_keys, cosine, sine_table)
    grad_proj = jnp.concatenate(
        [
            grad_query.reshape(length, model_width),
            grad_keys.reshape(length, model_width),
            grad_values.reshape(length, model_width),
        ],
        axis=1,
    ).astype(jnp.bfloat16)
    grad_qkv = lax.dot_general(
        first_normalized, grad_proj, TOKENS_CONTRACT, preferred_element_type=jnp.float32
    )
    first_normalized_gradient = lax.dot_general(
        grad_proj, w_qkv, ROWS_CONTRACT, preferred_element_type=jnp.float32
    )
    first_gain_gradient = jnp.sum(first_normalized_gradient * first_standardized, axis=0)
    token_input_gradient = residual_gradient + norm_backward(
        first_normalized_gradient, first_standardized, first_inverse_norm, paired_gains[0]
    )
    shard_qkv, shard_out, shard_in, shard_down, shard_gains = (
        lax.psum_scatter(grad_qkv, ("dp", "fsdp"), scatter_dimension=0, tiled=True),
        lax.psum_scatter(grad_out, ("dp", "fsdp"), scatter_dimension=0, tiled=True),
        lax.psum_scatter(grad_in, ("dp", "fsdp"), scatter_dimension=0, tiled=True),
        lax.psum_scatter(grad_down, ("dp", "fsdp"), scatter_dimension=0, tiled=True),
        lax.psum_scatter(
            jnp.stack([first_gain_gradient, second_gain_gradient]),
            ("dp", "fsdp"),
            scatter_dimension=1,
            tiled=True,
        ),
    )
    shards = (shard_qkv, shard_out, shard_in, shard_down, shard_gains)
    local_sum = sum((jnp.sum(piece * piece) for piece in shards))
    global_squares = lax.psum(local_sum, ("dp", "fsdp"))
    grad_norm = jnp.sqrt(global_squares)
    clip_factor = CLIP_NORM / jnp.maximum(grad_norm, CLIP_NORM)
    masters = (attn_in, attn_out, ff_in, ff_out, gains)
    firsts = (attn_in_m, attn_out_m, ff_in_m, ff_out_m, gains_m)
    seconds = (attn_in_v, attn_out_v, ff_in_v, ff_out_v, gains_v)
    decays = (WEIGHT_DECAY, WEIGHT_DECAY, WEIGHT_DECAY, WEIGHT_DECAY, 0.0)
    results = [
        adam_update(w, g, m, v, clip_factor, dec, rate)
        for w, g, m, v, dec, rate in zip(masters, shards, firsts, seconds, decays, LEARN_RATES)
    ]
    return (
        block_out,
        token_input_gradient,
        grad_norm,
        results[0][0],
        results[1][0],
        results[2][0],
        results[3][0],
        results[4][0],
        results[0][1],
        results[1][1],
        results[2][1],
        results[3][1],
        results[4][1],
        results[0][2],
        results[1][2],
        results[2][2],
        results[3][2],
        results[4][2],
    )


def solution(mesh):
    in_specs = (
        P(("dp", "fsdp"), None),
        P(("dp", "fsdp"), None),
        P(("dp", "fsdp"), None),
        P(("dp", "fsdp"), None),
        P(("dp", "fsdp"), None),
        P(("dp", "fsdp"), None),
        P(("dp", "fsdp"), None),
        P(None, ("dp", "fsdp")),
        P(("dp", "fsdp"), None),
        P(("dp", "fsdp"), None),
        P(("dp", "fsdp"), None),
        P(("dp", "fsdp"), None),
        P(None, ("dp", "fsdp")),
        P(("dp", "fsdp"), None),
        P(("dp", "fsdp"), None),
        P(("dp", "fsdp"), None),
        P(("dp", "fsdp"), None),
        P(None, ("dp", "fsdp")),
    )
    out_specs = (
        P(("dp", "fsdp"), None),
        P(("dp", "fsdp"), None),
        P(),
        P(("dp", "fsdp"), None),
        P(("dp", "fsdp"), None),
        P(("dp", "fsdp"), None),
        P(("dp", "fsdp"), None),
        P(None, ("dp", "fsdp")),
        P(("dp", "fsdp"), None),
        P(("dp", "fsdp"), None),
        P(("dp", "fsdp"), None),
        P(("dp", "fsdp"), None),
        P(None, ("dp", "fsdp")),
        P(("dp", "fsdp"), None),
        P(("dp", "fsdp"), None),
        P(("dp", "fsdp"), None),
        P(("dp", "fsdp"), None),
        P(None, ("dp", "fsdp")),
    )
    fast = dict(mesh.shape) == {"dp": 8, "fsdp": 4}
    run = fast_body if fast else body
    return jax.shard_map(run, mesh=mesh, in_specs=in_specs, out_specs=out_specs, check_vma=False)
```

```python
import jax
import jax.numpy as jnp
from jax import lax
from jax.experimental import pallas as pl
from jax.experimental.pallas import tpu as pltpu
from jax.sharding import PartitionSpec as P

BF = jnp.bfloat16
F32 = jnp.float32
MESH_ID = pl.DeviceIdType.MESH

WIDTHS = (2304, 768, 4096, 2048)
PIECES = (
    (0, 0, 384, 384, 128),
    (0, 768, 1152, 384, 256),
    (0, 1536, 1920, 384, 128),
    (1, 0, 384, 384, 256),
    (2, 0, 2048, 512, 256),
    (3, 0, 256, 256, 128),
    (2, 512, 2560, 512, 256),
    (3, 512, 768, 256, 128),
    (2, 1024, 3072, 512, 256),
    (3, 1024, 1280, 256, 128),
    (2, 1536, 3584, 512, 256),
    (3, 1536, 1792, 256, 128),
)
Z_LAST = (7, 11)
OFFSETS = tuple(sum(p[3] for p in PIECES[:k]) for k in range(len(PIECES)))
HALF = sum(p[3] for p in PIECES)
COUNT = len(PIECES)


class Place:
    def __init__(self):
        dp, fs = lax.axis_index("dp"), lax.axis_index("fsdp")
        self.dp, self.fs = dp, fs
        self.x, self.c = fs // 2, fs % 2
        self.z, self.y = dp // 2, dp % 2
        self.yx = self.y * 2 + self.x
        self.me = dp * 4 + fs
        self.sibling = (dp, self.x * 2 + 1 - self.c)
        self.xn = (dp, (1 - self.x) * 2 + self.c)
        self.yn = (self.z * 2 + 1 - self.y, fs)
        self.x_column = self.y * 2 + 1 - self.x
        self.y_column = (1 - self.y) * 2 + self.x
        self.diagonal = (1 - self.y) * 2 + 1 - self.x

    def z_peer(self, step):
        z = lax.rem(self.z + step, 4)
        return z, (z * 2 + self.y, self.fs)

    def group_peer(self, step):
        fs = lax.rem(self.fs + step, 4)
        return fs, (self.dp, fs)

    def plane_peer(self, step):
        dp = lax.rem(self.dp + step, 8)
        return dp, (dp, self.fs)

    def greet(self):
        barrier = pltpu.get_barrier_semaphore()
        for step in range(1, 4):
            pl.semaphore_signal(
                barrier, inc=1, device_id=self.group_peer(step)[1], device_id_type=MESH_ID
            )
        for step in range(1, 8):
            pl.semaphore_signal(
                barrier, inc=1, device_id=self.plane_peer(step)[1], device_id_type=MESH_ID
            )
        pl.semaphore_wait(barrier, 10)

    def columns(self, piece, sibling=False):
        first, second, width = piece[1], piece[2], piece[3]
        core = 1 - self.c if sibling else self.c
        start = jnp.where(core == 0, first, second)
        return pl.ds(pl.multiple_of(start, 128), width)

    def parts(self, piece):
        return (0, piece[4]), (piece[4], piece[3] - piece[4])


def remote(src, dst, send, recv, device):
    return pltpu.make_async_remote_copy(
        src_ref=src,
        dst_ref=dst,
        send_sem=send,
        recv_sem=recv,
        device_id=device,
        device_id_type=MESH_ID,
    )


GATHER_SEMS = 12
REDUCE_SEMS = 9


class Gather:
    def __init__(self, place, shards, whole, sibling_rows, send, recv):
        self.p, self.shards, self.whole = place, shards, whole
        self.rows, self.send, self.recv = sibling_rows, send, recv

    def copy(self, k, which):
        p, piece = self.p, PIECES[k]
        w = self.whole[piece[0]]
        sem = (self.send.at[k * GATHER_SEMS + which], self.recv.at[k * GATHER_SEMS + which])
        cols = p.columns(piece)

        def part(i):
            start, width = p.parts(piece)[i]
            return pl.ds(pl.multiple_of(cols.start + start, 128), width)

        if which == 0:
            shard = self.shards[piece[0]]
            return remote(
                shard.at[:, p.columns(piece, sibling=True)],
                self.rows.at[:, pl.ds(OFFSETS[k], piece[3])],
                *sem,
                p.sibling,
            )
        z_last = k in Z_LAST
        if which in (1, 2, 3):
            block = w.at[p.z, :, :, cols] if z_last else w.at[p.z, p.yx, :, cols]
            return remote(block, block, *sem, p.z_peer(which)[1])
        if which in (4, 5):
            block = w.at[p.z if z_last else slice(None), p.yx, :, cols]
            return remote(block, block, *sem, (p.xn, p.yn)[which - 4])
        if which in (6, 7):
            along_x = p.c == which - 6
            column = jnp.where(along_x, p.y_column, p.x_column)
            block = w.at[p.z if z_last else slice(None), column, :, part(which - 6)]
            device = (
                jnp.where(along_x, p.xn[0], p.yn[0]),
                jnp.where(along_x, p.xn[1], p.yn[1]),
            )
            return remote(block, block, *sem, device)
        if z_last:
            block = w.at[lax.rem(p.z + 12 - which, 4), :, :, cols]
        else:
            column = (p.yx, p.x_column, p.y_column, p.diagonal)[which - 8]
            block = w.at[:, column, :, cols]
        return remote(block, block, *sem, p.sibling)

    def exchange(self, k):
        self.copy(k, 0).start()

    def begin(self, k):
        p, piece = self.p, PIECES[k]
        self.copy(k, 0).wait_recv()
        mine = self.shards[piece[0]][:, p.columns(piece)]
        other = self.rows[:, OFFSETS[k] : OFFSETS[k] + piece[3]]
        first = p.c == 0
        both = jnp.concatenate(
            [jnp.where(first, mine, other), jnp.where(first, other, mine)], axis=0
        )
        self.whole[piece[0]][p.z, p.yx, :, p.columns(piece)] = both.astype(BF)
        self.start(k, (4, 5) if k in Z_LAST else (1, 2, 3))

    def start(self, k, which):
        for i in which:
            self.copy(k, i).start()

    def after(self, k, landed, started):
        for i in landed:
            self.copy(k, i).wait_recv()
        self.start(k, started)

    def step1(self, k):
        if k in Z_LAST:
            self.after(k, (4, 5), (6, 7))
        else:
            self.after(k, (1, 2, 3), (4, 5, 8))

    def step2(self, k):
        if k in Z_LAST:
            self.after(k, (6, 7), (1, 2, 3, 8))
        else:
            self.after(k, (4, 5), (6, 7, 9, 10))

    def step3(self, k):
        if k in Z_LAST:
            self.after(k, (1, 2, 3), (9, 10, 11))
        else:
            self.after(k, (6, 7), (11,))

    def finish(self, k):
        for i in (8, 9, 10, 11):
            self.copy(k, i).wait_recv()

    def drain(self, k):
        for i in range(GATHER_SEMS):
            self.copy(k, i).wait_send()


class Reduce:
    def __init__(self, place, mine, other, landed, diag, cols, zed, done, got, send, recv):
        self.p = place
        self.mine, self.other, self.landed = mine, other, landed
        self.diag, self.cols, self.zed, self.done, self.got = diag, cols, zed, done, got
        self.send, self.recv = send, recv

    def copy(self, k, which):
        p, piece = self.p, PIECES[k]
        off, width = OFFSETS[k], piece[3]
        sem = (self.send.at[k * REDUCE_SEMS + which], self.recv.at[k * REDUCE_SEMS + which])
        span = pl.ds(off, width)
        if which == 0:
            return remote(
                self.other(k), self.landed.at[:, :, :, span], *sem, p.sibling
            )
        if which in (1, 2):
            start, wide = p.parts(piece)[which - 1]
            part = pl.ds(off + start, wide)
            along_x = p.c == which - 1
            device = (
                jnp.where(along_x, p.xn[0], p.yn[0]),
                jnp.where(along_x, p.xn[1], p.yn[1]),
            )
            if k in Z_LAST:
                return remote(
                    self.mine.at[p.z, p.diagonal, :, part], self.zed.at[0, :, part], *sem, device
                )
            return remote(
                self.mine.at[:, p.diagonal, :, part], self.diag.at[:, :, part], *sem, device
            )
        if which in (3, 4):
            column, device = ((p.x_column, p.xn), (p.y_column, p.yn))[which - 3]
            if k in Z_LAST:
                return remote(
                    self.mine.at[p.z, column, :, span],
                    self.zed.at[which - 2, :, span],
                    *sem,
                    device,
                )
            return remote(
                self.mine.at[:, column, :, span], self.cols.at[which - 3, :, :, span], *sem, device
            )
        if which in (5, 6, 7):
            z, device = p.z_peer(which - 4)
            if k in Z_LAST:
                return remote(
                    self.mine.at[z, :, :, span], self.slab(which - 5).at[:, :, span], *sem, device
                )
            return remote(
                self.mine.at[z, p.yx, :, span], self.zed.at[which - 5, :, span], *sem, device
            )
        return remote(
            self.done.at[1 - p.c, :, span], self.got.at[:, span], *sem, p.sibling
        )

    def slab(self, i):
        return (self.cols.at[0], self.cols.at[1], self.diag)[i]

    def begin(self, k):
        self.copy(k, 0).start()

    def step1(self, k):
        off, width = OFFSETS[k], PIECES[k][3]
        self.copy(k, 0).wait_recv()

        @pl.loop(0, 4)
        def _(z):
            for yx in range(4):
                total = self.mine[z, yx, :, off : off + width].astype(F32) + self.landed[
                    z, yx, :, off : off + width
                ].astype(F32)
                self.mine[z, yx, :, off : off + width] = total.astype(BF)

        for i in (5, 6, 7) if k in Z_LAST else (1, 2):
            self.copy(k, i).start()

    def z_last_step2(self, k):
        p = self.p
        off, width = OFFSETS[k], PIECES[k][3]
        for i in (5, 6, 7):
            self.copy(k, i).wait_recv()
        span = slice(off, off + width)

        @pl.loop(0, 4)
        def _(yx):
            total = self.mine[p.z, yx, :, span].astype(F32)
            for i in range(3):
                total = total + self.slab(i)[yx, :, span].astype(F32)
            self.mine[p.z, yx, :, span] = total.astype(BF)

        for i in (1, 2):
            self.copy(k, i).start()

    def z_last_step3(self, k):
        p, piece = self.p, PIECES[k]
        off = OFFSETS[k]
        for i in (1, 2):
            self.copy(k, i).wait_recv()
        for i in (0, 1):
            start, wide = p.parts(piece)[i]
            column = jnp.where(p.c == i, p.y_column, p.x_column)
            part = slice(off + start, off + start + wide)
            total = self.mine[p.z, column, :, part].astype(F32) + self.zed[0, :, part].astype(F32)
            self.mine[p.z, column, :, part] = total.astype(BF)
        for i in (3, 4):
            self.copy(k, i).start()

    def step2(self, k):
        if k in Z_LAST:
            self.z_last_step2(k)
            return
        p, piece = self.p, PIECES[k]
        off = OFFSETS[k]
        for i in (1, 2):
            self.copy(k, i).wait_recv()
        for i in (0, 1):
            start, wide = p.parts(piece)[i]
            column = jnp.where(p.c == i, p.y_column, p.x_column)
            part = slice(off + start, off + start + wide)

            @pl.loop(0, 4)
            def _(z):
                total = self.mine[z, column, :, part].astype(F32) + self.diag[z, :, part].astype(
                    F32
                )
                self.mine[z, column, :, part] = total.astype(BF)

        for i in (3, 4):
            self.copy(k, i).start()

    def step3(self, k):
        if k in Z_LAST:
            self.z_last_step3(k)
            return
        p = self.p
        off, width = OFFSETS[k], PIECES[k][3]
        span = slice(off, off + width)
        for i in (3, 4):
            self.copy(k, i).wait_recv()

        @pl.loop(0, 4)
        def _(z):
            total = (
                self.mine[z, p.yx, :, span].astype(F32)
                + self.cols[0, z, :, span].astype(F32)
                + self.cols[1, z, :, span].astype(F32)
            )
            self.mine[z, p.yx, :, span] = total.astype(BF)

        for i in (5, 6, 7):
            self.copy(k, i).start()

    def step4(self, k):
        p = self.p
        off, width = OFFSETS[k], PIECES[k][3]
        span = slice(off, off + width)
        for i in (3, 4) if k in Z_LAST else (5, 6, 7):
            self.copy(k, i).wait_recv()
        total = self.mine[p.z, p.yx, :, span].astype(F32)
        for i in (1, 2) if k in Z_LAST else (0, 1, 2):
            total = total + self.zed[i, :, span].astype(F32)
        self.done[0, :, span] = total[:24]
        self.done[1, :, span] = total[24:]
        self.copy(k, 8).start()

    def finish(self, k):
        self.copy(k, 8).wait_recv()

    def drain(self, k):
        for i in range(REDUCE_SEMS):
            self.copy(k, i).wait_send()


SMALL_SEMS = 10


class Small:
    def __init__(self, place, group, plane, send, recv, base):
        self.p, self.group, self.plane = place, group, plane
        self.send, self.recv, self.base = send, recv, base

    def first(self, step):
        i = self.base + step - 1
        slot = self.group.at[self.p.fs]
        return remote(slot, slot, self.send.at[i], self.recv.at[i], self.p.group_peer(step)[1])

    def second(self, step):
        i = self.base + 2 + step
        slot = self.plane.at[self.p.dp]
        return remote(slot, slot, self.send.at[i], self.recv.at[i], self.p.plane_peer(step)[1])

    def start_first(self):
        for step in range(1, 4):
            self.first(step).start()

    def wait_first(self):
        for step in range(1, 4):
            self.first(step).wait_recv()

    def start_second(self):
        for step in range(1, 8):
            self.second(step).start()

    def wait_second(self):
        for step in range(1, 8):
            self.second(step).wait_recv()

    def drain(self):
        for step in range(1, 4):
            self.first(step).wait_send()
        for step in range(1, 8):
            self.second(step).wait_send()


def spread_gains(plane, count, wide, total):
    slots = plane.reshape(count, 8, 128)
    owner = lax.broadcasted_iota(jnp.int32, (count, total), 1) // wide
    pick = (owner == lax.broadcasted_iota(jnp.int32, (count, total), 0)).astype(F32)
    lane = lax.broadcasted_iota(jnp.int32, (128, total), 1) % wide
    keep = lane == lax.broadcasted_iota(jnp.int32, (128, total), 0)
    rows = []
    for g in range(2):
        spread = lax.dot_general(
            slots[:, g, :], pick, (((0,), (0,)), ((), ())), preferred_element_type=F32
        )
        rows.append(jnp.sum(jnp.where(keep, spread, 0.0), axis=0, keepdims=True))
    return rows


TOKENS_PER = 512
MODEL = 768
PAIRS = MODEL // 128
BLOCK = 512
ROW_STEP = 64
PLAN = (
    ((0, 0, 0), (0, 0, 1), (0, 0, 2),),
    ((0, 0, 3), (0, 0, 4), (0, 0, 5), (0, 0, 6), (0, 0, 7), (0, 0, 8), (0, 0, 9), (0, 0, 10), (0, 0, 11),),
    (),
    (),
    (),
    ((0, 1, 0), (0, 1, 1), (0, 2, 0), (0, 1, 2), (0, 2, 1), (0, 1, 3), (0, 3, 0), (0, 4, 0),),
    ((0, 2, 2), (0, 1, 4), (0, 3, 1), (0, 4, 1),),
    ((0, 1, 5), (0, 2, 3), (0, 3, 2), (0, 1, 6), (0, 1, 7), (0, 4, 2),),
    (),
    (),
    ((0, 2, 4),),
    ((0, 1, 8),),
    ((0, 2, 5), (0, 1, 9),),
    ((0, 3, 3),),
    ((0, 4, 3),),
    (),
    ((0, 2, 6), (0, 1, 10), (0, 2, 7), (0, 1, 11),),
    ((0, 3, 4), (0, 4, 4), (0, 2, 8), (0, 3, 5), (0, 4, 5),),
    (),
    ((0, 2, 9),),
    ((0, 3, 6),),
    ((0, 3, 7),),
    ((1, 0, 4), (0, 4, 6), (1, 0, 5), (0, 4, 7), (0, 2, 10),),
    (),
    ((0, 2, 11),),
    ((0, 3, 8),),
    ((0, 3, 9),),
    ((0, 4, 8), (1, 1, 4),),
    ((1, 1, 5), (1, 0, 6), (0, 4, 9), (1, 0, 7), (0, 3, 10),),
    (),
    (),
    ((0, 4, 10),),
    ((1, 2, 4), (0, 3, 11),),
    (),
    ((1, 2, 5), (1, 0, 8), (0, 4, 11), (1, 0, 9), (1, 1, 6),),
    (),
    (),
    (),
    ((1, 1, 7), (1, 1, 8), (1, 1, 9),),
    (),
    ((1, 0, 10), (1, 0, 11), (1, 3, 4),),
    ((1, 2, 6), (1, 2, 7), (1, 3, 5), (1, 4, 4),),
    ((1, 4, 5),),
    ((1, 2, 8),),
    ((1, 0, 3), (1, 2, 9),),
    ((1, 1, 10),),
    ((1, 1, 11), (1, 1, 3),),
    (),
    ((1, 3, 6), (1, 3, 7),),
    ((1, 2, 10), (1, 2, 11), (1, 4, 6), (1, 4, 7),),
    ((1, 3, 8), (1, 2, 3),),
    (),
    ((1, 3, 9), (1, 0, 0), (1, 4, 8), (1, 0, 1),),
    ((1, 0, 2), (1, 4, 9),),
    ((1, 3, 10), (1, 3, 11),),
    ((1, 1, 0),),
    ((1, 4, 10), (1, 4, 11), (1, 1, 1), (1, 3, 3),),
    ((1, 1, 2), (1, 4, 3), (1, 2, 0), (1, 2, 1), (1, 3, 0), (2, 0, 0), (1, 2, 2), (1, 4, 0), (1, 3, 1), (1, 4, 1), (1, 3, 2), (1, 4, 2),),
)


def nn(a, b):
    return lax.dot_general(a, b, (((1,), (0,)), ((), ())), preferred_element_type=F32)


def nt(a, b):
    return lax.dot_general(a, b, (((1,), (1,)), ((), ())), preferred_element_type=F32)


def tn(a, b):
    return lax.dot_general(a, b, (((0,), (0,)), ((), ())), preferred_element_type=F32)


def aligned(start, size):
    return pl.ds(pl.multiple_of(start, 128), size)


def layer_kernel(
    tok_in, cot_in, starts, gains, w0_in, w1_in, w2_in, w3_in,
    block_out, token_grad, shard0, shard1, shard2, shard3, gain_shard, square_out,
    big0, big1, big2, big3, rows, group, plane,
    mine, landed, diag, cols_in, zed, done, got, group_g, plane_g, group_s, plane_s,
    theirs_ff, theirs_at, gain_rows, dgain, cosine, signed_sine, bias, logs,
    h1, h1_t, query, keys, values, state, out_acc, dnorm, h2, h2_t, dy_t, dmixed,
    gate, up, dact, act, dgu,
    tok, cot, w0, w1, w2, w3,
    g_send, g_recv, r_send, r_recv, s_send, s_recv, local, load,
):
    loads = [
        pltpu.make_async_copy(source, dest, load.at[i])
        for i, (source, dest) in enumerate(
            ((w0_in, w0), (w1_in, w1), (w2_in, w2), (w3_in, w3), (tok_in, tok), (cot_in, cot))
        )
    ]
    for copy in loads:
        copy.start()
    place = Place()
    place.greet()
    whole = (big0, big1, big2, big3)
    mixed = h1
    gather = Gather(place, (w0, w1, w2, w3), whole, rows, g_send, g_recv)

    wide = gains.shape[1]
    small = Small(place, group, plane, s_send, s_recv, 0)
    small_g = Small(place, group_g, plane_g, s_send, s_recv, SMALL_SEMS)
    small_s = Small(place, group_s, plane_s, s_send, s_recv, 2 * SMALL_SEMS)
    group[place.fs] = jnp.zeros((8, 128), F32)
    group[place.fs, 0:2, 0:wide] = gains[...].astype(BF).astype(F32)
    small.start_first()
    for copy in loads[0:4]:
        copy.wait()
    for k in range(COUNT):
        gather.exchange(k)
    small.wait_first()
    for i in range(4):
        plane[place.dp, i] = group[i]
    small.start_second()

    reduce = Reduce(
        place, mine, None, landed, diag, cols_in, zed, done, got, r_send, r_recv
    )
    square = [jnp.zeros((1, 1), F32)]
    shards = (shard0, shard1, shard2, shard3)

    def write_shard(k):
        piece = PIECES[k]
        span = pl.ds(OFFSETS[k], piece[3])
        return [
            pltpu.make_async_copy(
                source, shards[piece[0]].at[:, place.columns(piece, sibling)], local.at[i]
            )
            for source, sibling, i in (
                (done.at[place.c, :, span], False, 2 + 2 * k),
                (got.at[:, span], True, 3 + 2 * k),
            )
        ]

    def finish(k):
        reduce.finish(k)
        piece = PIECES[k]
        span = slice(OFFSETS[k], OFFSETS[k] + piece[3])
        a, b = done[place.c, :, span], got[:, span]
        for copy in write_shard(k):
            copy.start()
        square[0] = square[0] + jnp.sum(a * a + b * b, axis=(0, 1), keepdims=True)

    stages = (
        (gather.begin, gather.step1, gather.step2, gather.step3, gather.finish),
        (reduce.step1, reduce.step2, reduce.step3, reduce.step4, finish),
    )
    points = iter(PLAN)

    def pump():
        for kind, stage, k in next(points):
            if kind == 2:
                share_gains()
            else:
                stages[kind][stage](k)

    def share_gains():
        small_g.wait_first()
        plane_g[place.dp] = group_g[0] + group_g[1] + group_g[2] + group_g[3]
        small_g.start_second()

    pump()

    tokens_n = TOKENS_PER
    images = starts.shape[1]
    place_in_half = lax.broadcasted_iota(jnp.int32, (1, 128), 1) % (HD // 2)
    freq = jnp.ones((1, 128), F32)
    for i in range(1, HD // 2):
        freq = jnp.where(place_in_half == i, ROPE_BASE ** (-2.0 * i / HD), freq)

    def began(t):
        latest = jnp.full(t.shape, -(10**6), jnp.int32)
        for j in range(images):
            s = starts[0, j]
            latest = jnp.maximum(latest, jnp.where(s <= t, s, -(10**6)))
        return latest

    @pl.loop(0, tokens_n // ROW_STEP)
    def _(i):
        r = pl.ds(pl.multiple_of(i * ROW_STEP, ROW_STEP), ROW_STEP)
        t = lax.broadcasted_iota(jnp.int32, (ROW_STEP, 128), 0) + i * ROW_STEP
        angle = (t - began(t)).astype(F32) * freq
        cosine[r, :] = jnp.cos(angle)
        lane = lax.broadcasted_iota(jnp.int32, (ROW_STEP, 128), 1)
        signed_sine[r, :] = jnp.where(lane % 64 < 32, -1.0, 1.0) * jnp.sin(angle)
        u = lax.broadcasted_iota(jnp.int32, (ROW_STEP, tokens_n), 0) + i * ROW_STEP
        t = lax.broadcasted_iota(jnp.int32, (1, tokens_n), 1)
        bias[r, :] = jnp.where((u <= t) & (u >= began(t)), 0.0, -1e30)

    pump()
    small.wait_second()
    first, second = spread_gains(plane, 32, wide, MODEL)
    gain_rows[0:1, :] = first
    gain_rows[1:2, :] = second
    dgain[...] = jnp.zeros_like(dgain)

    def inverse(x):
        return lax.rsqrt(jnp.mean(x * x, axis=-1, keepdims=True) + 1e-05)

    def row_loop(body):
        @pl.loop(0, tokens_n // ROW_STEP)
        def _(i):
            body(pl.ds(pl.multiple_of(i * ROW_STEP, ROW_STEP), ROW_STEP))

    def normed(source, gain, dest):
        def body(r):
            x = source[r, :].astype(F32)
            dest[r, :] = (x * inverse(x) * gain_rows[gain : gain + 1, :]).astype(BF)

        row_loop(body)

    def turn(source, dest):
        @pl.loop(0, PAIRS)
        def _(n):
            c = aligned(n * 128, 128)
            dest[c, :] = source[:, c].T

    loads[4].wait()
    normed(tok, 0, h1)
    pump()
    turn(h1, h1_t)
    pump()
    loads[5].wait()
    turn(cot, dy_t)
    pump()

    def weight(k, c):
        block = whole[k][:, :, :, c]
        return block.reshape(MODEL, block.shape[-1])

    lane = lax.broadcasted_iota(jnp.int32, (1, 128), 1)
    front = lane % 64 < 32
    of_head = (lane < 64, lane >= 64)

    def swap(v):
        return jnp.where(front, pltpu.roll(v, 96, 1), pltpu.roll(v, 32, 1))

    def project(part, dest):
        @pl.loop(0, MODEL // 256)
        def _(n):
            p = nn(h1[...], weight(0, aligned(part * MODEL + n * 256, 256)))
            for half in range(2):
                v = p[:, half * 128 : half * 128 + 128]
                if part < 2:
                    v = v * cosine[...] + swap(v) * signed_sine[...]
                v = v.astype(BF)
                if part == 0:
                    v = v * jnp.asarray(0.125, BF)
                dest[:, aligned(n * 256 + half * 128, 128)] = v

    def only(v, head):
        return jnp.where(of_head[head], v, jnp.zeros((), v.dtype))

    def attend(n):
        c = aligned(n * 128, 128)
        k, v, q = keys[:, c], values[:, c], query[:, c]
        for i in range(2):
            t, u = slice(256 * i, 256 * i + 256), slice(0, 256 * i + 256)
            o = []
            for head in range(2):
                s = nt(k[u], only(q[t], head)) + bias[u, t]
                top = jnp.max(s, axis=0, keepdims=True)
                p = jnp.exp(s - top)
                total = jnp.sum(p, axis=0, keepdims=True)
                p = (p * (1.0 / total)).astype(BF)
                logs[n, head : head + 1, t] = top + jnp.log(total)
                o.append(tn(p, v[u]))
            mixed[t, c] = jnp.where(of_head[0], o[0], o[1]).astype(BF)

    def attend_back(n):
        c = aligned(n * 128, 128)
        k, v, q, do = keys[:, c], values[:, c], query[:, c], dmixed[:, c]
        dq, dk, dv = [None, None], [], []
        low_k = low_v = high_k = high_v = None

        def plus(a, b):
            return b if a is None else a + b

        for head in range(2):
            km = only(k, head)
            for i in range(2):
                t, u = slice(256 * i, 256 * i + 256), slice(0, 256 * i + 256)
                qm, dom = only(q[t], head), only(do[t], head)
                s = nt(k[u], qm) + bias[u, t]
                p = jnp.exp(s - logs[n, head : head + 1, t])
                dp = nt(v[u], dom)
                centre = jnp.sum(p * dp, axis=0, keepdims=True)
                ds = (p * (dp - centre)).astype(BF)
                pb = p.astype(BF)
                dq[i] = plus(dq[i], tn(ds, km[u]))
                dk, dv = nn(ds, qm), nn(pb, dom)
                low_k, low_v = plus(low_k, dk[:256]), plus(low_v, dv[:256])
                if i == 1:
                    high_k, high_v = plus(high_k, dk[256:]), plus(high_v, dv[256:])

        def back(v, t):
            return v * cosine[t, :] - swap(v) * signed_sine[t, :]

        for i in range(2):
            t = slice(256 * i, 256 * i + 256)
            query[t, c] = back(dq[i] * 0.125, t).astype(BF)
            keys[t, c] = back((low_k, high_k)[i], t).astype(BF)
            values[t, c] = (low_v, high_v)[i].astype(BF)

    pump()
    project(0, query)
    pump()
    project(1, keys)
    pump()
    project(2, values)
    for n in range(PAIRS):
        pump()
        pl.loop(n, n + 1)(attend)
    pump()

    for n in range(3):
        c = slice(n * 256, n * 256 + 256)
        state[:, c] = tok[:, c].astype(F32) + nt(mixed[...], weight(1, slice(None))[c])
    pump()
    normed(state, 1, h2)
    pump()
    turn(h2, h2_t)

    def theirs(k):
        if k < 4:
            return theirs_at.at[:, :, :, pl.ds(OFFSETS[k], PIECES[k][3])]
        j, second = (k - 4) // 2, (k - 4) % 2
        return theirs_ff.at[j % 2, :, :, :, pl.ds(512 * second, 256 if second else 512)]

    reduce.other = theirs
    drained = set()

    def send_gradient(k, left, right, base):
        piece = PIECES[k]
        width = piece[3]
        step = 256 if width % 256 == 0 else 128

        def run(core, store):
            @pl.loop(0, width // step)
            def _(n):
                g = nn(left[...], right[:, aligned(base + core * width + n * step, step)])
                store(n * step, g.astype(BF).reshape(4, 4, 48, step))

        other = theirs(k)

        def to_other(start, g):
            other[:, :, :, aligned(start, step)] = g

        def to_mine(start, g):
            mine[:, :, :, aligned(OFFSETS[k] + start, step)] = g

        run(1 - place.c, to_other)
        reduce.begin(k)
        run(place.c, to_mine)

    out_acc[...] = state[...]
    dnorm[...] = jnp.zeros_like(dnorm)
    for j in range(4):
        kf, kd = 4 + 2 * j, 5 + 2 * j
        pump()
        gcols, ucols = slice(j * BLOCK, j * BLOCK + BLOCK), slice(2048 + j * BLOCK, 2048 + j * BLOCK + BLOCK)
        for n in range(BLOCK // 256):
            c = slice(n * 256, n * 256 + 256)
            gc = slice(gcols.start + c.start, gcols.start + c.stop)
            uc = slice(ucols.start + c.start, ucols.start + c.stop)
            gate[...] = nn(h2[...], weight(2, gc))
            up[...] = nn(h2[...], weight(2, uc))
            dact[...] = nn(cot[...], weight(3, gc))

            def pointwise(r):
                z, w, da = gate[r, :], up[r, :], dact[r, :]
                s = jax.nn.sigmoid(z)
                swish = z * s
                act[r, c] = (swish * w).astype(BF)
                dgu[r, c] = (da * w * s * (1.0 + z * (1.0 - s))).astype(BF)
                dgu[r, BLOCK + c.start : BLOCK + c.stop] = (da * swish).astype(BF)

            row_loop(pointwise)
            pump()

        if j >= 2:
            for k in (kf - 4, kd - 4):
                reduce.copy(k, 0).wait_send()
                drained.add(k)
        send_gradient(kf, h2_t, dgu, 0)
        pump()
        send_gradient(kd, dy_t, act, 0)
        pump()
        for n in range(3):
            c = slice(n * 256, n * 256 + 256)
            out_acc[:, c] += nt(act[...], weight(3, gcols)[c])
            dnorm[:, c] += nt(dgu[:, 0:BLOCK], weight(2, gcols)[c]) + nt(
                dgu[:, BLOCK : 2 * BLOCK], weight(2, ucols)[c]
            )
        pump()
    write_out = pltpu.make_async_copy(out_acc, block_out, local.at[0])
    write_out.start()

    def second_norm(r):
        x = state[r, :]
        inv = inverse(x)
        xh = x * inv
        dh = dnorm[r, :]
        dgain[1:2, :] += jnp.sum(dh * xh, axis=0, keepdims=True)
        e = dh * gain_rows[1:2, :]
        d = cot[r, :].astype(F32) + inv * (e - xh * jnp.mean(e * xh, axis=-1, keepdims=True))
        state[r, :] = d
        h2[r, :] = d.astype(BF)

    row_loop(second_norm)
    turn(h2, h2_t)
    pump()
    send_gradient(3, h2_t, mixed, 0)
    pump()
    for n in range(3):
        c = slice(n * 256, n * 256 + 256)
        dmixed[:, c] = nn(h2[...], weight(1, c)).astype(BF)
    pump()
    for n in range(PAIRS):
        pl.loop(n, n + 1)(attend_back)
        pump()
    send_gradient(0, h1_t, query, 0)
    pump()
    send_gradient(1, h1_t, keys, 0)
    pump()
    send_gradient(2, h1_t, values, 0)
    pump()
    for n in range(3):
        c = slice(n * 256, n * 256 + 256)
        dnorm[:, c] = (
            nt(query[...], weight(0, slice(0, MODEL))[c])
            + nt(keys[...], weight(0, slice(MODEL, 2 * MODEL))[c])
            + nt(values[...], weight(0, slice(2 * MODEL, 3 * MODEL))[c])
        )
        pump()

    def first_norm(r):
        x = tok[r, :].astype(F32)
        inv = inverse(x)
        xh = x * inv
        dh = dnorm[r, :]
        dgain[0:1, :] += jnp.sum(dh * xh, axis=0, keepdims=True)
        e = dh * gain_rows[0:1, :]
        state[r, :] += inv * (e - xh * jnp.mean(e * xh, axis=-1, keepdims=True))

    row_loop(first_norm)
    write_grad = pltpu.make_async_copy(state, token_grad, local.at[1])
    write_grad.start()
    group_g[place.fs] = dgain[...]
    small_g.start_first()
    pump()
    pump()
    assert next(points, None) is None
    small_g.wait_second()
    total = plane_g[0]
    for i in range(1, 8):
        total = total + plane_g[i]
    row = lax.broadcasted_iota(jnp.int32, (MODEL, 128), 0)
    lane = lax.broadcasted_iota(jnp.int32, (MODEL, 128), 1)
    wanted = (row == place.me * wide + lane) & (lane < wide)
    own = jnp.dot(
        total,
        wanted.astype(F32),
        preferred_element_type=F32,
        precision=lax.Precision.HIGHEST,
    )[0:2]
    gain_shard[...] = own[:, 0:wide]
    squares = square[0] + jnp.sum(own * own, axis=(0, 1), keepdims=True)
    group_s[place.fs] = jnp.broadcast_to(squares, (8, 128))
    small_s.start_first()
    small_s.wait_first()
    plane_s[place.dp] = group_s[0] + group_s[1] + group_s[2] + group_s[3]
    small_s.start_second()
    for k in range(COUNT):
        gather.drain(k)
        for i in range(1 if k in drained else 0, REDUCE_SEMS):
            reduce.copy(k, i).wait_send()
    small.drain()
    small_g.drain()
    write_out.wait()
    write_grad.wait()
    for k in range(COUNT):
        for copy in write_shard(k):
            copy.wait()
    small_s.wait_second()
    squares = plane_s[0]
    for i in range(1, 8):
        squares = squares + plane_s[i]
    square_out[...] = squares
    small_s.drain()


def update_kernel(*refs):
    squares, out_block, out_grad = refs[0:3]
    grads, weights, firsts, seconds = (refs[3 + 5 * i : 8 + 5 * i] for i in range(4))
    new_block, new_grad, norm = refs[23:26]
    new_w, new_m, new_v = (refs[26 + 5 * i : 31 + 5 * i] for i in range(3))
    local = refs[41]
    copies = [
        pltpu.make_async_copy(out_block, new_block, local.at[0]),
        pltpu.make_async_copy(out_grad, new_grad, local.at[1]),
    ]
    for copy in copies:
        copy.start()
    root = jnp.sqrt(squares[0:1, 0:1])
    norm[...] = root
    clip = CLIP_NORM / jnp.maximum(root, CLIP_NORM)
    decays = (WEIGHT_DECAY, WEIGHT_DECAY, WEIGHT_DECAY, WEIGHT_DECAY, 0.0)
    for i in range(5):
        step = 256 if weights[i].shape[1] % 256 == 0 else weights[i].shape[1]
        for n in range(weights[i].shape[1] // step):
            c = slice(n * step, n * step + step)
            results = adam_update(
                weights[i][:, c], grads[i][:, c], firsts[i][:, c], seconds[i][:, c],
                clip, decays[i], LEARN_RATES[i],
            )
            for dest, value in zip((new_w, new_m, new_v), results):
                dest[i][:, c] = value
    for copy in copies:
        copy.wait()


def any_spec():
    return pl.BlockSpec(memory_space=pl.ANY)


def vmem_spec():
    return pl.BlockSpec(memory_space=pltpu.VMEM)


def fast_body(tokens, cotangent, starts, *state):
    weights, firsts, seconds = state[0:5], state[5:10], state[10:15]
    wide = weights[4].shape[1]
    dma = pltpu.SemaphoreType.DMA
    shape = jax.ShapeDtypeStruct
    tall = (TOKENS_PER, MODEL)
    scratch = [pltpu.VMEM((4, 4, 48, w), BF) for w in WIDTHS] + [
        pltpu.VMEM((24, HALF), F32),
        pltpu.VMEM((4, 8, 128), F32),
        pltpu.VMEM((8, 4, 8, 128), F32),
        pltpu.VMEM((4, 4, 48, HALF), BF),
        pltpu.VMEM((4, 4, 48, HALF), BF),
        pltpu.VMEM((4, 48, HALF), BF),
        pltpu.VMEM((2, 4, 48, HALF), BF),
        pltpu.VMEM((3, 48, HALF), BF),
        pltpu.VMEM((2, 24, HALF), F32),
        pltpu.VMEM((24, HALF), F32),
        pltpu.VMEM((4, 8, MODEL), F32),
        pltpu.VMEM((8, 8, MODEL), F32),
        pltpu.VMEM((4, 8, 128), F32),
        pltpu.VMEM((8, 8, 128), F32),
        pltpu.VMEM((2, 4, 4, 48, 768), BF),
        pltpu.VMEM((4, 4, 48, 1536), BF),
        pltpu.VMEM((8, MODEL), F32),
        pltpu.VMEM((8, MODEL), F32),
        pltpu.VMEM((TOKENS_PER, 128), F32),
        pltpu.VMEM((TOKENS_PER, 128), F32),
        pltpu.VMEM((TOKENS_PER, TOKENS_PER), F32),
        pltpu.VMEM((PAIRS, 8, TOKENS_PER), F32),
        pltpu.VMEM(tall, BF),
        pltpu.VMEM((MODEL, TOKENS_PER), BF),
        pltpu.VMEM(tall, BF),
        pltpu.VMEM(tall, BF),
        pltpu.VMEM(tall, BF),
        pltpu.VMEM(tall, F32),
        pltpu.VMEM(tall, F32),
        pltpu.VMEM(tall, F32),
        pltpu.VMEM(tall, BF),
        pltpu.VMEM((MODEL, TOKENS_PER), BF),
        pltpu.VMEM((MODEL, TOKENS_PER), BF),
        pltpu.VMEM(tall, BF),
        pltpu.VMEM((TOKENS_PER, 256), F32),
        pltpu.VMEM((TOKENS_PER, 256), F32),
        pltpu.VMEM((TOKENS_PER, 256), F32),
        pltpu.VMEM((TOKENS_PER, BLOCK), BF),
        pltpu.VMEM((TOKENS_PER, 2 * BLOCK), BF),
        pltpu.VMEM(tall, BF),
        pltpu.VMEM(tall, BF),
        *[pltpu.VMEM((24, w), F32) for w in WIDTHS],
        dma((COUNT * GATHER_SEMS,)),
        dma((COUNT * GATHER_SEMS,)),
        dma((COUNT * REDUCE_SEMS,)),
        dma((COUNT * REDUCE_SEMS,)),
        dma((3 * SMALL_SEMS,)),
        dma((3 * SMALL_SEMS,)),
        dma((2 + 2 * COUNT,)),
        dma((6,)),
    ]
    block_out, token_grad, *shards, squares = pl.pallas_call(
        layer_kernel,
        out_shape=[shape(tall, F32)] * 2
        + [shape((24, w), F32) for w in WIDTHS]
        + [shape((2, wide), F32), shape((8, 128), F32)],
        in_specs=[any_spec()] * 2
        + [pl.BlockSpec(memory_space=pltpu.SMEM), vmem_spec()]
        + [any_spec()] * 4,
        out_specs=[any_spec()] * 6 + [vmem_spec()] * 2,
        scratch_shapes=scratch,
        compiler_params=pltpu.CompilerParams(
            collective_id=1, has_side_effects=True, vmem_limit_bytes=64 * 2**20 - 2**18
        ),
        name="layer_and_gradients",
    )(tokens, cotangent, starts, weights[4], *weights[0:4])
    outs = pl.pallas_call(
        update_kernel,
        out_shape=[shape(tall, F32)] * 2
        + [shape((1, 1), F32)]
        + [shape(w.shape, F32) for _ in range(3) for w in weights],
        in_specs=[vmem_spec()] * 23,
        out_specs=[any_spec()] * 2 + [vmem_spec()] * 16,
        scratch_shapes=[dma((2,))],
        compiler_params=pltpu.CompilerParams(vmem_limit_bytes=64 * 2**20 - 2**18),
        name="update_weights",
    )(squares, block_out, token_grad, *shards, *weights, *firsts, *seconds)
    return (outs[0], outs[1], outs[2].reshape(()), *outs[3:])


HD = 64
IMG = 257
STEP = 10


NORM_EPS = 1e-05
CLIP_NORM = 1.0
LEARN_RATES = (0.02, 0.1, 0.02, 0.02, 0.5)
FIRST_DECAY = 0.5
SECOND_DECAY = 0.5
ADAM_EPS = 1e-08
WEIGHT_DECAY = 0.05
ROPE_BASE = 10000.0
MASKED = -1e30
ROWS_CONTRACT = (((1,), (1,)), ((), ()))
TOKENS_CONTRACT = (((0,), (0,)), ((), ()))


def positions(begins, length):
    tok_index = jnp.arange(length, dtype=jnp.int32)
    began = begins[None, :] <= tok_index[:, None]
    segment = jnp.sum(began.astype(jnp.int32), axis=1)
    latest = jnp.max(jnp.where(began, begins[None, :], -4 * IMG), axis=1)
    return ((tok_index - latest).astype(jnp.float32), segment)


def rotation(rotary_place):
    half = HD // 2
    freq = ROPE_BASE ** (-jnp.arange(half, dtype=jnp.float32) * (2.0 / HD))
    angle = rotary_place[:, None] * freq[None, :]
    return (jnp.cos(angle), jnp.sin(angle))


def rotate(values, cosine, sine_table):
    half = values.shape[-1] // 2
    front, behind = (values[..., :half], values[..., half:])
    cos_part = cosine[:, None, :]
    sin_part = sine_table[:, None, :]
    return jnp.concatenate(
        [front * cos_part - behind * sin_part, behind * cos_part + front * sin_part], axis=-1
    )


def unrotate(grads, cosine, sine_table):
    half = grads.shape[-1] // 2
    front, behind = (grads[..., :half], grads[..., half:])
    cos_part = cosine[:, None, :]
    sin_part = sine_table[:, None, :]
    return jnp.concatenate(
        [front * cos_part + behind * sin_part, behind * cos_part - front * sin_part], axis=-1
    )


def norm_backward(normalized_gradient, standardized_input, inverse_norm, norm_gain):
    gain_scaled = normalized_gradient * norm_gain
    return inverse_norm * (
        gain_scaled
        - standardized_input * jnp.mean(gain_scaled * standardized_input, axis=-1, keepdims=True)
    )


def adam_update(weight, grad, first, second, clip_factor, decay, rate):
    grad = grad * clip_factor
    first = FIRST_DECAY * first + (1.0 - FIRST_DECAY) * grad
    second = SECOND_DECAY * second + (1.0 - SECOND_DECAY) * grad * grad
    fix_one = 1.0 - FIRST_DECAY**STEP
    fix_two = 1.0 - SECOND_DECAY**STEP
    change = first / fix_one / (jnp.sqrt(second / fix_two) + ADAM_EPS) + decay * weight
    return (weight - rate * change, first, second)


def body(
    tokens,
    cotangent,
    starts,
    attn_in,
    attn_out,
    ff_in,
    ff_out,
    gains,
    attn_in_m,
    attn_out_m,
    ff_in_m,
    ff_out_m,
    gains_m,
    attn_in_v,
    attn_out_v,
    ff_in_v,
    ff_out_v,
    gains_v,
):
    length, model_width = tokens.shape
    head_count = model_width // HD
    hidden_width = ff_in.shape[1] // 2
    scale = HD ** (-0.5)
    lowered = (
        attn_in.astype(jnp.bfloat16),
        attn_out.astype(jnp.bfloat16),
        ff_in.astype(jnp.bfloat16),
        ff_out.astype(jnp.bfloat16),
        gains.astype(jnp.bfloat16),
    )
    w_qkv, w_out, w_in, w_down, paired_gains = (
        lax.all_gather(lowered[0], ("dp", "fsdp"), axis=0, tiled=True),
        lax.all_gather(lowered[1], ("dp", "fsdp"), axis=0, tiled=True),
        lax.all_gather(lowered[2], ("dp", "fsdp"), axis=0, tiled=True),
        lax.all_gather(lowered[3], ("dp", "fsdp"), axis=0, tiled=True),
        lax.all_gather(lowered[4], ("dp", "fsdp"), axis=1, tiled=True),
    )
    paired_gains = paired_gains.astype(jnp.float32)
    rotary_place, segment = positions(starts[0], length)
    cosine, sine_table = rotation(rotary_place)
    tok_index = jnp.arange(length, dtype=jnp.int32)
    allowed = (segment[:, None] == segment[None, :]) & (tok_index[None, :] <= tok_index[:, None])
    layer_input = tokens.astype(jnp.float32)
    first_inverse_norm = lax.rsqrt(
        jnp.mean(layer_input * layer_input, axis=-1, keepdims=True) + NORM_EPS
    )
    first_standardized = layer_input * first_inverse_norm
    first_normalized = (first_standardized * paired_gains[0]).astype(jnp.bfloat16)
    projected = jnp.dot(first_normalized, w_qkv, preferred_element_type=jnp.float32)
    query = rotate(
        projected[:, :model_width].reshape(length, head_count, HD), cosine, sine_table
    ).astype(jnp.bfloat16)
    keys = rotate(
        projected[:, model_width : 2 * model_width].reshape(length, head_count, HD),
        cosine,
        sine_table,
    ).astype(jnp.bfloat16)
    values = projected[:, 2 * model_width :].reshape(length, head_count, HD).astype(jnp.bfloat16)
    span_rows = min(512, length)
    starting = 0
    scores = jnp.einsum("qhd,khd->hqk", query, keys, preferred_element_type=jnp.float32) * scale
    scores = jnp.where(allowed[None, starting : starting + span_rows], scores, MASKED)
    highest = jnp.max(scores, axis=-1, keepdims=True)
    shifted = jnp.exp(scores - highest)
    totals = jnp.sum(shifted, axis=-1, keepdims=True)
    soft_weights = (shifted / totals).astype(jnp.bfloat16)
    mixed_parts = jnp.einsum(
        "hqk,khd->qhd", soft_weights, values, preferred_element_type=jnp.float32
    )
    total_parts = highest[..., 0] + jnp.log(totals[..., 0])
    mixed = mixed_parts.reshape(length, model_width).astype(jnp.bfloat16)
    residual_state = layer_input + lax.dot_general(
        mixed, w_out, ROWS_CONTRACT, preferred_element_type=jnp.float32
    )
    second_inverse_norm = lax.rsqrt(
        jnp.mean(residual_state * residual_state, axis=-1, keepdims=True) + NORM_EPS
    )
    second_standardized = residual_state * second_inverse_norm
    second_normalized = (second_standardized * paired_gains[1]).astype(jnp.bfloat16)
    gate_up = jnp.dot(second_normalized, w_in, preferred_element_type=jnp.float32)
    gate_part = gate_up[:, :hidden_width]
    up_part = gate_up[:, hidden_width:]
    sigmoid_gate = jax.nn.sigmoid(gate_part)
    swish = gate_part * sigmoid_gate
    activated = (swish * up_part).astype(jnp.bfloat16)
    block_out = residual_state + lax.dot_general(
        activated, w_down, ROWS_CONTRACT, preferred_element_type=jnp.float32
    )
    incoming_gradient = cotangent.astype(jnp.float32)
    grad_down = lax.dot_general(
        cotangent, activated, TOKENS_CONTRACT, preferred_element_type=jnp.float32
    )
    grad_act = jnp.dot(cotangent, w_down, preferred_element_type=jnp.float32)
    grad_gate = grad_act * up_part * sigmoid_gate * (1.0 + gate_part * (1.0 - sigmoid_gate))
    grad_up = grad_act * swish
    grad_gu = jnp.concatenate([grad_gate, grad_up], axis=1).astype(jnp.bfloat16)
    grad_in = lax.dot_general(
        second_normalized, grad_gu, TOKENS_CONTRACT, preferred_element_type=jnp.float32
    )
    second_normalized_gradient = lax.dot_general(
        grad_gu, w_in, ROWS_CONTRACT, preferred_element_type=jnp.float32
    )
    second_gain_gradient = jnp.sum(second_normalized_gradient * second_standardized, axis=0)
    residual_gradient = incoming_gradient + norm_backward(
        second_normalized_gradient, second_standardized, second_inverse_norm, paired_gains[1]
    )
    grad_branch = residual_gradient.astype(jnp.bfloat16)
    grad_out = lax.dot_general(
        grad_branch, mixed, TOKENS_CONTRACT, preferred_element_type=jnp.float32
    )
    grad_mixed = jnp.dot(grad_branch, w_out, preferred_element_type=jnp.float32).astype(
        jnp.bfloat16
    )
    grad_mixed = grad_mixed.reshape(length, head_count, HD)
    starting = 0
    scores = jnp.einsum("qhd,khd->hqk", query, keys, preferred_element_type=jnp.float32) * scale
    scores = jnp.where(allowed[None, starting : starting + span_rows], scores, MASKED)
    soft_weights = jnp.exp(scores - total_parts[:, starting : starting + span_rows, None])
    grad_soft = jnp.einsum("qhd,khd->hqk", grad_mixed, values, preferred_element_type=jnp.float32)
    centre = jnp.sum(soft_weights * grad_soft, axis=-1, keepdims=True)
    grad_scores = (soft_weights * (grad_soft - centre)).astype(jnp.bfloat16)
    query_parts = (
        jnp.einsum("hqk,khd->qhd", grad_scores, keys, preferred_element_type=jnp.float32) * scale
    )
    grad_keys = (
        jnp.einsum("hqk,qhd->khd", grad_scores, query, preferred_element_type=jnp.float32) * scale
    )
    grad_values = jnp.einsum(
        "hqk,qhd->khd",
        soft_weights.astype(jnp.bfloat16),
        grad_mixed,
        preferred_element_type=jnp.float32,
    )
    grad_query = unrotate(query_parts, cosine, sine_table)
    grad_keys = unrotate(grad_keys, cosine, sine_table)
    grad_proj = jnp.concatenate(
        [
            grad_query.reshape(length, model_width),
            grad_keys.reshape(length, model_width),
            grad_values.reshape(length, model_width),
        ],
        axis=1,
    ).astype(jnp.bfloat16)
    grad_qkv = lax.dot_general(
        first_normalized, grad_proj, TOKENS_CONTRACT, preferred_element_type=jnp.float32
    )
    first_normalized_gradient = lax.dot_general(
        grad_proj, w_qkv, ROWS_CONTRACT, preferred_element_type=jnp.float32
    )
    first_gain_gradient = jnp.sum(first_normalized_gradient * first_standardized, axis=0)
    token_input_gradient = residual_gradient + norm_backward(
        first_normalized_gradient, first_standardized, first_inverse_norm, paired_gains[0]
    )
    shard_qkv, shard_out, shard_in, shard_down, shard_gains = (
        lax.psum_scatter(grad_qkv, ("dp", "fsdp"), scatter_dimension=0, tiled=True),
        lax.psum_scatter(grad_out, ("dp", "fsdp"), scatter_dimension=0, tiled=True),
        lax.psum_scatter(grad_in, ("dp", "fsdp"), scatter_dimension=0, tiled=True),
        lax.psum_scatter(grad_down, ("dp", "fsdp"), scatter_dimension=0, tiled=True),
        lax.psum_scatter(
            jnp.stack([first_gain_gradient, second_gain_gradient]),
            ("dp", "fsdp"),
            scatter_dimension=1,
            tiled=True,
        ),
    )
    shards = (shard_qkv, shard_out, shard_in, shard_down, shard_gains)
    local_sum = sum((jnp.sum(piece * piece) for piece in shards))
    global_squares = lax.psum(local_sum, ("dp", "fsdp"))
    grad_norm = jnp.sqrt(global_squares)
    clip_factor = CLIP_NORM / jnp.maximum(grad_norm, CLIP_NORM)
    masters = (attn_in, attn_out, ff_in, ff_out, gains)
    firsts = (attn_in_m, attn_out_m, ff_in_m, ff_out_m, gains_m)
    seconds = (attn_in_v, attn_out_v, ff_in_v, ff_out_v, gains_v)
    decays = (WEIGHT_DECAY, WEIGHT_DECAY, WEIGHT_DECAY, WEIGHT_DECAY, 0.0)
    results = [
        adam_update(w, g, m, v, clip_factor, dec, rate)
        for w, g, m, v, dec, rate in zip(masters, shards, firsts, seconds, decays, LEARN_RATES)
    ]
    return (
        block_out,
        token_input_gradient,
        grad_norm,
        results[0][0],
        results[1][0],
        results[2][0],
        results[3][0],
        results[4][0],
        results[0][1],
        results[1][1],
        results[2][1],
        results[3][1],
        results[4][1],
        results[0][2],
        results[1][2],
        results[2][2],
        results[3][2],
        results[4][2],
    )


def solution(mesh):
    in_specs = (
        P(("dp", "fsdp"), None),
        P(("dp", "fsdp"), None),
        P(("dp", "fsdp"), None),
        P(("dp", "fsdp"), None),
        P(("dp", "fsdp"), None),
        P(("dp", "fsdp"), None),
        P(("dp", "fsdp"), None),
        P(None, ("dp", "fsdp")),
        P(("dp", "fsdp"), None),
        P(("dp", "fsdp"), None),
        P(("dp", "fsdp"), None),
        P(("dp", "fsdp"), None),
        P(None, ("dp", "fsdp")),
        P(("dp", "fsdp"), None),
        P(("dp", "fsdp"), None),
        P(("dp", "fsdp"), None),
        P(("dp", "fsdp"), None),
        P(None, ("dp", "fsdp")),
    )
    out_specs = (
        P(("dp", "fsdp"), None),
        P(("dp", "fsdp"), None),
        P(),
        P(("dp", "fsdp"), None),
        P(("dp", "fsdp"), None),
        P(("dp", "fsdp"), None),
        P(("dp", "fsdp"), None),
        P(None, ("dp", "fsdp")),
        P(("dp", "fsdp"), None),
        P(("dp", "fsdp"), None),
        P(("dp", "fsdp"), None),
        P(("dp", "fsdp"), None),
        P(None, ("dp", "fsdp")),
        P(("dp", "fsdp"), None),
        P(("dp", "fsdp"), None),
        P(("dp", "fsdp"), None),
        P(("dp", "fsdp"), None),
        P(None, ("dp", "fsdp")),
    )
    fast = dict(mesh.shape) == {"dp": 8, "fsdp": 4}
    run = fast_body if fast else body
    return jax.shard_map(run, mesh=mesh, in_specs=in_specs, out_specs=out_specs, check_vma=False)
```

```python
import jax
import jax.numpy as jnp
from jax import lax
from jax.experimental import pallas as pl
from jax.experimental.pallas import tpu as pltpu
from jax.sharding import PartitionSpec as P

BF = jnp.bfloat16
F32 = jnp.float32
MESH_ID = pl.DeviceIdType.MESH

WIDTHS = (2304, 768, 4096, 2048)
PIECES = (
    (0, 0, 384, 384, 128),
    (0, 768, 1152, 384, 256),
    (0, 1536, 1920, 384, 128),
    (1, 0, 384, 384, 256),
    (2, 0, 2048, 512, 256),
    (3, 0, 256, 256, 128),
    (2, 512, 2560, 512, 256),
    (3, 512, 768, 256, 128),
    (2, 1024, 3072, 512, 256),
    (3, 1024, 1280, 256, 128),
    (2, 1536, 3584, 512, 256),
    (3, 1536, 1792, 256, 128),
)
Z_LAST = (7, 11)
EARLY = (0, 1, 2)
OFFSETS = tuple(sum(p[3] for p in PIECES[:k]) for k in range(len(PIECES)))
HALF = sum(p[3] for p in PIECES)
COUNT = len(PIECES)


class Place:
    def __init__(self):
        dp, fs = lax.axis_index("dp"), lax.axis_index("fsdp")
        self.dp, self.fs = dp, fs
        self.x, self.c = fs // 2, fs % 2
        self.z, self.y = dp // 2, dp % 2
        self.yx = self.y * 2 + self.x
        self.me = dp * 4 + fs
        self.sibling = (dp, self.x * 2 + 1 - self.c)
        self.xn = (dp, (1 - self.x) * 2 + self.c)
        self.yn = (self.z * 2 + 1 - self.y, fs)
        self.x_column = self.y * 2 + 1 - self.x
        self.y_column = (1 - self.y) * 2 + self.x
        self.diagonal = (1 - self.y) * 2 + 1 - self.x

    def z_peer(self, step):
        z = lax.rem(self.z + step, 4)
        return z, (z * 2 + self.y, self.fs)

    def group_peer(self, step):
        fs = lax.rem(self.fs + step, 4)
        return fs, (self.dp, fs)

    def plane_peer(self, step):
        dp = lax.rem(self.dp + step, 8)
        return dp, (dp, self.fs)

    def greet(self):
        barrier = pltpu.get_barrier_semaphore()
        for step in range(1, 4):
            pl.semaphore_signal(
                barrier, inc=1, device_id=self.group_peer(step)[1], device_id_type=MESH_ID
            )
        for step in range(1, 8):
            pl.semaphore_signal(
                barrier, inc=1, device_id=self.plane_peer(step)[1], device_id_type=MESH_ID
            )
        pl.semaphore_wait(barrier, 10)

    def columns(self, piece, sibling=False):
        first, second, width = piece[1], piece[2], piece[3]
        core = 1 - self.c if sibling else self.c
        start = jnp.where(core == 0, first, second)
        return pl.ds(pl.multiple_of(start, 128), width)

    def parts(self, piece):
        return (0, piece[4]), (piece[4], piece[3] - piece[4])


def remote(src, dst, send, recv, device):
    return pltpu.make_async_remote_copy(
        src_ref=src,
        dst_ref=dst,
        send_sem=send,
        recv_sem=recv,
        device_id=device,
        device_id_type=MESH_ID,
    )


GATHER_SEMS = 12
EARLY_SEMS = 8
GATHER_TOTAL = COUNT * GATHER_SEMS + len(EARLY) * EARLY_SEMS
REDUCE_SEMS = 9


class Gather:
    def __init__(self, place, shards, whole, sibling_rows, send, recv):
        self.p, self.shards, self.whole = place, shards, whole
        self.rows, self.send, self.recv = sibling_rows, send, recv

    def copy(self, k, which):
        p, piece = self.p, PIECES[k]
        w = self.whole[piece[0]]
        place = k * GATHER_SEMS + which
        if which >= GATHER_SEMS:
            place = COUNT * GATHER_SEMS + EARLY.index(k) * EARLY_SEMS + which - GATHER_SEMS
        sem = (self.send.at[place], self.recv.at[place])
        cols = p.columns(piece)

        def part(i):
            start, width = p.parts(piece)[i]
            return pl.ds(pl.multiple_of(cols.start + start, 128), width)

        if which == 0:
            shard = self.shards[piece[0]]
            return remote(
                shard.at[:, p.columns(piece, sibling=True)],
                self.rows.at[:, pl.ds(OFFSETS[k], piece[3])],
                *sem,
                p.sibling,
            )
        z_last = k in Z_LAST
        if which >= GATHER_SEMS:
            axis, step = (which - GATHER_SEMS) // 4, (which - GATHER_SEMS) % 4
            block = w.at[lax.rem(p.z + step, 4), p.yx, :, cols]
            return remote(block, block, *sem, (p.xn, p.yn)[axis])
        if which in (1, 2, 3):
            block = w.at[p.z, :, :, cols] if z_last else w.at[p.z, p.yx, :, cols]
            return remote(block, block, *sem, p.z_peer(which)[1])
        if which in (4, 5):
            block = w.at[p.z if z_last else slice(None), p.yx, :, cols]
            return remote(block, block, *sem, (p.xn, p.yn)[which - 4])
        if which in (6, 7):
            along_x = p.c == which - 6
            column = jnp.where(along_x, p.y_column, p.x_column)
            block = w.at[p.z if z_last else slice(None), column, :, part(which - 6)]
            device = (
                jnp.where(along_x, p.xn[0], p.yn[0]),
                jnp.where(along_x, p.xn[1], p.yn[1]),
            )
            return remote(block, block, *sem, device)
        if z_last:
            block = w.at[lax.rem(p.z + 12 - which, 4), :, :, cols]
        else:
            column = (p.yx, p.x_column, p.y_column, p.diagonal)[which - 8]
            block = w.at[:, column, :, cols]
        return remote(block, block, *sem, p.sibling)

    def exchange(self, k):
        self.copy(k, 0).start()

    def begin(self, k):
        p, piece = self.p, PIECES[k]
        self.copy(k, 0).wait_recv()
        mine = self.shards[piece[0]][:, p.columns(piece)]
        other = self.rows[:, OFFSETS[k] : OFFSETS[k] + piece[3]]
        first = p.c == 0
        both = jnp.concatenate(
            [jnp.where(first, mine, other), jnp.where(first, other, mine)], axis=0
        )
        self.whole[piece[0]][p.z, p.yx, :, p.columns(piece)] = both.astype(BF)
        self.start(k, (4, 5) if k in Z_LAST else (1, 2, 3))
        if k in EARLY:
            self.start(k, (12, 16))

    def start(self, k, which):
        for i in which:
            self.copy(k, i).start()

    def after(self, k, landed, started):
        for i in landed:
            self.copy(k, i).wait_recv()
        self.start(k, started)

    def step1(self, k):
        if k in Z_LAST:
            self.after(k, (4, 5), (6, 7))
        elif k in EARLY:
            self.after(k, (1, 2, 3), (13, 17, 14, 18, 15, 19, 8))
        else:
            self.after(k, (1, 2, 3), (4, 5, 8))

    def step2(self, k):
        if k in Z_LAST:
            self.after(k, (6, 7), (1, 2, 3, 8))
        elif k in EARLY:
            self.after(k, range(12, 20), (6, 7, 9, 10))
        else:
            self.after(k, (4, 5), (6, 7, 9, 10))

    def step3(self, k):
        if k in Z_LAST:
            self.after(k, (1, 2, 3), (9, 10, 11))
        else:
            self.after(k, (6, 7), (11,))

    def finish(self, k):
        for i in (8, 9, 10, 11):
            self.copy(k, i).wait_recv()

    def drain(self, k):
        early = k in EARLY
        for i in range(GATHER_SEMS + EARLY_SEMS if early else GATHER_SEMS):
            if not (early and i in (4, 5)):
                self.copy(k, i).wait_send()


class Reduce:
    def __init__(self, place, mine, other, landed, diag, cols, zed, done, got, send, recv):
        self.p = place
        self.mine, self.other, self.landed = mine, other, landed
        self.diag, self.cols, self.zed, self.done, self.got = diag, cols, zed, done, got
        self.send, self.recv = send, recv

    def copy(self, k, which):
        p, piece = self.p, PIECES[k]
        off, width = OFFSETS[k], piece[3]
        sem = (self.send.at[k * REDUCE_SEMS + which], self.recv.at[k * REDUCE_SEMS + which])
        span = pl.ds(off, width)
        if which == 0:
            return remote(
                self.other(k), self.landed.at[:, :, :, span], *sem, p.sibling
            )
        if which in (1, 2):
            start, wide = p.parts(piece)[which - 1]
            part = pl.ds(off + start, wide)
            along_x = p.c == which - 1
            device = (
                jnp.where(along_x, p.xn[0], p.yn[0]),
                jnp.where(along_x, p.xn[1], p.yn[1]),
            )
            if k in Z_LAST:
                return remote(
                    self.mine.at[p.z, p.diagonal, :, part], self.zed.at[0, :, part], *sem, device
                )
            return remote(
                self.mine.at[:, p.diagonal, :, part], self.diag.at[:, :, part], *sem, device
            )
        if which in (3, 4):
            column, device = ((p.x_column, p.xn), (p.y_column, p.yn))[which - 3]
            if k in Z_LAST:
                return remote(
                    self.mine.at[p.z, column, :, span],
                    self.zed.at[which - 2, :, span],
                    *sem,
                    device,
                )
            return remote(
                self.mine.at[:, column, :, span], self.cols.at[which - 3, :, :, span], *sem, device
            )
        if which in (5, 6, 7):
            z, device = p.z_peer(which - 4)
            if k in Z_LAST:
                return remote(
                    self.mine.at[z, :, :, span], self.slab(which - 5).at[:, :, span], *sem, device
                )
            return remote(
                self.mine.at[z, p.yx, :, span], self.zed.at[which - 5, :, span], *sem, device
            )
        return remote(
            self.done.at[1 - p.c, :, span], self.got.at[:, span], *sem, p.sibling
        )

    def slab(self, i):
        return (self.cols.at[0], self.cols.at[1], self.diag)[i]

    def begin(self, k):
        self.copy(k, 0).start()

    def step1(self, k):
        off, width = OFFSETS[k], PIECES[k][3]
        self.copy(k, 0).wait_recv()

        @pl.loop(0, 4)
        def _(z):
            for yx in range(4):
                total = self.mine[z, yx, :, off : off + width].astype(F32) + self.landed[
                    z, yx, :, off : off + width
                ].astype(F32)
                self.mine[z, yx, :, off : off + width] = total.astype(BF)

        for i in (5, 6, 7) if k in Z_LAST else (1, 2):
            self.copy(k, i).start()

    def z_last_step2(self, k):
        p = self.p
        off, width = OFFSETS[k], PIECES[k][3]
        for i in (5, 6, 7):
            self.copy(k, i).wait_recv()
        span = slice(off, off + width)

        @pl.loop(0, 4)
        def _(yx):
            total = self.mine[p.z, yx, :, span].astype(F32)
            for i in range(3):
                total = total + self.slab(i)[yx, :, span].astype(F32)
            self.mine[p.z, yx, :, span] = total.astype(BF)

        for i in (1, 2):
            self.copy(k, i).start()

    def z_last_step3(self, k):
        p, piece = self.p, PIECES[k]
        off = OFFSETS[k]
        for i in (1, 2):
            self.copy(k, i).wait_recv()
        for i in (0, 1):
            start, wide = p.parts(piece)[i]
            column = jnp.where(p.c == i, p.y_column, p.x_column)
            part = slice(off + start, off + start + wide)
            total = self.mine[p.z, column, :, part].astype(F32) + self.zed[0, :, part].astype(F32)
            self.mine[p.z, column, :, part] = total.astype(BF)
        for i in (3, 4):
            self.copy(k, i).start()

    def step2(self, k):
        if k in Z_LAST:
            self.z_last_step2(k)
            return
        p, piece = self.p, PIECES[k]
        off = OFFSETS[k]
        for i in (1, 2):
            self.copy(k, i).wait_recv()
        for i in (0, 1):
            start, wide = p.parts(piece)[i]
            column = jnp.where(p.c == i, p.y_column, p.x_column)
            part = slice(off + start, off + start + wide)

            @pl.loop(0, 4)
            def _(z):
                total = self.mine[z, column, :, part].astype(F32) + self.diag[z, :, part].astype(
                    F32
                )
                self.mine[z, column, :, part] = total.astype(BF)

        for i in (3, 4):
            self.copy(k, i).start()

    def step3(self, k):
        if k in Z_LAST:
            self.z_last_step3(k)
            return
        p = self.p
        off, width = OFFSETS[k], PIECES[k][3]
        span = slice(off, off + width)
        for i in (3, 4):
            self.copy(k, i).wait_recv()

        @pl.loop(0, 4)
        def _(z):
            total = (
                self.mine[z, p.yx, :, span].astype(F32)
                + self.cols[0, z, :, span].astype(F32)
                + self.cols[1, z, :, span].astype(F32)
            )
            self.mine[z, p.yx, :, span] = total.astype(BF)

        for i in (5, 6, 7):
            self.copy(k, i).start()

    def step4(self, k):
        p = self.p
        off, width = OFFSETS[k], PIECES[k][3]
        span = slice(off, off + width)
        for i in (3, 4) if k in Z_LAST else (5, 6, 7):
            self.copy(k, i).wait_recv()
        total = self.mine[p.z, p.yx, :, span].astype(F32)
        for i in (1, 2) if k in Z_LAST else (0, 1, 2):
            total = total + self.zed[i, :, span].astype(F32)
        self.done[0, :, span] = total[:24]
        self.done[1, :, span] = total[24:]
        self.copy(k, 8).start()

    def finish(self, k):
        self.copy(k, 8).wait_recv()

    def drain(self, k):
        for i in range(REDUCE_SEMS):
            self.copy(k, i).wait_send()


SMALL_SEMS = 10


class Small:
    def __init__(self, place, group, plane, send, recv, base):
        self.p, self.group, self.plane = place, group, plane
        self.send, self.recv, self.base = send, recv, base

    def first(self, step):
        i = self.base + step - 1
        slot = self.group.at[self.p.fs]
        return remote(slot, slot, self.send.at[i], self.recv.at[i], self.p.group_peer(step)[1])

    def second(self, step):
        i = self.base + 2 + step
        slot = self.plane.at[self.p.dp]
        return remote(slot, slot, self.send.at[i], self.recv.at[i], self.p.plane_peer(step)[1])

    def start_first(self):
        for step in range(1, 4):
            self.first(step).start()

    def wait_first(self):
        for step in range(1, 4):
            self.first(step).wait_recv()

    def start_second(self):
        for step in range(1, 8):
            self.second(step).start()

    def wait_second(self):
        for step in range(1, 8):
            self.second(step).wait_recv()

    def drain(self):
        for step in range(1, 4):
            self.first(step).wait_send()
        for step in range(1, 8):
            self.second(step).wait_send()


def spread_gains(plane, count, wide, total):
    slots = plane.reshape(count, 8, 128)
    owner = lax.broadcasted_iota(jnp.int32, (count, total), 1) // wide
    pick = (owner == lax.broadcasted_iota(jnp.int32, (count, total), 0)).astype(F32)
    lane = lax.broadcasted_iota(jnp.int32, (128, total), 1) % wide
    keep = lane == lax.broadcasted_iota(jnp.int32, (128, total), 0)
    rows = []
    for g in range(2):
        spread = lax.dot_general(
            slots[:, g, :], pick, (((0,), (0,)), ((), ())), preferred_element_type=F32
        )
        rows.append(jnp.sum(jnp.where(keep, spread, 0.0), axis=0, keepdims=True))
    return rows


TOKENS_PER = 512
MODEL = 768
PAIRS = MODEL // 128
BLOCK = 512
ROW_STEP = 64
PLAN = (
    ((0, 0, 0),),
    ((0, 0, 1), (0, 0, 2),),
    ((0, 0, 3), (0, 0, 4), (0, 0, 5), (0, 0, 6), (0, 0, 7), (0, 0, 8), (0, 0, 9), (0, 0, 10), (0, 0, 11),),
    (),
    (),
    ((0, 1, 0), (0, 1, 1), (0, 2, 0), (0, 1, 2), (0, 2, 1), (0, 3, 0), (0, 1, 3), (0, 4, 0),),
    ((0, 2, 2), (0, 3, 1), (0, 1, 4), (0, 4, 1),),
    ((0, 1, 5), (0, 2, 3), (0, 3, 2), (0, 4, 2),),
    ((0, 1, 6), (0, 1, 7),),
    (),
    ((0, 2, 4),),
    ((0, 2, 5), (0, 1, 8),),
    ((0, 3, 3),),
    ((0, 1, 9), (0, 4, 3),),
    (),
    ((0, 2, 6), (0, 2, 7),),
    ((0, 1, 10), (0, 1, 11),),
    ((0, 3, 4), (0, 3, 5), (0, 4, 4), (0, 4, 5),),
    (),
    (),
    ((0, 2, 8),),
    ((0, 2, 9),),
    ((1, 0, 4), (1, 0, 5), (0, 3, 6), (0, 3, 7),),
    ((0, 4, 6), (0, 4, 7),),
    (),
    ((0, 2, 10), (0, 2, 11),),
    ((0, 3, 8),),
    ((0, 3, 9),),
    ((1, 0, 6), (0, 4, 8), (1, 0, 7), (0, 4, 9), (1, 1, 4),),
    (),
    ((1, 1, 5),),
    ((0, 3, 10),),
    ((1, 1, 6), (0, 4, 10),),
    ((0, 3, 11),),
    ((1, 0, 8), (1, 0, 9), (0, 4, 11),),
    (),
    ((1, 2, 4),),
    ((1, 2, 5),),
    (),
    ((1, 1, 7),),
    ((1, 2, 6), (1, 0, 10), (1, 0, 11), (1, 1, 8),),
    ((1, 1, 9), (1, 2, 7), (1, 3, 4),),
    ((1, 3, 5), (1, 4, 4), (1, 1, 10),),
    ((1, 0, 3), (1, 4, 5),),
    ((1, 3, 6),),
    ((1, 2, 8), (1, 4, 6), (1, 2, 9),),
    ((1, 3, 7),),
    ((1, 4, 7),),
    ((1, 2, 10), (1, 1, 11), (1, 1, 3),),
    (),
    ((1, 2, 11), (1, 3, 8),),
    ((1, 0, 0), (1, 4, 8), (1, 3, 9), (1, 2, 3),),
    ((1, 0, 1), (1, 4, 9),),
    ((1, 0, 2), (1, 1, 0), (1, 3, 10), (1, 3, 11),),
    ((1, 4, 10), (1, 4, 11), (1, 1, 1),),
    ((1, 3, 3),),
    ((1, 1, 2), (1, 4, 3),),
    ((1, 2, 0), (1, 2, 1), (1, 3, 0), (2, 0, 0), (1, 2, 2), (1, 4, 0), (1, 3, 1), (1, 4, 1), (1, 3, 2), (1, 4, 2),),
)


def nn(a, b):
    return lax.dot_general(a, b, (((1,), (0,)), ((), ())), preferred_element_type=F32)


def nt(a, b):
    return lax.dot_general(a, b, (((1,), (1,)), ((), ())), preferred_element_type=F32)


def tn(a, b):
    return lax.dot_general(a, b, (((0,), (0,)), ((), ())), preferred_element_type=F32)


def aligned(start, size):
    return pl.ds(pl.multiple_of(start, 128), size)


def layer_kernel(
    tok_in, cot_in, starts, gains, w0_in, w1_in, w2_in, w3_in,
    block_out, token_grad, shard0, shard1, shard2, shard3, gain_shard, square_out,
    big0, big1, big2, big3, rows, group, plane,
    mine, landed, diag, cols_in, zed, done, got, group_g, plane_g, group_s, plane_s,
    theirs_ff, theirs_at, gain_rows, dgain, cosine, signed_sine, bias, logs,
    h1, h1_t, query, keys, values, state, out_acc, dnorm, h2, h2_t, dy_t, dmixed,
    gate, up, dact, act, dgu,
    tok, cot, w0, w1, w2, w3,
    g_send, g_recv, r_send, r_recv, s_send, s_recv, local, load,
):
    loads = [
        pltpu.make_async_copy(source, dest, load.at[i])
        for i, (source, dest) in enumerate(
            ((w0_in, w0), (w1_in, w1), (w2_in, w2), (w3_in, w3), (tok_in, tok), (cot_in, cot))
        )
    ]
    for copy in loads:
        copy.start()
    place = Place()
    place.greet()
    whole = (big0, big1, big2, big3)
    mixed = h1
    gather = Gather(place, (w0, w1, w2, w3), whole, rows, g_send, g_recv)

    wide = gains.shape[1]
    small = Small(place, group, plane, s_send, s_recv, 0)
    small_g = Small(place, group_g, plane_g, s_send, s_recv, SMALL_SEMS)
    small_s = Small(place, group_s, plane_s, s_send, s_recv, 2 * SMALL_SEMS)
    group[place.fs] = jnp.zeros((8, 128), F32)
    group[place.fs, 0:2, 0:wide] = gains[...].astype(BF).astype(F32)
    small.start_first()
    for copy in loads[0:4]:
        copy.wait()
    for k in range(COUNT):
        gather.exchange(k)
    reduce = Reduce(
        place, mine, None, landed, diag, cols_in, zed, done, got, r_send, r_recv
    )
    square = [jnp.zeros((1, 1), F32)]
    shards = (shard0, shard1, shard2, shard3)

    def write_shard(k):
        piece = PIECES[k]
        span = pl.ds(OFFSETS[k], piece[3])
        return [
            pltpu.make_async_copy(
                source, shards[piece[0]].at[:, place.columns(piece, sibling)], local.at[i]
            )
            for source, sibling, i in (
                (done.at[place.c, :, span], False, 2 + 2 * k),
                (got.at[:, span], True, 3 + 2 * k),
            )
        ]

    def finish(k):
        reduce.finish(k)
        piece = PIECES[k]
        span = slice(OFFSETS[k], OFFSETS[k] + piece[3])
        a, b = done[place.c, :, span], got[:, span]
        for copy in write_shard(k):
            copy.start()
        square[0] = square[0] + jnp.sum(a * a + b * b, axis=(0, 1), keepdims=True)

    stages = (
        (gather.begin, gather.step1, gather.step2, gather.step3, gather.finish),
        (reduce.step1, reduce.step2, reduce.step3, reduce.step4, finish),
    )
    points = iter(PLAN)

    def pump():
        for kind, stage, k in next(points):
            if kind == 2:
                share_gains()
            else:
                stages[kind][stage](k)

    def share_gains():
        small_g.wait_first()
        plane_g[place.dp] = group_g[0] + group_g[1] + group_g[2] + group_g[3]
        small_g.start_second()

    pump()
    small.wait_first()
    for i in range(4):
        plane[place.dp, i] = group[i]
    small.start_second()
    pump()

    tokens_n = TOKENS_PER
    images = starts.shape[1]
    place_in_half = lax.broadcasted_iota(jnp.int32, (1, 128), 1) % (HD // 2)
    freq = jnp.ones((1, 128), F32)
    for i in range(1, HD // 2):
        freq = jnp.where(place_in_half == i, ROPE_BASE ** (-2.0 * i / HD), freq)

    def began(t):
        latest = jnp.full(t.shape, -(10**6), jnp.int32)
        for j in range(images):
            s = starts[0, j]
            latest = jnp.maximum(latest, jnp.where(s <= t, s, -(10**6)))
        return latest

    @pl.loop(0, tokens_n // ROW_STEP)
    def _(i):
        r = pl.ds(pl.multiple_of(i * ROW_STEP, ROW_STEP), ROW_STEP)
        t = lax.broadcasted_iota(jnp.int32, (ROW_STEP, 128), 0) + i * ROW_STEP
        angle = (t - began(t)).astype(F32) * freq
        cosine[r, :] = jnp.cos(angle)
        lane = lax.broadcasted_iota(jnp.int32, (ROW_STEP, 128), 1)
        signed_sine[r, :] = jnp.where(lane % 64 < 32, -1.0, 1.0) * jnp.sin(angle)
        u = lax.broadcasted_iota(jnp.int32, (ROW_STEP, tokens_n), 0) + i * ROW_STEP
        t = lax.broadcasted_iota(jnp.int32, (1, tokens_n), 1)
        bias[r, :] = jnp.where((u <= t) & (u >= began(t)), 0.0, -1e30)


    def turn(source, dest):
        @pl.loop(0, PAIRS)
        def _(n):
            c = aligned(n * 128, 128)
            dest[c, :] = source[:, c].T

    loads[5].wait()
    turn(cot, dy_t)
    pump()
    small.wait_second()
    first, second = spread_gains(plane, 32, wide, MODEL)
    gain_rows[0:1, :] = first
    gain_rows[1:2, :] = second
    dgain[...] = jnp.zeros_like(dgain)

    def inverse(x):
        return lax.rsqrt(jnp.mean(x * x, axis=-1, keepdims=True) + 1e-05)

    def row_loop(body):
        @pl.loop(0, tokens_n // ROW_STEP)
        def _(i):
            body(pl.ds(pl.multiple_of(i * ROW_STEP, ROW_STEP), ROW_STEP))

    def normed(source, gain, dest):
        def body(r):
            x = source[r, :].astype(F32)
            dest[r, :] = (x * inverse(x) * gain_rows[gain : gain + 1, :]).astype(BF)

        row_loop(body)

    loads[4].wait()
    normed(tok, 0, h1)
    pump()
    turn(h1, h1_t)
    pump()

    def weight(k, c):
        block = whole[k][:, :, :, c]
        return block.reshape(MODEL, block.shape[-1])

    lane = lax.broadcasted_iota(jnp.int32, (1, 128), 1)
    front = lane % 64 < 32
    of_head = (lane < 64, lane >= 64)

    def swap(v):
        return jnp.where(front, pltpu.roll(v, 96, 1), pltpu.roll(v, 32, 1))

    def project(part, dest):
        @pl.loop(0, MODEL // 256)
        def _(n):
            p = nn(h1[...], weight(0, aligned(part * MODEL + n * 256, 256)))
            for half in range(2):
                v = p[:, half * 128 : half * 128 + 128]
                if part < 2:
                    v = v * cosine[...] + swap(v) * signed_sine[...]
                v = v.astype(BF)
                if part == 0:
                    v = v * jnp.asarray(0.125, BF)
                dest[:, aligned(n * 256 + half * 128, 128)] = v

    def only(v, head):
        return jnp.where(of_head[head], v, jnp.zeros((), v.dtype))

    def attend(n):
        c = aligned(n * 128, 128)
        k, v, q = keys[:, c], values[:, c], query[:, c]
        for i in range(2):
            t, u = slice(256 * i, 256 * i + 256), slice(0, 256 * i + 256)
            o = []
            for head in range(2):
                s = nt(k[u], only(q[t], head)) + bias[u, t]
                top = jnp.max(s, axis=0, keepdims=True)
                p = jnp.exp(s - top)
                total = jnp.sum(p, axis=0, keepdims=True)
                p = (p * (1.0 / total)).astype(BF)
                logs[n, head : head + 1, t] = top + jnp.log(total)
                o.append(tn(p, v[u]))
            mixed[t, c] = jnp.where(of_head[0], o[0], o[1]).astype(BF)

    def attend_back(n):
        c = aligned(n * 128, 128)
        k, v, q, do = keys[:, c], values[:, c], query[:, c], dmixed[:, c]
        dq, dk, dv = [None, None], [], []
        low_k = low_v = high_k = high_v = None

        def plus(a, b):
            return b if a is None else a + b

        for head in range(2):
            km = only(k, head)
            for i in range(2):
                t, u = slice(256 * i, 256 * i + 256), slice(0, 256 * i + 256)
                qm, dom = only(q[t], head), only(do[t], head)
                s = nt(k[u], qm) + bias[u, t]
                p = jnp.exp(s - logs[n, head : head + 1, t])
                dp = nt(v[u], dom)
                centre = jnp.sum(p * dp, axis=0, keepdims=True)
                ds = (p * (dp - centre)).astype(BF)
                pb = p.astype(BF)
                dq[i] = plus(dq[i], tn(ds, km[u]))
                dk, dv = nn(ds, qm), nn(pb, dom)
                low_k, low_v = plus(low_k, dk[:256]), plus(low_v, dv[:256])
                if i == 1:
                    high_k, high_v = plus(high_k, dk[256:]), plus(high_v, dv[256:])

        def back(v, t):
            return v * cosine[t, :] - swap(v) * signed_sine[t, :]

        for i in range(2):
            t = slice(256 * i, 256 * i + 256)
            query[t, c] = back(dq[i] * 0.125, t).astype(BF)
            keys[t, c] = back((low_k, high_k)[i], t).astype(BF)
            values[t, c] = (low_v, high_v)[i].astype(BF)

    pump()
    project(0, query)
    pump()
    project(1, keys)
    pump()
    project(2, values)
    for n in range(PAIRS):
        pump()
        pl.loop(n, n + 1)(attend)
    pump()

    for n in range(3):
        c = slice(n * 256, n * 256 + 256)
        state[:, c] = tok[:, c].astype(F32) + nt(mixed[...], weight(1, slice(None))[c])
    pump()
    normed(state, 1, h2)
    pump()
    turn(h2, h2_t)

    def theirs(k):
        if k < 4:
            return theirs_at.at[:, :, :, pl.ds(OFFSETS[k], PIECES[k][3])]
        j, second = (k - 4) // 2, (k - 4) % 2
        return theirs_ff.at[j % 2, :, :, :, pl.ds(512 * second, 256 if second else 512)]

    reduce.other = theirs
    drained = set()

    def send_gradient(k, left, right, base):
        piece = PIECES[k]
        width = piece[3]
        step = 256 if width % 256 == 0 else 128

        def run(core, store):
            @pl.loop(0, width // step)
            def _(n):
                g = nn(left[...], right[:, aligned(base + core * width + n * step, step)])
                store(n * step, g.astype(BF).reshape(4, 4, 48, step))

        other = theirs(k)

        def to_other(start, g):
            other[:, :, :, aligned(start, step)] = g

        def to_mine(start, g):
            mine[:, :, :, aligned(OFFSETS[k] + start, step)] = g

        run(1 - place.c, to_other)
        reduce.begin(k)
        run(place.c, to_mine)

    out_acc[...] = state[...]
    dnorm[...] = jnp.zeros_like(dnorm)
    for j in range(4):
        kf, kd = 4 + 2 * j, 5 + 2 * j
        pump()
        gcols, ucols = slice(j * BLOCK, j * BLOCK + BLOCK), slice(2048 + j * BLOCK, 2048 + j * BLOCK + BLOCK)
        for n in range(BLOCK // 256):
            c = slice(n * 256, n * 256 + 256)
            gc = slice(gcols.start + c.start, gcols.start + c.stop)
            uc = slice(ucols.start + c.start, ucols.start + c.stop)
            gate[...] = nn(h2[...], weight(2, gc))
            up[...] = nn(h2[...], weight(2, uc))
            dact[...] = nn(cot[...], weight(3, gc))

            def pointwise(r):
                z, w, da = gate[r, :], up[r, :], dact[r, :]
                s = jax.nn.sigmoid(z)
                swish = z * s
                act[r, c] = (swish * w).astype(BF)
                dgu[r, c] = (da * w * s * (1.0 + z * (1.0 - s))).astype(BF)
                dgu[r, BLOCK + c.start : BLOCK + c.stop] = (da * swish).astype(BF)

            row_loop(pointwise)
            pump()

        if j >= 2:
            for k in (kf - 4, kd - 4):
                reduce.copy(k, 0).wait_send()
                drained.add(k)
        send_gradient(kf, h2_t, dgu, 0)
        pump()
        send_gradient(kd, dy_t, act, 0)
        pump()
        for n in range(3):
            c = slice(n * 256, n * 256 + 256)
            out_acc[:, c] += nt(act[...], weight(3, gcols)[c])
            dnorm[:, c] += nt(dgu[:, 0:BLOCK], weight(2, gcols)[c]) + nt(
                dgu[:, BLOCK : 2 * BLOCK], weight(2, ucols)[c]
            )
        pump()
    write_out = pltpu.make_async_copy(out_acc, block_out, local.at[0])
    write_out.start()

    def second_norm(r):
        x = state[r, :]
        inv = inverse(x)
        xh = x * inv
        dh = dnorm[r, :]
        dgain[1:2, :] += jnp.sum(dh * xh, axis=0, keepdims=True)
        e = dh * gain_rows[1:2, :]
        d = cot[r, :].astype(F32) + inv * (e - xh * jnp.mean(e * xh, axis=-1, keepdims=True))
        state[r, :] = d
        h2[r, :] = d.astype(BF)

    row_loop(second_norm)
    turn(h2, h2_t)
    pump()
    send_gradient(3, h2_t, mixed, 0)
    pump()
    for n in range(3):
        c = slice(n * 256, n * 256 + 256)
        dmixed[:, c] = nn(h2[...], weight(1, c)).astype(BF)
    pump()
    for n in range(PAIRS):
        pl.loop(n, n + 1)(attend_back)
        pump()
    send_gradient(0, h1_t, query, 0)
    pump()
    send_gradient(1, h1_t, keys, 0)
    pump()
    send_gradient(2, h1_t, values, 0)
    pump()
    for n in range(3):
        c = slice(n * 256, n * 256 + 256)
        dnorm[:, c] = (
            nt(query[...], weight(0, slice(0, MODEL))[c])
            + nt(keys[...], weight(0, slice(MODEL, 2 * MODEL))[c])
            + nt(values[...], weight(0, slice(2 * MODEL, 3 * MODEL))[c])
        )
        pump()

    def first_norm(r):
        x = tok[r, :].astype(F32)
        inv = inverse(x)
        xh = x * inv
        dh = dnorm[r, :]
        dgain[0:1, :] += jnp.sum(dh * xh, axis=0, keepdims=True)
        e = dh * gain_rows[0:1, :]
        state[r, :] += inv * (e - xh * jnp.mean(e * xh, axis=-1, keepdims=True))

    row_loop(first_norm)
    write_grad = pltpu.make_async_copy(state, token_grad, local.at[1])
    write_grad.start()
    group_g[place.fs] = dgain[...]
    small_g.start_first()
    pump()
    pump()
    assert next(points, None) is None
    small_g.wait_second()
    total = plane_g[0]
    for i in range(1, 8):
        total = total + plane_g[i]
    row = lax.broadcasted_iota(jnp.int32, (MODEL, 128), 0)
    lane = lax.broadcasted_iota(jnp.int32, (MODEL, 128), 1)
    wanted = (row == place.me * wide + lane) & (lane < wide)
    own = jnp.dot(
        total,
        wanted.astype(F32),
        preferred_element_type=F32,
        precision=lax.Precision.HIGHEST,
    )[0:2]
    gain_shard[...] = own[:, 0:wide]
    squares = square[0] + jnp.sum(own * own, axis=(0, 1), keepdims=True)
    group_s[place.fs] = jnp.broadcast_to(squares, (8, 128))
    small_s.start_first()
    small_s.wait_first()
    plane_s[place.dp] = group_s[0] + group_s[1] + group_s[2] + group_s[3]
    small_s.start_second()
    for k in range(COUNT):
        gather.drain(k)
        for i in range(1 if k in drained else 0, REDUCE_SEMS):
            reduce.copy(k, i).wait_send()
    small.drain()
    small_g.drain()
    write_out.wait()
    write_grad.wait()
    for k in range(COUNT):
        for copy in write_shard(k):
            copy.wait()
    small_s.wait_second()
    squares = plane_s[0]
    for i in range(1, 8):
        squares = squares + plane_s[i]
    square_out[...] = squares
    small_s.drain()


def update_kernel(*refs):
    squares, out_block, out_grad = refs[0:3]
    grads, weights, firsts, seconds = (refs[3 + 5 * i : 8 + 5 * i] for i in range(4))
    new_block, new_grad, norm = refs[23:26]
    new_w, new_m, new_v = (refs[26 + 5 * i : 31 + 5 * i] for i in range(3))
    local = refs[41]
    copies = [
        pltpu.make_async_copy(out_block, new_block, local.at[0]),
        pltpu.make_async_copy(out_grad, new_grad, local.at[1]),
    ]
    for copy in copies:
        copy.start()
    root = jnp.sqrt(squares[0:1, 0:1])
    norm[...] = root
    clip = CLIP_NORM / jnp.maximum(root, CLIP_NORM)
    decays = (WEIGHT_DECAY, WEIGHT_DECAY, WEIGHT_DECAY, WEIGHT_DECAY, 0.0)
    for i in range(5):
        step = 256 if weights[i].shape[1] % 256 == 0 else weights[i].shape[1]
        for n in range(weights[i].shape[1] // step):
            c = slice(n * step, n * step + step)
            results = adam_update(
                weights[i][:, c], grads[i][:, c], firsts[i][:, c], seconds[i][:, c],
                clip, decays[i], LEARN_RATES[i],
            )
            for dest, value in zip((new_w, new_m, new_v), results):
                dest[i][:, c] = value
    for copy in copies:
        copy.wait()


def any_spec():
    return pl.BlockSpec(memory_space=pl.ANY)


def vmem_spec():
    return pl.BlockSpec(memory_space=pltpu.VMEM)


def fast_body(tokens, cotangent, starts, *state):
    weights, firsts, seconds = state[0:5], state[5:10], state[10:15]
    wide = weights[4].shape[1]
    dma = pltpu.SemaphoreType.DMA
    shape = jax.ShapeDtypeStruct
    tall = (TOKENS_PER, MODEL)
    scratch = [pltpu.VMEM((4, 4, 48, w), BF) for w in WIDTHS] + [
        pltpu.VMEM((24, HALF), F32),
        pltpu.VMEM((4, 8, 128), F32),
        pltpu.VMEM((8, 4, 8, 128), F32),
        pltpu.VMEM((4, 4, 48, HALF), BF),
        pltpu.VMEM((4, 4, 48, HALF), BF),
        pltpu.VMEM((4, 48, HALF), BF),
        pltpu.VMEM((2, 4, 48, HALF), BF),
        pltpu.VMEM((3, 48, HALF), BF),
        pltpu.VMEM((2, 24, HALF), F32),
        pltpu.VMEM((24, HALF), F32),
        pltpu.VMEM((4, 8, MODEL), F32),
        pltpu.VMEM((8, 8, MODEL), F32),
        pltpu.VMEM((4, 8, 128), F32),
        pltpu.VMEM((8, 8, 128), F32),
        pltpu.VMEM((2, 4, 4, 48, 768), BF),
        pltpu.VMEM((4, 4, 48, 1536), BF),
        pltpu.VMEM((8, MODEL), F32),
        pltpu.VMEM((8, MODEL), F32),
        pltpu.VMEM((TOKENS_PER, 128), F32),
        pltpu.VMEM((TOKENS_PER, 128), F32),
        pltpu.VMEM((TOKENS_PER, TOKENS_PER), F32),
        pltpu.VMEM((PAIRS, 8, TOKENS_PER), F32),
        pltpu.VMEM(tall, BF),
        pltpu.VMEM((MODEL, TOKENS_PER), BF),
        pltpu.VMEM(tall, BF),
        pltpu.VMEM(tall, BF),
        pltpu.VMEM(tall, BF),
        pltpu.VMEM(tall, F32),
        pltpu.VMEM(tall, F32),
        pltpu.VMEM(tall, F32),
        pltpu.VMEM(tall, BF),
        pltpu.VMEM((MODEL, TOKENS_PER), BF),
        pltpu.VMEM((MODEL, TOKENS_PER), BF),
        pltpu.VMEM(tall, BF),
        pltpu.VMEM((TOKENS_PER, 256), F32),
        pltpu.VMEM((TOKENS_PER, 256), F32),
        pltpu.VMEM((TOKENS_PER, 256), F32),
        pltpu.VMEM((TOKENS_PER, BLOCK), BF),
        pltpu.VMEM((TOKENS_PER, 2 * BLOCK), BF),
        pltpu.VMEM(tall, BF),
        pltpu.VMEM(tall, BF),
        *[pltpu.VMEM((24, w), F32) for w in WIDTHS],
        dma((GATHER_TOTAL,)),
        dma((GATHER_TOTAL,)),
        dma((COUNT * REDUCE_SEMS,)),
        dma((COUNT * REDUCE_SEMS,)),
        dma((3 * SMALL_SEMS,)),
        dma((3 * SMALL_SEMS,)),
        dma((2 + 2 * COUNT,)),
        dma((6,)),
    ]
    block_out, token_grad, *shards, squares = pl.pallas_call(
        layer_kernel,
        out_shape=[shape(tall, F32)] * 2
        + [shape((24, w), F32) for w in WIDTHS]
        + [shape((2, wide), F32), shape((8, 128), F32)],
        in_specs=[any_spec()] * 2
        + [pl.BlockSpec(memory_space=pltpu.SMEM), vmem_spec()]
        + [any_spec()] * 4,
        out_specs=[any_spec()] * 6 + [vmem_spec()] * 2,
        scratch_shapes=scratch,
        compiler_params=pltpu.CompilerParams(
            collective_id=1, has_side_effects=True, vmem_limit_bytes=64 * 2**20 - 2**18
        ),
        name="layer_and_gradients",
    )(tokens, cotangent, starts, weights[4], *weights[0:4])
    outs = pl.pallas_call(
        update_kernel,
        out_shape=[shape(tall, F32)] * 2
        + [shape((1, 1), F32)]
        + [shape(w.shape, F32) for _ in range(3) for w in weights],
        in_specs=[vmem_spec()] * 23,
        out_specs=[any_spec()] * 2 + [vmem_spec()] * 16,
        scratch_shapes=[dma((2,))],
        compiler_params=pltpu.CompilerParams(vmem_limit_bytes=64 * 2**20 - 2**18),
        name="update_weights",
    )(squares, block_out, token_grad, *shards, *weights, *firsts, *seconds)
    return (outs[0], outs[1], outs[2].reshape(()), *outs[3:])


HD = 64
IMG = 257
STEP = 10


NORM_EPS = 1e-05
CLIP_NORM = 1.0
LEARN_RATES = (0.02, 0.1, 0.02, 0.02, 0.5)
FIRST_DECAY = 0.5
SECOND_DECAY = 0.5
ADAM_EPS = 1e-08
WEIGHT_DECAY = 0.05
ROPE_BASE = 10000.0
MASKED = -1e30
ROWS_CONTRACT = (((1,), (1,)), ((), ()))
TOKENS_CONTRACT = (((0,), (0,)), ((), ()))


def positions(begins, length):
    tok_index = jnp.arange(length, dtype=jnp.int32)
    began = begins[None, :] <= tok_index[:, None]
    segment = jnp.sum(began.astype(jnp.int32), axis=1)
    latest = jnp.max(jnp.where(began, begins[None, :], -4 * IMG), axis=1)
    return ((tok_index - latest).astype(jnp.float32), segment)


def rotation(rotary_place):
    half = HD // 2
    freq = ROPE_BASE ** (-jnp.arange(half, dtype=jnp.float32) * (2.0 / HD))
    angle = rotary_place[:, None] * freq[None, :]
    return (jnp.cos(angle), jnp.sin(angle))


def rotate(values, cosine, sine_table):
    half = values.shape[-1] // 2
    front, behind = (values[..., :half], values[..., half:])
    cos_part = cosine[:, None, :]
    sin_part = sine_table[:, None, :]
    return jnp.concatenate(
        [front * cos_part - behind * sin_part, behind * cos_part + front * sin_part], axis=-1
    )


def unrotate(grads, cosine, sine_table):
    half = grads.shape[-1] // 2
    front, behind = (grads[..., :half], grads[..., half:])
    cos_part = cosine[:, None, :]
    sin_part = sine_table[:, None, :]
    return jnp.concatenate(
        [front * cos_part + behind * sin_part, behind * cos_part - front * sin_part], axis=-1
    )


def norm_backward(normalized_gradient, standardized_input, inverse_norm, norm_gain):
    gain_scaled = normalized_gradient * norm_gain
    return inverse_norm * (
        gain_scaled
        - standardized_input * jnp.mean(gain_scaled * standardized_input, axis=-1, keepdims=True)
    )


def adam_update(weight, grad, first, second, clip_factor, decay, rate):
    grad = grad * clip_factor
    first = FIRST_DECAY * first + (1.0 - FIRST_DECAY) * grad
    second = SECOND_DECAY * second + (1.0 - SECOND_DECAY) * grad * grad
    fix_one = 1.0 - FIRST_DECAY**STEP
    fix_two = 1.0 - SECOND_DECAY**STEP
    change = first / fix_one / (jnp.sqrt(second / fix_two) + ADAM_EPS) + decay * weight
    return (weight - rate * change, first, second)


def body(
    tokens,
    cotangent,
    starts,
    attn_in,
    attn_out,
    ff_in,
    ff_out,
    gains,
    attn_in_m,
    attn_out_m,
    ff_in_m,
    ff_out_m,
    gains_m,
    attn_in_v,
    attn_out_v,
    ff_in_v,
    ff_out_v,
    gains_v,
):
    length, model_width = tokens.shape
    head_count = model_width // HD
    hidden_width = ff_in.shape[1] // 2
    scale = HD ** (-0.5)
    lowered = (
        attn_in.astype(jnp.bfloat16),
        attn_out.astype(jnp.bfloat16),
        ff_in.astype(jnp.bfloat16),
        ff_out.astype(jnp.bfloat16),
        gains.astype(jnp.bfloat16),
    )
    w_qkv, w_out, w_in, w_down, paired_gains = (
        lax.all_gather(lowered[0], ("dp", "fsdp"), axis=0, tiled=True),
        lax.all_gather(lowered[1], ("dp", "fsdp"), axis=0, tiled=True),
        lax.all_gather(lowered[2], ("dp", "fsdp"), axis=0, tiled=True),
        lax.all_gather(lowered[3], ("dp", "fsdp"), axis=0, tiled=True),
        lax.all_gather(lowered[4], ("dp", "fsdp"), axis=1, tiled=True),
    )
    paired_gains = paired_gains.astype(jnp.float32)
    rotary_place, segment = positions(starts[0], length)
    cosine, sine_table = rotation(rotary_place)
    tok_index = jnp.arange(length, dtype=jnp.int32)
    allowed = (segment[:, None] == segment[None, :]) & (tok_index[None, :] <= tok_index[:, None])
    layer_input = tokens.astype(jnp.float32)
    first_inverse_norm = lax.rsqrt(
        jnp.mean(layer_input * layer_input, axis=-1, keepdims=True) + NORM_EPS
    )
    first_standardized = layer_input * first_inverse_norm
    first_normalized = (first_standardized * paired_gains[0]).astype(jnp.bfloat16)
    projected = jnp.dot(first_normalized, w_qkv, preferred_element_type=jnp.float32)
    query = rotate(
        projected[:, :model_width].reshape(length, head_count, HD), cosine, sine_table
    ).astype(jnp.bfloat16)
    keys = rotate(
        projected[:, model_width : 2 * model_width].reshape(length, head_count, HD),
        cosine,
        sine_table,
    ).astype(jnp.bfloat16)
    values = projected[:, 2 * model_width :].reshape(length, head_count, HD).astype(jnp.bfloat16)
    span_rows = min(512, length)
    starting = 0
    scores = jnp.einsum("qhd,khd->hqk", query, keys, preferred_element_type=jnp.float32) * scale
    scores = jnp.where(allowed[None, starting : starting + span_rows], scores, MASKED)
    highest = jnp.max(scores, axis=-1, keepdims=True)
    shifted = jnp.exp(scores - highest)
    totals = jnp.sum(shifted, axis=-1, keepdims=True)
    soft_weights = (shifted / totals).astype(jnp.bfloat16)
    mixed_parts = jnp.einsum(
        "hqk,khd->qhd", soft_weights, values, preferred_element_type=jnp.float32
    )
    total_parts = highest[..., 0] + jnp.log(totals[..., 0])
    mixed = mixed_parts.reshape(length, model_width).astype(jnp.bfloat16)
    residual_state = layer_input + lax.dot_general(
        mixed, w_out, ROWS_CONTRACT, preferred_element_type=jnp.float32
    )
    second_inverse_norm = lax.rsqrt(
        jnp.mean(residual_state * residual_state, axis=-1, keepdims=True) + NORM_EPS
    )
    second_standardized = residual_state * second_inverse_norm
    second_normalized = (second_standardized * paired_gains[1]).astype(jnp.bfloat16)
    gate_up = jnp.dot(second_normalized, w_in, preferred_element_type=jnp.float32)
    gate_part = gate_up[:, :hidden_width]
    up_part = gate_up[:, hidden_width:]
    sigmoid_gate = jax.nn.sigmoid(gate_part)
    swish = gate_part * sigmoid_gate
    activated = (swish * up_part).astype(jnp.bfloat16)
    block_out = residual_state + lax.dot_general(
        activated, w_down, ROWS_CONTRACT, preferred_element_type=jnp.float32
    )
    incoming_gradient = cotangent.astype(jnp.float32)
    grad_down = lax.dot_general(
        cotangent, activated, TOKENS_CONTRACT, preferred_element_type=jnp.float32
    )
    grad_act = jnp.dot(cotangent, w_down, preferred_element_type=jnp.float32)
    grad_gate = grad_act * up_part * sigmoid_gate * (1.0 + gate_part * (1.0 - sigmoid_gate))
    grad_up = grad_act * swish
    grad_gu = jnp.concatenate([grad_gate, grad_up], axis=1).astype(jnp.bfloat16)
    grad_in = lax.dot_general(
        second_normalized, grad_gu, TOKENS_CONTRACT, preferred_element_type=jnp.float32
    )
    second_normalized_gradient = lax.dot_general(
        grad_gu, w_in, ROWS_CONTRACT, preferred_element_type=jnp.float32
    )
    second_gain_gradient = jnp.sum(second_normalized_gradient * second_standardized, axis=0)
    residual_gradient = incoming_gradient + norm_backward(
        second_normalized_gradient, second_standardized, second_inverse_norm, paired_gains[1]
    )
    grad_branch = residual_gradient.astype(jnp.bfloat16)
    grad_out = lax.dot_general(
        grad_branch, mixed, TOKENS_CONTRACT, preferred_element_type=jnp.float32
    )
    grad_mixed = jnp.dot(grad_branch, w_out, preferred_element_type=jnp.float32).astype(
        jnp.bfloat16
    )
    grad_mixed = grad_mixed.reshape(length, head_count, HD)
    starting = 0
    scores = jnp.einsum("qhd,khd->hqk", query, keys, preferred_element_type=jnp.float32) * scale
    scores = jnp.where(allowed[None, starting : starting + span_rows], scores, MASKED)
    soft_weights = jnp.exp(scores - total_parts[:, starting : starting + span_rows, None])
    grad_soft = jnp.einsum("qhd,khd->hqk", grad_mixed, values, preferred_element_type=jnp.float32)
    centre = jnp.sum(soft_weights * grad_soft, axis=-1, keepdims=True)
    grad_scores = (soft_weights * (grad_soft - centre)).astype(jnp.bfloat16)
    query_parts = (
        jnp.einsum("hqk,khd->qhd", grad_scores, keys, preferred_element_type=jnp.float32) * scale
    )
    grad_keys = (
        jnp.einsum("hqk,qhd->khd", grad_scores, query, preferred_element_type=jnp.float32) * scale
    )
    grad_values = jnp.einsum(
        "hqk,qhd->khd",
        soft_weights.astype(jnp.bfloat16),
        grad_mixed,
        preferred_element_type=jnp.float32,
    )
    grad_query = unrotate(query_parts, cosine, sine_table)
    grad_keys = unrotate(grad_keys, cosine, sine_table)
    grad_proj = jnp.concatenate(
        [
            grad_query.reshape(length, model_width),
            grad_keys.reshape(length, model_width),
            grad_values.reshape(length, model_width),
        ],
        axis=1,
    ).astype(jnp.bfloat16)
    grad_qkv = lax.dot_general(
        first_normalized, grad_proj, TOKENS_CONTRACT, preferred_element_type=jnp.float32
    )
    first_normalized_gradient = lax.dot_general(
        grad_proj, w_qkv, ROWS_CONTRACT, preferred_element_type=jnp.float32
    )
    first_gain_gradient = jnp.sum(first_normalized_gradient * first_standardized, axis=0)
    token_input_gradient = residual_gradient + norm_backward(
        first_normalized_gradient, first_standardized, first_inverse_norm, paired_gains[0]
    )
    shard_qkv, shard_out, shard_in, shard_down, shard_gains = (
        lax.psum_scatter(grad_qkv, ("dp", "fsdp"), scatter_dimension=0, tiled=True),
        lax.psum_scatter(grad_out, ("dp", "fsdp"), scatter_dimension=0, tiled=True),
        lax.psum_scatter(grad_in, ("dp", "fsdp"), scatter_dimension=0, tiled=True),
        lax.psum_scatter(grad_down, ("dp", "fsdp"), scatter_dimension=0, tiled=True),
        lax.psum_scatter(
            jnp.stack([first_gain_gradient, second_gain_gradient]),
            ("dp", "fsdp"),
            scatter_dimension=1,
            tiled=True,
        ),
    )
    shards = (shard_qkv, shard_out, shard_in, shard_down, shard_gains)
    local_sum = sum((jnp.sum(piece * piece) for piece in shards))
    global_squares = lax.psum(local_sum, ("dp", "fsdp"))
    grad_norm = jnp.sqrt(global_squares)
    clip_factor = CLIP_NORM / jnp.maximum(grad_norm, CLIP_NORM)
    masters = (attn_in, attn_out, ff_in, ff_out, gains)
    firsts = (attn_in_m, attn_out_m, ff_in_m, ff_out_m, gains_m)
    seconds = (attn_in_v, attn_out_v, ff_in_v, ff_out_v, gains_v)
    decays = (WEIGHT_DECAY, WEIGHT_DECAY, WEIGHT_DECAY, WEIGHT_DECAY, 0.0)
    results = [
        adam_update(w, g, m, v, clip_factor, dec, rate)
        for w, g, m, v, dec, rate in zip(masters, shards, firsts, seconds, decays, LEARN_RATES)
    ]
    return (
        block_out,
        token_input_gradient,
        grad_norm,
        results[0][0],
        results[1][0],
        results[2][0],
        results[3][0],
        results[4][0],
        results[0][1],
        results[1][1],
        results[2][1],
        results[3][1],
        results[4][1],
        results[0][2],
        results[1][2],
        results[2][2],
        results[3][2],
        results[4][2],
    )


def solution(mesh):
    in_specs = (
        P(("dp", "fsdp"), None),
        P(("dp", "fsdp"), None),
        P(("dp", "fsdp"), None),
        P(("dp", "fsdp"), None),
        P(("dp", "fsdp"), None),
        P(("dp", "fsdp"), None),
        P(("dp", "fsdp"), None),
        P(None, ("dp", "fsdp")),
        P(("dp", "fsdp"), None),
        P(("dp", "fsdp"), None),
        P(("dp", "fsdp"), None),
        P(("dp", "fsdp"), None),
        P(None, ("dp", "fsdp")),
        P(("dp", "fsdp"), None),
        P(("dp", "fsdp"), None),
        P(("dp", "fsdp"), None),
        P(("dp", "fsdp"), None),
        P(None, ("dp", "fsdp")),
    )
    out_specs = (
        P(("dp", "fsdp"), None),
        P(("dp", "fsdp"), None),
        P(),
        P(("dp", "fsdp"), None),
        P(("dp", "fsdp"), None),
        P(("dp", "fsdp"), None),
        P(("dp", "fsdp"), None),
        P(None, ("dp", "fsdp")),
        P(("dp", "fsdp"), None),
        P(("dp", "fsdp"), None),
        P(("dp", "fsdp"), None),
        P(("dp", "fsdp"), None),
        P(None, ("dp", "fsdp")),
        P(("dp", "fsdp"), None),
        P(("dp", "fsdp"), None),
        P(("dp", "fsdp"), None),
        P(("dp", "fsdp"), None),
        P(None, ("dp", "fsdp")),
    )
    fast = dict(mesh.shape) == {"dp": 8, "fsdp": 4}
    run = fast_body if fast else body
    return jax.shard_map(run, mesh=mesh, in_specs=in_specs, out_specs=out_specs, check_vma=False)
```

```python
import jax
import jax.numpy as jnp
from jax import lax
from jax.experimental import pallas as pl
from jax.experimental.pallas import tpu as pltpu
from jax.sharding import PartitionSpec as P

BF = jnp.bfloat16
F32 = jnp.float32
MESH_ID = pl.DeviceIdType.MESH

WIDTHS = (2304, 768, 4096, 2048)
PIECES = (
    (0, 0, 384, 384, 128),
    (0, 768, 1152, 384, 256),
    (0, 1536, 1920, 384, 128),
    (1, 0, 384, 384, 256),
    (2, 0, 2048, 512, 256),
    (3, 0, 256, 256, 128),
    (2, 512, 2560, 512, 256),
    (3, 512, 768, 256, 128),
    (2, 1024, 3072, 512, 256),
    (3, 1024, 1280, 256, 128),
    (2, 1536, 3584, 512, 256),
    (3, 1536, 1792, 256, 128),
)
Z_LAST = (7, 11)
EARLY = (0, 1, 2, 3, 4)
OFFSETS = tuple(sum(p[3] for p in PIECES[:k]) for k in range(len(PIECES)))
HALF = sum(p[3] for p in PIECES)
COUNT = len(PIECES)


class Place:
    def __init__(self):
        dp, fs = lax.axis_index("dp"), lax.axis_index("fsdp")
        self.dp, self.fs = dp, fs
        self.x, self.c = fs // 2, fs % 2
        self.z, self.y = dp // 2, dp % 2
        self.yx = self.y * 2 + self.x
        self.me = dp * 4 + fs
        self.sibling = (dp, self.x * 2 + 1 - self.c)
        self.xn = (dp, (1 - self.x) * 2 + self.c)
        self.yn = (self.z * 2 + 1 - self.y, fs)
        self.x_column = self.y * 2 + 1 - self.x
        self.y_column = (1 - self.y) * 2 + self.x
        self.diagonal = (1 - self.y) * 2 + 1 - self.x

    def z_peer(self, step):
        z = lax.rem(self.z + step, 4)
        return z, (z * 2 + self.y, self.fs)

    def group_peer(self, step):
        fs = lax.rem(self.fs + step, 4)
        return fs, (self.dp, fs)

    def plane_peer(self, step):
        dp = lax.rem(self.dp + step, 8)
        return dp, (dp, self.fs)

    def greet(self):
        barrier = pltpu.get_barrier_semaphore()
        for step in range(1, 4):
            pl.semaphore_signal(
                barrier, inc=1, device_id=self.group_peer(step)[1], device_id_type=MESH_ID
            )
        for step in range(1, 8):
            pl.semaphore_signal(
                barrier, inc=1, device_id=self.plane_peer(step)[1], device_id_type=MESH_ID
            )
        pl.semaphore_wait(barrier, 10)

    def columns(self, piece, sibling=False):
        first, second, width = piece[1], piece[2], piece[3]
        core = 1 - self.c if sibling else self.c
        start = jnp.where(core == 0, first, second)
        return pl.ds(pl.multiple_of(start, 128), width)

    def parts(self, piece):
        return (0, piece[4]), (piece[4], piece[3] - piece[4])


def remote(src, dst, send, recv, device):
    return pltpu.make_async_remote_copy(
        src_ref=src,
        dst_ref=dst,
        send_sem=send,
        recv_sem=recv,
        device_id=device,
        device_id_type=MESH_ID,
    )


GATHER_SEMS = 12
EARLY_SEMS = 8
GATHER_TOTAL = COUNT * GATHER_SEMS + len(EARLY) * EARLY_SEMS
REDUCE_SEMS = 9


class Gather:
    def __init__(self, place, shards, whole, sibling_rows, send, recv):
        self.p, self.shards, self.whole = place, shards, whole
        self.rows, self.send, self.recv = sibling_rows, send, recv

    def copy(self, k, which):
        p, piece = self.p, PIECES[k]
        w = self.whole[piece[0]]
        place = k * GATHER_SEMS + which
        if which >= GATHER_SEMS:
            place = COUNT * GATHER_SEMS + EARLY.index(k) * EARLY_SEMS + which - GATHER_SEMS
        sem = (self.send.at[place], self.recv.at[place])
        cols = p.columns(piece)

        def part(i):
            start, width = p.parts(piece)[i]
            return pl.ds(pl.multiple_of(cols.start + start, 128), width)

        if which == 0:
            shard = self.shards[piece[0]]
            return remote(
                shard.at[:, p.columns(piece, sibling=True)],
                self.rows.at[:, pl.ds(OFFSETS[k], piece[3])],
                *sem,
                p.sibling,
            )
        z_last = k in Z_LAST
        if which >= GATHER_SEMS:
            axis, step = (which - GATHER_SEMS) // 4, (which - GATHER_SEMS) % 4
            block = w.at[lax.rem(p.z + step, 4), p.yx, :, cols]
            return remote(block, block, *sem, (p.xn, p.yn)[axis])
        if which in (1, 2, 3):
            block = w.at[p.z, :, :, cols] if z_last else w.at[p.z, p.yx, :, cols]
            return remote(block, block, *sem, p.z_peer(which)[1])
        if which in (4, 5):
            block = w.at[p.z if z_last else slice(None), p.yx, :, cols]
            return remote(block, block, *sem, (p.xn, p.yn)[which - 4])
        if which in (6, 7):
            along_x = p.c == which - 6
            column = jnp.where(along_x, p.y_column, p.x_column)
            block = w.at[p.z if z_last else slice(None), column, :, part(which - 6)]
            device = (
                jnp.where(along_x, p.xn[0], p.yn[0]),
                jnp.where(along_x, p.xn[1], p.yn[1]),
            )
            return remote(block, block, *sem, device)
        if z_last:
            block = w.at[lax.rem(p.z + 12 - which, 4), :, :, cols]
        else:
            column = (p.yx, p.x_column, p.y_column, p.diagonal)[which - 8]
            block = w.at[:, column, :, cols]
        return remote(block, block, *sem, p.sibling)

    def exchange(self, k):
        self.copy(k, 0).start()

    def begin(self, k):
        p, piece = self.p, PIECES[k]
        self.copy(k, 0).wait_recv()
        mine = self.shards[piece[0]][:, p.columns(piece)]
        other = self.rows[:, OFFSETS[k] : OFFSETS[k] + piece[3]]
        first = p.c == 0
        both = jnp.concatenate(
            [jnp.where(first, mine, other), jnp.where(first, other, mine)], axis=0
        )
        self.whole[piece[0]][p.z, p.yx, :, p.columns(piece)] = both.astype(BF)
        self.start(k, (4, 5) if k in Z_LAST else (1, 2, 3))
        if k in EARLY:
            self.start(k, (12, 16))

    def start(self, k, which):
        for i in which:
            self.copy(k, i).start()

    def after(self, k, landed, started):
        for i in landed:
            self.copy(k, i).wait_recv()
        self.start(k, started)

    def step1(self, k):
        if k in Z_LAST:
            self.after(k, (4, 5), (6, 7))
        elif k in EARLY:
            self.after(k, (1, 2, 3), (13, 17, 14, 18, 15, 19, 8))
        else:
            self.after(k, (1, 2, 3), (4, 5, 8))

    def step2(self, k):
        if k in Z_LAST:
            self.after(k, (6, 7), (1, 2, 3, 8))
        elif k in EARLY:
            self.after(k, range(12, 20), (6, 7, 9, 10))
        else:
            self.after(k, (4, 5), (6, 7, 9, 10))

    def step3(self, k):
        if k in Z_LAST:
            self.after(k, (1, 2, 3), (9, 10, 11))
        else:
            self.after(k, (6, 7), (11,))

    def finish(self, k):
        for i in (8, 9, 10, 11):
            self.copy(k, i).wait_recv()

    def drain(self, k):
        early = k in EARLY
        for i in range(GATHER_SEMS + EARLY_SEMS if early else GATHER_SEMS):
            if not (early and i in (4, 5)):
                self.copy(k, i).wait_send()


class Reduce:
    def __init__(self, place, mine, other, landed, diag, cols, zed, done, got, send, recv):
        self.p = place
        self.mine, self.other, self.landed = mine, other, landed
        self.diag, self.cols, self.zed, self.done, self.got = diag, cols, zed, done, got
        self.send, self.recv = send, recv

    def copy(self, k, which):
        p, piece = self.p, PIECES[k]
        off, width = OFFSETS[k], piece[3]
        sem = (self.send.at[k * REDUCE_SEMS + which], self.recv.at[k * REDUCE_SEMS + which])
        span = pl.ds(off, width)
        if which == 0:
            return remote(
                self.other(k), self.landed.at[:, :, :, span], *sem, p.sibling
            )
        if which in (1, 2):
            start, wide = p.parts(piece)[which - 1]
            part = pl.ds(off + start, wide)
            along_x = p.c == which - 1
            device = (
                jnp.where(along_x, p.xn[0], p.yn[0]),
                jnp.where(along_x, p.xn[1], p.yn[1]),
            )
            if k in Z_LAST:
                return remote(
                    self.mine.at[p.z, p.diagonal, :, part], self.zed.at[0, :, part], *sem, device
                )
            return remote(
                self.mine.at[:, p.diagonal, :, part], self.diag.at[:, :, part], *sem, device
            )
        if which in (3, 4):
            column, device = ((p.x_column, p.xn), (p.y_column, p.yn))[which - 3]
            if k in Z_LAST:
                return remote(
                    self.mine.at[p.z, column, :, span],
                    self.zed.at[which - 2, :, span],
                    *sem,
                    device,
                )
            return remote(
                self.mine.at[:, column, :, span], self.cols.at[which - 3, :, :, span], *sem, device
            )
        if which in (5, 6, 7):
            z, device = p.z_peer(which - 4)
            if k in Z_LAST:
                return remote(
                    self.mine.at[z, :, :, span], self.slab(which - 5).at[:, :, span], *sem, device
                )
            return remote(
                self.mine.at[z, p.yx, :, span], self.zed.at[which - 5, :, span], *sem, device
            )
        return remote(
            self.done.at[1 - p.c, :, span], self.got.at[:, span], *sem, p.sibling
        )

    def slab(self, i):
        return (self.cols.at[0], self.cols.at[1], self.diag)[i]

    def begin(self, k):
        self.copy(k, 0).start()

    def step1(self, k):
        off, width = OFFSETS[k], PIECES[k][3]
        self.copy(k, 0).wait_recv()

        @pl.loop(0, 4)
        def _(z):
            for yx in range(4):
                total = self.mine[z, yx, :, off : off + width].astype(F32) + self.landed[
                    z, yx, :, off : off + width
                ].astype(F32)
                self.mine[z, yx, :, off : off + width] = total.astype(BF)

        for i in (5, 6, 7) if k in Z_LAST else (1, 2):
            self.copy(k, i).start()

    def z_last_step2(self, k):
        p = self.p
        off, width = OFFSETS[k], PIECES[k][3]
        for i in (5, 6, 7):
            self.copy(k, i).wait_recv()
        span = slice(off, off + width)

        @pl.loop(0, 4)
        def _(yx):
            total = self.mine[p.z, yx, :, span].astype(F32)
            for i in range(3):
                total = total + self.slab(i)[yx, :, span].astype(F32)
            self.mine[p.z, yx, :, span] = total.astype(BF)

        for i in (1, 2):
            self.copy(k, i).start()

    def z_last_step3(self, k):
        p, piece = self.p, PIECES[k]
        off = OFFSETS[k]
        for i in (1, 2):
            self.copy(k, i).wait_recv()
        for i in (0, 1):
            start, wide = p.parts(piece)[i]
            column = jnp.where(p.c == i, p.y_column, p.x_column)
            part = slice(off + start, off + start + wide)
            total = self.mine[p.z, column, :, part].astype(F32) + self.zed[0, :, part].astype(F32)
            self.mine[p.z, column, :, part] = total.astype(BF)
        for i in (3, 4):
            self.copy(k, i).start()

    def step2(self, k):
        if k in Z_LAST:
            self.z_last_step2(k)
            return
        p, piece = self.p, PIECES[k]
        off = OFFSETS[k]
        for i in (1, 2):
            self.copy(k, i).wait_recv()
        for i in (0, 1):
            start, wide = p.parts(piece)[i]
            column = jnp.where(p.c == i, p.y_column, p.x_column)
            part = slice(off + start, off + start + wide)

            @pl.loop(0, 4)
            def _(z):
                total = self.mine[z, column, :, part].astype(F32) + self.diag[z, :, part].astype(
                    F32
                )
                self.mine[z, column, :, part] = total.astype(BF)

        for i in (3, 4):
            self.copy(k, i).start()

    def step3(self, k):
        if k in Z_LAST:
            self.z_last_step3(k)
            return
        p = self.p
        off, width = OFFSETS[k], PIECES[k][3]
        span = slice(off, off + width)
        for i in (3, 4):
            self.copy(k, i).wait_recv()

        @pl.loop(0, 4)
        def _(z):
            total = (
                self.mine[z, p.yx, :, span].astype(F32)
                + self.cols[0, z, :, span].astype(F32)
                + self.cols[1, z, :, span].astype(F32)
            )
            self.mine[z, p.yx, :, span] = total.astype(BF)

        for i in (5, 6, 7):
            self.copy(k, i).start()

    def step4(self, k):
        p = self.p
        off, width = OFFSETS[k], PIECES[k][3]
        span = slice(off, off + width)
        for i in (3, 4) if k in Z_LAST else (5, 6, 7):
            self.copy(k, i).wait_recv()
        total = self.mine[p.z, p.yx, :, span].astype(F32)
        for i in (1, 2) if k in Z_LAST else (0, 1, 2):
            total = total + self.zed[i, :, span].astype(F32)
        self.done[0, :, span] = total[:24]
        self.done[1, :, span] = total[24:]
        self.copy(k, 8).start()

    def finish(self, k):
        self.copy(k, 8).wait_recv()

    def drain(self, k):
        for i in range(REDUCE_SEMS):
            self.copy(k, i).wait_send()


SMALL_SEMS = 10


class Small:
    def __init__(self, place, group, plane, send, recv, base):
        self.p, self.group, self.plane = place, group, plane
        self.send, self.recv, self.base = send, recv, base

    def first(self, step):
        i = self.base + step - 1
        slot = self.group.at[self.p.fs]
        return remote(slot, slot, self.send.at[i], self.recv.at[i], self.p.group_peer(step)[1])

    def second(self, step):
        i = self.base + 2 + step
        slot = self.plane.at[self.p.dp]
        return remote(slot, slot, self.send.at[i], self.recv.at[i], self.p.plane_peer(step)[1])

    def start_first(self):
        for step in range(1, 4):
            self.first(step).start()

    def wait_first(self):
        for step in range(1, 4):
            self.first(step).wait_recv()

    def start_second(self):
        for step in range(1, 8):
            self.second(step).start()

    def wait_second(self):
        for step in range(1, 8):
            self.second(step).wait_recv()

    def drain(self):
        for step in range(1, 4):
            self.first(step).wait_send()
        for step in range(1, 8):
            self.second(step).wait_send()


def spread_gains(plane, count, wide, total):
    slots = plane.reshape(count, 8, 128)
    owner = lax.broadcasted_iota(jnp.int32, (count, total), 1) // wide
    pick = (owner == lax.broadcasted_iota(jnp.int32, (count, total), 0)).astype(F32)
    lane = lax.broadcasted_iota(jnp.int32, (128, total), 1) % wide
    keep = lane == lax.broadcasted_iota(jnp.int32, (128, total), 0)
    rows = []
    for g in range(2):
        spread = lax.dot_general(
            slots[:, g, :], pick, (((0,), (0,)), ((), ())), preferred_element_type=F32
        )
        rows.append(jnp.sum(jnp.where(keep, spread, 0.0), axis=0, keepdims=True))
    return rows


TOKENS_PER = 512
MODEL = 768
PAIRS = MODEL // 128
BLOCK = 512
ROW_STEP = 64
PLAN = (
    ((0, 0, 0),),
    ((0, 0, 1), (0, 0, 2),),
    ((0, 0, 3), (0, 0, 4), (0, 0, 5), (0, 0, 6), (0, 0, 7), (0, 0, 8), (0, 0, 9), (0, 0, 10), (0, 0, 11),),
    (),
    (),
    ((0, 1, 0), (0, 1, 1), (0, 2, 0), (0, 1, 2), (0, 2, 1), (0, 3, 0), (0, 1, 3), (0, 4, 0),),
    ((0, 2, 2), (0, 3, 1), (0, 1, 4), (0, 4, 1),),
    ((0, 2, 3), (0, 1, 5), (0, 3, 2), (0, 4, 2),),
    (),
    ((0, 1, 6), (0, 1, 7), (0, 2, 4),),
    ((0, 3, 3),),
    ((0, 2, 5), (0, 4, 3),),
    ((0, 1, 8),),
    ((0, 1, 9),),
    (),
    ((0, 2, 6), (0, 2, 7),),
    ((0, 3, 4), (0, 1, 10), (0, 1, 11),),
    ((0, 3, 5), (0, 4, 4), (0, 4, 5),),
    (),
    ((0, 2, 8),),
    (),
    ((0, 2, 9),),
    ((1, 0, 4), (1, 0, 5), (0, 3, 6), (0, 3, 7),),
    ((0, 4, 6), (0, 4, 7),),
    ((0, 2, 10),),
    ((0, 2, 11),),
    ((0, 3, 8), (0, 3, 9),),
    (),
    ((1, 0, 6), (0, 4, 8), (0, 4, 9), (1, 1, 4), (1, 0, 7), (1, 1, 5),),
    (),
    ((0, 3, 10),),
    ((0, 4, 10),),
    ((1, 1, 6),),
    ((0, 3, 11),),
    ((1, 0, 8), (1, 0, 9), (0, 4, 11), (1, 2, 4),),
    (),
    ((1, 2, 5),),
    (),
    (),
    ((1, 1, 7), (1, 2, 6), (1, 0, 10),),
    ((1, 0, 11), (1, 1, 8), (1, 1, 9), (1, 2, 7),),
    ((1, 3, 4),),
    ((1, 1, 10), (1, 3, 5), (1, 4, 4),),
    ((1, 0, 3), (1, 4, 5),),
    ((1, 2, 8), (1, 3, 6),),
    ((1, 2, 9), (1, 3, 7), (1, 4, 6),),
    ((1, 4, 7),),
    ((1, 2, 10),),
    ((1, 1, 11), (1, 1, 3),),
    (),
    ((1, 2, 11), (1, 3, 8),),
    ((1, 0, 0), (1, 4, 8), (1, 3, 9), (1, 2, 3),),
    ((1, 0, 1), (1, 4, 9),),
    ((1, 0, 2), (1, 1, 0), (1, 3, 10), (1, 3, 11),),
    ((1, 4, 10), (1, 4, 11), (1, 1, 1),),
    ((1, 3, 3),),
    ((1, 1, 2), (1, 4, 3),),
    ((1, 2, 0), (1, 2, 1), (1, 3, 0), (2, 0, 0), (1, 2, 2), (1, 4, 0), (1, 3, 1), (1, 4, 1), (1, 3, 2), (1, 4, 2),),
)


def nn(a, b):
    return lax.dot_general(a, b, (((1,), (0,)), ((), ())), preferred_element_type=F32)


def nt(a, b):
    return lax.dot_general(a, b, (((1,), (1,)), ((), ())), preferred_element_type=F32)


def tn(a, b):
    return lax.dot_general(a, b, (((0,), (0,)), ((), ())), preferred_element_type=F32)


def aligned(start, size):
    return pl.ds(pl.multiple_of(start, 128), size)


def layer_kernel(
    tok_in, cot_in, starts, gains, w0_in, w1_in, w2_in, w3_in,
    block_out, token_grad, shard0, shard1, shard2, shard3, gain_shard, square_out,
    big0, big1, big2, big3, rows, group, plane,
    mine, landed, diag, cols_in, zed, done, got, group_g, plane_g, group_s, plane_s,
    theirs_ff, theirs_at, gain_rows, dgain, cosine, signed_sine, bias, logs,
    h1, h1_t, query, keys, values, state, out_acc, dnorm, h2, h2_t, dy_t, dmixed,
    gate, up, dact, act, dgu,
    tok, cot, w0, w1, w2, w3,
    g_send, g_recv, r_send, r_recv, s_send, s_recv, local, load,
):
    loads = [
        pltpu.make_async_copy(source, dest, load.at[i])
        for i, (source, dest) in enumerate(
            ((w0_in, w0), (w1_in, w1), (w2_in, w2), (w3_in, w3), (tok_in, tok), (cot_in, cot))
        )
    ]
    for copy in loads:
        copy.start()
    place = Place()
    place.greet()
    whole = (big0, big1, big2, big3)
    mixed = h1
    gather = Gather(place, (w0, w1, w2, w3), whole, rows, g_send, g_recv)

    wide = gains.shape[1]
    small = Small(place, group, plane, s_send, s_recv, 0)
    small_g = Small(place, group_g, plane_g, s_send, s_recv, SMALL_SEMS)
    small_s = Small(place, group_s, plane_s, s_send, s_recv, 2 * SMALL_SEMS)
    group[place.fs] = jnp.zeros((8, 128), F32)
    group[place.fs, 0:2, 0:wide] = gains[...].astype(BF).astype(F32)
    small.start_first()
    for copy in loads[0:4]:
        copy.wait()
    for k in range(COUNT):
        gather.exchange(k)
    reduce = Reduce(
        place, mine, None, landed, diag, cols_in, zed, done, got, r_send, r_recv
    )
    square = [jnp.zeros((1, 1), F32)]
    shards = (shard0, shard1, shard2, shard3)

    def write_shard(k):
        piece = PIECES[k]
        span = pl.ds(OFFSETS[k], piece[3])
        return [
            pltpu.make_async_copy(
                source, shards[piece[0]].at[:, place.columns(piece, sibling)], local.at[i]
            )
            for source, sibling, i in (
                (done.at[place.c, :, span], False, 2 + 2 * k),
                (got.at[:, span], True, 3 + 2 * k),
            )
        ]

    def finish(k):
        reduce.finish(k)
        piece = PIECES[k]
        span = slice(OFFSETS[k], OFFSETS[k] + piece[3])
        a, b = done[place.c, :, span], got[:, span]
        for copy in write_shard(k):
            copy.start()
        square[0] = square[0] + jnp.sum(a * a + b * b, axis=(0, 1), keepdims=True)

    stages = (
        (gather.begin, gather.step1, gather.step2, gather.step3, gather.finish),
        (reduce.step1, reduce.step2, reduce.step3, reduce.step4, finish),
    )
    points = iter(PLAN)

    def pump():
        for kind, stage, k in next(points):
            if kind == 2:
                share_gains()
            else:
                stages[kind][stage](k)

    def share_gains():
        small_g.wait_first()
        plane_g[place.dp] = group_g[0] + group_g[1] + group_g[2] + group_g[3]
        small_g.start_second()

    pump()
    small.wait_first()
    for i in range(4):
        plane[place.dp, i] = group[i]
    small.start_second()
    pump()

    tokens_n = TOKENS_PER
    images = starts.shape[1]
    place_in_half = lax.broadcasted_iota(jnp.int32, (1, 128), 1) % (HD // 2)
    freq = jnp.ones((1, 128), F32)
    for i in range(1, HD // 2):
        freq = jnp.where(place_in_half == i, ROPE_BASE ** (-2.0 * i / HD), freq)

    def began(t):
        latest = jnp.full(t.shape, -(10**6), jnp.int32)
        for j in range(images):
            s = starts[0, j]
            latest = jnp.maximum(latest, jnp.where(s <= t, s, -(10**6)))
        return latest

    @pl.loop(0, tokens_n // ROW_STEP)
    def _(i):
        r = pl.ds(pl.multiple_of(i * ROW_STEP, ROW_STEP), ROW_STEP)
        t = lax.broadcasted_iota(jnp.int32, (ROW_STEP, 128), 0) + i * ROW_STEP
        angle = (t - began(t)).astype(F32) * freq
        cosine[r, :] = jnp.cos(angle)
        lane = lax.broadcasted_iota(jnp.int32, (ROW_STEP, 128), 1)
        signed_sine[r, :] = jnp.where(lane % 64 < 32, -1.0, 1.0) * jnp.sin(angle)
        u = lax.broadcasted_iota(jnp.int32, (ROW_STEP, tokens_n), 0) + i * ROW_STEP
        t = lax.broadcasted_iota(jnp.int32, (1, tokens_n), 1)
        bias[r, :] = jnp.where((u <= t) & (u >= began(t)), 0.0, -1e30)


    def turn(source, dest):
        @pl.loop(0, PAIRS)
        def _(n):
            c = aligned(n * 128, 128)
            dest[c, :] = source[:, c].T

    loads[5].wait()
    turn(cot, dy_t)
    pump()
    small.wait_second()
    first, second = spread_gains(plane, 32, wide, MODEL)
    gain_rows[0:1, :] = first
    gain_rows[1:2, :] = second
    dgain[...] = jnp.zeros_like(dgain)

    def inverse(x):
        return lax.rsqrt(jnp.mean(x * x, axis=-1, keepdims=True) + 1e-05)

    def row_loop(body):
        @pl.loop(0, tokens_n // ROW_STEP)
        def _(i):
            body(pl.ds(pl.multiple_of(i * ROW_STEP, ROW_STEP), ROW_STEP))

    def normed(source, gain, dest):
        def body(r):
            x = source[r, :].astype(F32)
            dest[r, :] = (x * inverse(x) * gain_rows[gain : gain + 1, :]).astype(BF)

        row_loop(body)

    loads[4].wait()
    normed(tok, 0, h1)
    pump()
    turn(h1, h1_t)
    pump()

    def weight(k, c):
        block = whole[k][:, :, :, c]
        return block.reshape(MODEL, block.shape[-1])

    lane = lax.broadcasted_iota(jnp.int32, (1, 128), 1)
    front = lane % 64 < 32
    of_head = (lane < 64, lane >= 64)

    def swap(v):
        return jnp.where(front, pltpu.roll(v, 96, 1), pltpu.roll(v, 32, 1))

    def project(part, dest):
        @pl.loop(0, MODEL // 256)
        def _(n):
            p = nn(h1[...], weight(0, aligned(part * MODEL + n * 256, 256)))
            for half in range(2):
                v = p[:, half * 128 : half * 128 + 128]
                if part < 2:
                    v = v * cosine[...] + swap(v) * signed_sine[...]
                v = v.astype(BF)
                if part == 0:
                    v = v * jnp.asarray(0.125, BF)
                dest[:, aligned(n * 256 + half * 128, 128)] = v

    def only(v, head):
        return jnp.where(of_head[head], v, jnp.zeros((), v.dtype))

    def attend(n):
        c = aligned(n * 128, 128)
        k, v, q = keys[:, c], values[:, c], query[:, c]
        for i in range(2):
            t, u = slice(256 * i, 256 * i + 256), slice(0, 256 * i + 256)
            o = []
            for head in range(2):
                s = nt(k[u], only(q[t], head)) + bias[u, t]
                top = jnp.max(s, axis=0, keepdims=True)
                p = jnp.exp(s - top)
                total = jnp.sum(p, axis=0, keepdims=True)
                p = (p * (1.0 / total)).astype(BF)
                logs[n, head : head + 1, t] = top + jnp.log(total)
                o.append(tn(p, v[u]))
            mixed[t, c] = jnp.where(of_head[0], o[0], o[1]).astype(BF)

    def attend_back(n):
        c = aligned(n * 128, 128)
        k, v, q, do = keys[:, c], values[:, c], query[:, c], dmixed[:, c]
        dq, dk, dv = [None, None], [], []
        low_k = low_v = high_k = high_v = None

        def plus(a, b):
            return b if a is None else a + b

        for head in range(2):
            km = only(k, head)
            for i in range(2):
                t, u = slice(256 * i, 256 * i + 256), slice(0, 256 * i + 256)
                qm, dom = only(q[t], head), only(do[t], head)
                s = nt(k[u], qm) + bias[u, t]
                p = jnp.exp(s - logs[n, head : head + 1, t])
                dp = nt(v[u], dom)
                centre = jnp.sum(p * dp, axis=0, keepdims=True)
                ds = (p * (dp - centre)).astype(BF)
                pb = p.astype(BF)
                dq[i] = plus(dq[i], tn(ds, km[u]))
                dk, dv = nn(ds, qm), nn(pb, dom)
                low_k, low_v = plus(low_k, dk[:256]), plus(low_v, dv[:256])
                if i == 1:
                    high_k, high_v = plus(high_k, dk[256:]), plus(high_v, dv[256:])

        def back(v, t):
            return v * cosine[t, :] - swap(v) * signed_sine[t, :]

        for i in range(2):
            t = slice(256 * i, 256 * i + 256)
            query[t, c] = back(dq[i] * 0.125, t).astype(BF)
            keys[t, c] = back((low_k, high_k)[i], t).astype(BF)
            values[t, c] = (low_v, high_v)[i].astype(BF)

    pump()
    project(0, query)
    pump()
    project(1, keys)
    pump()
    project(2, values)
    for n in range(PAIRS):
        pump()
        pl.loop(n, n + 1)(attend)
    pump()

    for n in range(3):
        c = slice(n * 256, n * 256 + 256)
        state[:, c] = tok[:, c].astype(F32) + nt(mixed[...], weight(1, slice(None))[c])
    pump()
    normed(state, 1, h2)
    pump()
    turn(h2, h2_t)

    def theirs(k):
        if k < 4:
            return theirs_at.at[:, :, :, pl.ds(OFFSETS[k], PIECES[k][3])]
        j, second = (k - 4) // 2, (k - 4) % 2
        return theirs_ff.at[j % 2, :, :, :, pl.ds(512 * second, 256 if second else 512)]

    reduce.other = theirs
    drained = set()

    def send_gradient(k, left, right, base):
        piece = PIECES[k]
        width = piece[3]
        step = 256 if width % 256 == 0 else 128

        def run(core, store):
            @pl.loop(0, width // step)
            def _(n):
                g = nn(left[...], right[:, aligned(base + core * width + n * step, step)])
                store(n * step, g.astype(BF).reshape(4, 4, 48, step))

        other = theirs(k)

        def to_other(start, g):
            other[:, :, :, aligned(start, step)] = g

        def to_mine(start, g):
            mine[:, :, :, aligned(OFFSETS[k] + start, step)] = g

        run(1 - place.c, to_other)
        reduce.begin(k)
        run(place.c, to_mine)

    out_acc[...] = state[...]
    dnorm[...] = jnp.zeros_like(dnorm)
    for j in range(4):
        kf, kd = 4 + 2 * j, 5 + 2 * j
        pump()
        gcols, ucols = slice(j * BLOCK, j * BLOCK + BLOCK), slice(2048 + j * BLOCK, 2048 + j * BLOCK + BLOCK)
        for n in range(BLOCK // 256):
            c = slice(n * 256, n * 256 + 256)
            gc = slice(gcols.start + c.start, gcols.start + c.stop)
            uc = slice(ucols.start + c.start, ucols.start + c.stop)
            gate[...] = nn(h2[...], weight(2, gc))
            up[...] = nn(h2[...], weight(2, uc))
            dact[...] = nn(cot[...], weight(3, gc))

            def pointwise(r):
                z, w, da = gate[r, :], up[r, :], dact[r, :]
                s = jax.nn.sigmoid(z)
                swish = z * s
                act[r, c] = (swish * w).astype(BF)
                dgu[r, c] = (da * w * s * (1.0 + z * (1.0 - s))).astype(BF)
                dgu[r, BLOCK + c.start : BLOCK + c.stop] = (da * swish).astype(BF)

            row_loop(pointwise)
            pump()

        if j >= 2:
            for k in (kf - 4, kd - 4):
                reduce.copy(k, 0).wait_send()
                drained.add(k)
        send_gradient(kf, h2_t, dgu, 0)
        pump()
        send_gradient(kd, dy_t, act, 0)
        pump()
        for n in range(3):
            c = slice(n * 256, n * 256 + 256)
            out_acc[:, c] += nt(act[...], weight(3, gcols)[c])
            dnorm[:, c] += nt(dgu[:, 0:BLOCK], weight(2, gcols)[c]) + nt(
                dgu[:, BLOCK : 2 * BLOCK], weight(2, ucols)[c]
            )
        pump()
    write_out = pltpu.make_async_copy(out_acc, block_out, local.at[0])
    write_out.start()

    def second_norm(r):
        x = state[r, :]
        inv = inverse(x)
        xh = x * inv
        dh = dnorm[r, :]
        dgain[1:2, :] += jnp.sum(dh * xh, axis=0, keepdims=True)
        e = dh * gain_rows[1:2, :]
        d = cot[r, :].astype(F32) + inv * (e - xh * jnp.mean(e * xh, axis=-1, keepdims=True))
        state[r, :] = d
        h2[r, :] = d.astype(BF)

    row_loop(second_norm)
    turn(h2, h2_t)
    pump()
    send_gradient(3, h2_t, mixed, 0)
    pump()
    for n in range(3):
        c = slice(n * 256, n * 256 + 256)
        dmixed[:, c] = nn(h2[...], weight(1, c)).astype(BF)
    pump()
    for n in range(PAIRS):
        pl.loop(n, n + 1)(attend_back)
        pump()
    send_gradient(0, h1_t, query, 0)
    pump()
    send_gradient(1, h1_t, keys, 0)
    pump()
    send_gradient(2, h1_t, values, 0)
    pump()
    for n in range(3):
        c = slice(n * 256, n * 256 + 256)
        dnorm[:, c] = (
            nt(query[...], weight(0, slice(0, MODEL))[c])
            + nt(keys[...], weight(0, slice(MODEL, 2 * MODEL))[c])
            + nt(values[...], weight(0, slice(2 * MODEL, 3 * MODEL))[c])
        )
        pump()

    def first_norm(r):
        x = tok[r, :].astype(F32)
        inv = inverse(x)
        xh = x * inv
        dh = dnorm[r, :]
        dgain[0:1, :] += jnp.sum(dh * xh, axis=0, keepdims=True)
        e = dh * gain_rows[0:1, :]
        state[r, :] += inv * (e - xh * jnp.mean(e * xh, axis=-1, keepdims=True))

    row_loop(first_norm)
    write_grad = pltpu.make_async_copy(state, token_grad, local.at[1])
    write_grad.start()
    group_g[place.fs] = dgain[...]
    small_g.start_first()
    pump()
    pump()
    assert next(points, None) is None
    small_g.wait_second()
    total = plane_g[0]
    for i in range(1, 8):
        total = total + plane_g[i]
    row = lax.broadcasted_iota(jnp.int32, (MODEL, 128), 0)
    lane = lax.broadcasted_iota(jnp.int32, (MODEL, 128), 1)
    wanted = (row == place.me * wide + lane) & (lane < wide)
    own = jnp.dot(
        total,
        wanted.astype(F32),
        preferred_element_type=F32,
        precision=lax.Precision.HIGHEST,
    )[0:2]
    gain_shard[...] = own[:, 0:wide]
    squares = square[0] + jnp.sum(own * own, axis=(0, 1), keepdims=True)
    group_s[place.fs] = jnp.broadcast_to(squares, (8, 128))
    small_s.start_first()
    small_s.wait_first()
    plane_s[place.dp] = group_s[0] + group_s[1] + group_s[2] + group_s[3]
    small_s.start_second()
    for k in range(COUNT):
        gather.drain(k)
        for i in range(1 if k in drained else 0, REDUCE_SEMS):
            reduce.copy(k, i).wait_send()
    small.drain()
    small_g.drain()
    write_out.wait()
    write_grad.wait()
    for k in range(COUNT):
        for copy in write_shard(k):
            copy.wait()
    small_s.wait_second()
    squares = plane_s[0]
    for i in range(1, 8):
        squares = squares + plane_s[i]
    square_out[...] = squares
    small_s.drain()


def update_kernel(*refs):
    squares, out_block, out_grad = refs[0:3]
    grads, weights, firsts, seconds = (refs[3 + 5 * i : 8 + 5 * i] for i in range(4))
    new_block, new_grad, norm = refs[23:26]
    new_w, new_m, new_v = (refs[26 + 5 * i : 31 + 5 * i] for i in range(3))
    local = refs[41]
    copies = [
        pltpu.make_async_copy(out_block, new_block, local.at[0]),
        pltpu.make_async_copy(out_grad, new_grad, local.at[1]),
    ]
    for copy in copies:
        copy.start()
    root = jnp.sqrt(squares[0:1, 0:1])
    norm[...] = root
    clip = CLIP_NORM / jnp.maximum(root, CLIP_NORM)
    decays = (WEIGHT_DECAY, WEIGHT_DECAY, WEIGHT_DECAY, WEIGHT_DECAY, 0.0)
    for i in range(5):
        step = 256 if weights[i].shape[1] % 256 == 0 else weights[i].shape[1]
        for n in range(weights[i].shape[1] // step):
            c = slice(n * step, n * step + step)
            results = adam_update(
                weights[i][:, c], grads[i][:, c], firsts[i][:, c], seconds[i][:, c],
                clip, decays[i], LEARN_RATES[i],
            )
            for dest, value in zip((new_w, new_m, new_v), results):
                dest[i][:, c] = value
    for copy in copies:
        copy.wait()


def any_spec():
    return pl.BlockSpec(memory_space=pl.ANY)


def vmem_spec():
    return pl.BlockSpec(memory_space=pltpu.VMEM)


def fast_body(tokens, cotangent, starts, *state):
    weights, firsts, seconds = state[0:5], state[5:10], state[10:15]
    wide = weights[4].shape[1]
    dma = pltpu.SemaphoreType.DMA
    shape = jax.ShapeDtypeStruct
    tall = (TOKENS_PER, MODEL)
    scratch = [pltpu.VMEM((4, 4, 48, w), BF) for w in WIDTHS] + [
        pltpu.VMEM((24, HALF), F32),
        pltpu.VMEM((4, 8, 128), F32),
        pltpu.VMEM((8, 4, 8, 128), F32),
        pltpu.VMEM((4, 4, 48, HALF), BF),
        pltpu.VMEM((4, 4, 48, HALF), BF),
        pltpu.VMEM((4, 48, HALF), BF),
        pltpu.VMEM((2, 4, 48, HALF), BF),
        pltpu.VMEM((3, 48, HALF), BF),
        pltpu.VMEM((2, 24, HALF), F32),
        pltpu.VMEM((24, HALF), F32),
        pltpu.VMEM((4, 8, MODEL), F32),
        pltpu.VMEM((8, 8, MODEL), F32),
        pltpu.VMEM((4, 8, 128), F32),
        pltpu.VMEM((8, 8, 128), F32),
        pltpu.VMEM((2, 4, 4, 48, 768), BF),
        pltpu.VMEM((4, 4, 48, 1536), BF),
        pltpu.VMEM((8, MODEL), F32),
        pltpu.VMEM((8, MODEL), F32),
        pltpu.VMEM((TOKENS_PER, 128), F32),
        pltpu.VMEM((TOKENS_PER, 128), F32),
        pltpu.VMEM((TOKENS_PER, TOKENS_PER), F32),
        pltpu.VMEM((PAIRS, 8, TOKENS_PER), F32),
        pltpu.VMEM(tall, BF),
        pltpu.VMEM((MODEL, TOKENS_PER), BF),
        pltpu.VMEM(tall, BF),
        pltpu.VMEM(tall, BF),
        pltpu.VMEM(tall, BF),
        pltpu.VMEM(tall, F32),
        pltpu.VMEM(tall, F32),
        pltpu.VMEM(tall, F32),
        pltpu.VMEM(tall, BF),
        pltpu.VMEM((MODEL, TOKENS_PER), BF),
        pltpu.VMEM((MODEL, TOKENS_PER), BF),
        pltpu.VMEM(tall, BF),
        pltpu.VMEM((TOKENS_PER, 256), F32),
        pltpu.VMEM((TOKENS_PER, 256), F32),
        pltpu.VMEM((TOKENS_PER, 256), F32),
        pltpu.VMEM((TOKENS_PER, BLOCK), BF),
        pltpu.VMEM((TOKENS_PER, 2 * BLOCK), BF),
        pltpu.VMEM(tall, BF),
        pltpu.VMEM(tall, BF),
        *[pltpu.VMEM((24, w), F32) for w in WIDTHS],
        dma((GATHER_TOTAL,)),
        dma((GATHER_TOTAL,)),
        dma((COUNT * REDUCE_SEMS,)),
        dma((COUNT * REDUCE_SEMS,)),
        dma((3 * SMALL_SEMS,)),
        dma((3 * SMALL_SEMS,)),
        dma((2 + 2 * COUNT,)),
        dma((6,)),
    ]
    block_out, token_grad, *shards, squares = pl.pallas_call(
        layer_kernel,
        out_shape=[shape(tall, F32)] * 2
        + [shape((24, w), F32) for w in WIDTHS]
        + [shape((2, wide), F32), shape((8, 128), F32)],
        in_specs=[any_spec()] * 2
        + [pl.BlockSpec(memory_space=pltpu.SMEM), vmem_spec()]
        + [any_spec()] * 4,
        out_specs=[any_spec()] * 6 + [vmem_spec()] * 2,
        scratch_shapes=scratch,
        compiler_params=pltpu.CompilerParams(
            collective_id=1, has_side_effects=True, vmem_limit_bytes=64 * 2**20 - 2**18
        ),
        name="layer_and_gradients",
    )(tokens, cotangent, starts, weights[4], *weights[0:4])
    outs = pl.pallas_call(
        update_kernel,
        out_shape=[shape(tall, F32)] * 2
        + [shape((1, 1), F32)]
        + [shape(w.shape, F32) for _ in range(3) for w in weights],
        in_specs=[vmem_spec()] * 23,
        out_specs=[any_spec()] * 2 + [vmem_spec()] * 16,
        scratch_shapes=[dma((2,))],
        compiler_params=pltpu.CompilerParams(vmem_limit_bytes=64 * 2**20 - 2**18),
        name="update_weights",
    )(squares, block_out, token_grad, *shards, *weights, *firsts, *seconds)
    return (outs[0], outs[1], outs[2].reshape(()), *outs[3:])


HD = 64
IMG = 257
STEP = 10


NORM_EPS = 1e-05
CLIP_NORM = 1.0
LEARN_RATES = (0.02, 0.1, 0.02, 0.02, 0.5)
FIRST_DECAY = 0.5
SECOND_DECAY = 0.5
ADAM_EPS = 1e-08
WEIGHT_DECAY = 0.05
ROPE_BASE = 10000.0
MASKED = -1e30
ROWS_CONTRACT = (((1,), (1,)), ((), ()))
TOKENS_CONTRACT = (((0,), (0,)), ((), ()))


def positions(begins, length):
    tok_index = jnp.arange(length, dtype=jnp.int32)
    began = begins[None, :] <= tok_index[:, None]
    segment = jnp.sum(began.astype(jnp.int32), axis=1)
    latest = jnp.max(jnp.where(began, begins[None, :], -4 * IMG), axis=1)
    return ((tok_index - latest).astype(jnp.float32), segment)


def rotation(rotary_place):
    half = HD // 2
    freq = ROPE_BASE ** (-jnp.arange(half, dtype=jnp.float32) * (2.0 / HD))
    angle = rotary_place[:, None] * freq[None, :]
    return (jnp.cos(angle), jnp.sin(angle))


def rotate(values, cosine, sine_table):
    half = values.shape[-1] // 2
    front, behind = (values[..., :half], values[..., half:])
    cos_part = cosine[:, None, :]
    sin_part = sine_table[:, None, :]
    return jnp.concatenate(
        [front * cos_part - behind * sin_part, behind * cos_part + front * sin_part], axis=-1
    )


def unrotate(grads, cosine, sine_table):
    half = grads.shape[-1] // 2
    front, behind = (grads[..., :half], grads[..., half:])
    cos_part = cosine[:, None, :]
    sin_part = sine_table[:, None, :]
    return jnp.concatenate(
        [front * cos_part + behind * sin_part, behind * cos_part - front * sin_part], axis=-1
    )


def norm_backward(normalized_gradient, standardized_input, inverse_norm, norm_gain):
    gain_scaled = normalized_gradient * norm_gain
    return inverse_norm * (
        gain_scaled
        - standardized_input * jnp.mean(gain_scaled * standardized_input, axis=-1, keepdims=True)
    )


def adam_update(weight, grad, first, second, clip_factor, decay, rate):
    grad = grad * clip_factor
    first = FIRST_DECAY * first + (1.0 - FIRST_DECAY) * grad
    second = SECOND_DECAY * second + (1.0 - SECOND_DECAY) * grad * grad
    fix_one = 1.0 - FIRST_DECAY**STEP
    fix_two = 1.0 - SECOND_DECAY**STEP
    change = first / fix_one / (jnp.sqrt(second / fix_two) + ADAM_EPS) + decay * weight
    return (weight - rate * change, first, second)


def body(
    tokens,
    cotangent,
    starts,
    attn_in,
    attn_out,
    ff_in,
    ff_out,
    gains,
    attn_in_m,
    attn_out_m,
    ff_in_m,
    ff_out_m,
    gains_m,
    attn_in_v,
    attn_out_v,
    ff_in_v,
    ff_out_v,
    gains_v,
):
    length, model_width = tokens.shape
    head_count = model_width // HD
    hidden_width = ff_in.shape[1] // 2
    scale = HD ** (-0.5)
    lowered = (
        attn_in.astype(jnp.bfloat16),
        attn_out.astype(jnp.bfloat16),
        ff_in.astype(jnp.bfloat16),
        ff_out.astype(jnp.bfloat16),
        gains.astype(jnp.bfloat16),
    )
    w_qkv, w_out, w_in, w_down, paired_gains = (
        lax.all_gather(lowered[0], ("dp", "fsdp"), axis=0, tiled=True),
        lax.all_gather(lowered[1], ("dp", "fsdp"), axis=0, tiled=True),
        lax.all_gather(lowered[2], ("dp", "fsdp"), axis=0, tiled=True),
        lax.all_gather(lowered[3], ("dp", "fsdp"), axis=0, tiled=True),
        lax.all_gather(lowered[4], ("dp", "fsdp"), axis=1, tiled=True),
    )
    paired_gains = paired_gains.astype(jnp.float32)
    rotary_place, segment = positions(starts[0], length)
    cosine, sine_table = rotation(rotary_place)
    tok_index = jnp.arange(length, dtype=jnp.int32)
    allowed = (segment[:, None] == segment[None, :]) & (tok_index[None, :] <= tok_index[:, None])
    layer_input = tokens.astype(jnp.float32)
    first_inverse_norm = lax.rsqrt(
        jnp.mean(layer_input * layer_input, axis=-1, keepdims=True) + NORM_EPS
    )
    first_standardized = layer_input * first_inverse_norm
    first_normalized = (first_standardized * paired_gains[0]).astype(jnp.bfloat16)
    projected = jnp.dot(first_normalized, w_qkv, preferred_element_type=jnp.float32)
    query = rotate(
        projected[:, :model_width].reshape(length, head_count, HD), cosine, sine_table
    ).astype(jnp.bfloat16)
    keys = rotate(
        projected[:, model_width : 2 * model_width].reshape(length, head_count, HD),
        cosine,
        sine_table,
    ).astype(jnp.bfloat16)
    values = projected[:, 2 * model_width :].reshape(length, head_count, HD).astype(jnp.bfloat16)
    span_rows = min(512, length)
    starting = 0
    scores = jnp.einsum("qhd,khd->hqk", query, keys, preferred_element_type=jnp.float32) * scale
    scores = jnp.where(allowed[None, starting : starting + span_rows], scores, MASKED)
    highest = jnp.max(scores, axis=-1, keepdims=True)
    shifted = jnp.exp(scores - highest)
    totals = jnp.sum(shifted, axis=-1, keepdims=True)
    soft_weights = (shifted / totals).astype(jnp.bfloat16)
    mixed_parts = jnp.einsum(
        "hqk,khd->qhd", soft_weights, values, preferred_element_type=jnp.float32
    )
    total_parts = highest[..., 0] + jnp.log(totals[..., 0])
    mixed = mixed_parts.reshape(length, model_width).astype(jnp.bfloat16)
    residual_state = layer_input + lax.dot_general(
        mixed, w_out, ROWS_CONTRACT, preferred_element_type=jnp.float32
    )
    second_inverse_norm = lax.rsqrt(
        jnp.mean(residual_state * residual_state, axis=-1, keepdims=True) + NORM_EPS
    )
    second_standardized = residual_state * second_inverse_norm
    second_normalized = (second_standardized * paired_gains[1]).astype(jnp.bfloat16)
    gate_up = jnp.dot(second_normalized, w_in, preferred_element_type=jnp.float32)
    gate_part = gate_up[:, :hidden_width]
    up_part = gate_up[:, hidden_width:]
    sigmoid_gate = jax.nn.sigmoid(gate_part)
    swish = gate_part * sigmoid_gate
    activated = (swish * up_part).astype(jnp.bfloat16)
    block_out = residual_state + lax.dot_general(
        activated, w_down, ROWS_CONTRACT, preferred_element_type=jnp.float32
    )
    incoming_gradient = cotangent.astype(jnp.float32)
    grad_down = lax.dot_general(
        cotangent, activated, TOKENS_CONTRACT, preferred_element_type=jnp.float32
    )
    grad_act = jnp.dot(cotangent, w_down, preferred_element_type=jnp.float32)
    grad_gate = grad_act * up_part * sigmoid_gate * (1.0 + gate_part * (1.0 - sigmoid_gate))
    grad_up = grad_act * swish
    grad_gu = jnp.concatenate([grad_gate, grad_up], axis=1).astype(jnp.bfloat16)
    grad_in = lax.dot_general(
        second_normalized, grad_gu, TOKENS_CONTRACT, preferred_element_type=jnp.float32
    )
    second_normalized_gradient = lax.dot_general(
        grad_gu, w_in, ROWS_CONTRACT, preferred_element_type=jnp.float32
    )
    second_gain_gradient = jnp.sum(second_normalized_gradient * second_standardized, axis=0)
    residual_gradient = incoming_gradient + norm_backward(
        second_normalized_gradient, second_standardized, second_inverse_norm, paired_gains[1]
    )
    grad_branch = residual_gradient.astype(jnp.bfloat16)
    grad_out = lax.dot_general(
        grad_branch, mixed, TOKENS_CONTRACT, preferred_element_type=jnp.float32
    )
    grad_mixed = jnp.dot(grad_branch, w_out, preferred_element_type=jnp.float32).astype(
        jnp.bfloat16
    )
    grad_mixed = grad_mixed.reshape(length, head_count, HD)
    starting = 0
    scores = jnp.einsum("qhd,khd->hqk", query, keys, preferred_element_type=jnp.float32) * scale
    scores = jnp.where(allowed[None, starting : starting + span_rows], scores, MASKED)
    soft_weights = jnp.exp(scores - total_parts[:, starting : starting + span_rows, None])
    grad_soft = jnp.einsum("qhd,khd->hqk", grad_mixed, values, preferred_element_type=jnp.float32)
    centre = jnp.sum(soft_weights * grad_soft, axis=-1, keepdims=True)
    grad_scores = (soft_weights * (grad_soft - centre)).astype(jnp.bfloat16)
    query_parts = (
        jnp.einsum("hqk,khd->qhd", grad_scores, keys, preferred_element_type=jnp.float32) * scale
    )
    grad_keys = (
        jnp.einsum("hqk,qhd->khd", grad_scores, query, preferred_element_type=jnp.float32) * scale
    )
    grad_values = jnp.einsum(
        "hqk,qhd->khd",
        soft_weights.astype(jnp.bfloat16),
        grad_mixed,
        preferred_element_type=jnp.float32,
    )
    grad_query = unrotate(query_parts, cosine, sine_table)
    grad_keys = unrotate(grad_keys, cosine, sine_table)
    grad_proj = jnp.concatenate(
        [
            grad_query.reshape(length, model_width),
            grad_keys.reshape(length, model_width),
            grad_values.reshape(length, model_width),
        ],
        axis=1,
    ).astype(jnp.bfloat16)
    grad_qkv = lax.dot_general(
        first_normalized, grad_proj, TOKENS_CONTRACT, preferred_element_type=jnp.float32
    )
    first_normalized_gradient = lax.dot_general(
        grad_proj, w_qkv, ROWS_CONTRACT, preferred_element_type=jnp.float32
    )
    first_gain_gradient = jnp.sum(first_normalized_gradient * first_standardized, axis=0)
    token_input_gradient = residual_gradient + norm_backward(
        first_normalized_gradient, first_standardized, first_inverse_norm, paired_gains[0]
    )
    shard_qkv, shard_out, shard_in, shard_down, shard_gains = (
        lax.psum_scatter(grad_qkv, ("dp", "fsdp"), scatter_dimension=0, tiled=True),
        lax.psum_scatter(grad_out, ("dp", "fsdp"), scatter_dimension=0, tiled=True),
        lax.psum_scatter(grad_in, ("dp", "fsdp"), scatter_dimension=0, tiled=True),
        lax.psum_scatter(grad_down, ("dp", "fsdp"), scatter_dimension=0, tiled=True),
        lax.psum_scatter(
            jnp.stack([first_gain_gradient, second_gain_gradient]),
            ("dp", "fsdp"),
            scatter_dimension=1,
            tiled=True,
        ),
    )
    shards = (shard_qkv, shard_out, shard_in, shard_down, shard_gains)
    local_sum = sum((jnp.sum(piece * piece) for piece in shards))
    global_squares = lax.psum(local_sum, ("dp", "fsdp"))
    grad_norm = jnp.sqrt(global_squares)
    clip_factor = CLIP_NORM / jnp.maximum(grad_norm, CLIP_NORM)
    masters = (attn_in, attn_out, ff_in, ff_out, gains)
    firsts = (attn_in_m, attn_out_m, ff_in_m, ff_out_m, gains_m)
    seconds = (attn_in_v, attn_out_v, ff_in_v, ff_out_v, gains_v)
    decays = (WEIGHT_DECAY, WEIGHT_DECAY, WEIGHT_DECAY, WEIGHT_DECAY, 0.0)
    results = [
        adam_update(w, g, m, v, clip_factor, dec, rate)
        for w, g, m, v, dec, rate in zip(masters, shards, firsts, seconds, decays, LEARN_RATES)
    ]
    return (
        block_out,
        token_input_gradient,
        grad_norm,
        results[0][0],
        results[1][0],
        results[2][0],
        results[3][0],
        results[4][0],
        results[0][1],
        results[1][1],
        results[2][1],
        results[3][1],
        results[4][1],
        results[0][2],
        results[1][2],
        results[2][2],
        results[3][2],
        results[4][2],
    )


def solution(mesh):
    in_specs = (
        P(("dp", "fsdp"), None),
        P(("dp", "fsdp"), None),
        P(("dp", "fsdp"), None),
        P(("dp", "fsdp"), None),
        P(("dp", "fsdp"), None),
        P(("dp", "fsdp"), None),
        P(("dp", "fsdp"), None),
        P(None, ("dp", "fsdp")),
        P(("dp", "fsdp"), None),
        P(("dp", "fsdp"), None),
        P(("dp", "fsdp"), None),
        P(("dp", "fsdp"), None),
        P(None, ("dp", "fsdp")),
        P(("dp", "fsdp"), None),
        P(("dp", "fsdp"), None),
        P(("dp", "fsdp"), None),
        P(("dp", "fsdp"), None),
        P(None, ("dp", "fsdp")),
    )
    out_specs = (
        P(("dp", "fsdp"), None),
        P(("dp", "fsdp"), None),
        P(),
        P(("dp", "fsdp"), None),
        P(("dp", "fsdp"), None),
        P(("dp", "fsdp"), None),
        P(("dp", "fsdp"), None),
        P(None, ("dp", "fsdp")),
        P(("dp", "fsdp"), None),
        P(("dp", "fsdp"), None),
        P(("dp", "fsdp"), None),
        P(("dp", "fsdp"), None),
        P(None, ("dp", "fsdp")),
        P(("dp", "fsdp"), None),
        P(("dp", "fsdp"), None),
        P(("dp", "fsdp"), None),
        P(("dp", "fsdp"), None),
        P(None, ("dp", "fsdp")),
    )
    fast = dict(mesh.shape) == {"dp": 8, "fsdp": 4}
    run = fast_body if fast else body
    return jax.shard_map(run, mesh=mesh, in_specs=in_specs, out_specs=out_specs, check_vma=False)
```
